32 devices in a mesh: section: 2 (over core), dp: 16 (over z, y, x).
Axes of the slice: x: 2, y: 2, z: 4, core: 2. Of those that a mesh axis runs over, the one named last changes fastest.
Arguments:
- inputs: bfloat16 [2, 256, 16, 1024], P(None, 'dp'), may hold values from -6 to 6
- lengths: int32 [2, 256], P(None, 'dp'), may hold values from 1 to 16, as said below
- w_in: bfloat16 [2, 1024, 4096], P('section'), may hold values from -0.1875 to 0.1875
- w_rec: bfloat16 [2, 1024, 4096], P('section'), may hold values from -0.1875 to 0.1875
- bias: float32 [2, 4096], P('section'), may hold values from -3 to 3
- cotangent: bfloat16 [2, 256, 16, 1024], P(None, 'dp'), may hold values from -6 to 6
Outputs:
- hidden_states: bfloat16 [2, 2, 256, 16, 1024], P('section', None, 'dp')
- input_grads: bfloat16 [2, 2, 256, 16, 1024], P('section', None, 'dp')
- grad_in: float32 [2, 1024, 4096], P('section', 'dp')
- grad_rec: float32 [2, 1024, 4096], P('section', 'dp')
- grad_bias: float32 [2, 4096], P('section', 'dp')
The draws below stay inside these ranges and needn't reach their ends.
Inputs may be any that keep to these rules, and one draw needn't show every extreme that they name: `lengths`: each micro-batch has a sequence of length exactly 16.
All inputs are finite; a program needn't handle non-finite values.
Results may differ from the reference program's by a relative error of at most 0.006.
Values may be sent and summed in bfloat16 or wider, within the bound.
A program may use at most 320 MiB of HBM per device.

```python
import jax
import jax.numpy as jnp
from jax import lax

D = 1024
H = 1024
M = 2
L = 16
ROWS = 256


def draw_lengths(key, part):
    key = jax.random.fold_in(key, 5)
    first_key, second_key = jax.random.split(key)
    base = jax.random.randint(first_key, (M, ROWS), 1, L + 1, dtype=jnp.int32)
    picked = jax.random.randint(second_key, (M, 1), 0, ROWS, dtype=jnp.int32)
    row_index = jnp.arange(ROWS, dtype=jnp.int32)[None, :]
    return jnp.where(row_index == picked, L, base).astype(jnp.int32)


def spiked(drawn, key, source, target, blocks, factor):
    def block_of(axis_at):
        return (jnp.arange(drawn.shape[axis_at]) // (drawn.shape[axis_at] // blocks)).reshape((-1,) + (1,) * (drawn.ndim - 1 - axis_at))

    near = jax.random.permutation(key, blocks)[block_of(target)]
    second = (block_of(target) + blocks // 2) % blocks
    return jnp.where((block_of(source) == near) | (block_of(source) == second), factor * drawn, drawn)


def block_scale(rng, extent, shards, low, largest):
    loudness = 1.0
    for position, blocks in shards:
        draws = jax.random.uniform(jax.random.fold_in(jax.random.fold_in(rng, 6), position), (blocks,), jnp.float32, low / len(shards), largest / len(shards))
        loudness = loudness * jnp.repeat(jnp.exp(draws), extent[position] // blocks).reshape((-1,) + (1,) * (len(extent) - 1 - position))
    return loudness


def normal_values(key, extent, scale, most, cuts=(), kind=jnp.bfloat16):
    gain = block_scale(key, extent, cuts, -0.22, 0.18) if cuts else 1.0
    values = jax.random.normal(key, extent, jnp.float32) * scale * gain
    return jnp.minimum(jnp.maximum(values, -most), most).astype(kind)


def gaussian_with(own_key, extent, deviation, reach, cuts, heavy, kind=jnp.bfloat16):
    drawn = deviation * jax.random.normal(own_key, extent, jnp.float32)
    if cuts:
        drawn = drawn * block_scale(own_key, extent, cuts, -0.22, 0.18)
    return jnp.clip(spiked(drawn, jax.random.fold_in(own_key, 3), *heavy), -reach, reach).astype(kind)


def setup_inputs(seed: int = 0) -> dict:
    keys = jax.random.split(jax.random.key(seed), 7)
    inputs = gaussian_with(keys[0], (M, ROWS, L, D), 1.0, 6.0, ((1, 16),), (1, 3, 16, 2.0))
    lengths = draw_lengths(jax.random.fold_in(keys[6], 71), 0)
    w_in = normal_values(keys[2], (2, D, 4 * H), D ** -0.5, 0.1875, ((0, 2),))
    w_rec = normal_values(keys[3], (2, H, 4 * H), H ** -0.5, 0.1875, ((0, 2),))
    bias = normal_values(keys[4], (2, 4 * H), 0.5, 3.0, ((0, 2),), jnp.float32)
    cotangent = gaussian_with(keys[5], (M, ROWS, L, H), 1.0, 6.0, ((1, 16),), (1, 3, 16, 2.0))
    return dict(inputs=inputs, lengths=lengths, w_in=w_in, w_rec=w_rec, bias=bias, cotangent=cotangent)


@jax.custom_vjp
def low(v):
    return lax.optimization_barrier(v.astype(jnp.bfloat16)).astype(jnp.float32)

@jax.custom_vjp
def low_back(v):
    return v

def low_keep(v):
    return (low(v), None)

def low_pass(kept, grad):
    return (grad,)

def back_keep(v):
    return (v, None)

def back_low(kept, grad):
    return (low(grad),)
low.defvjp(low_keep, low_pass)
low_back.defvjp(back_keep, back_low)
highest = lax.Precision.HIGHEST

def lstm_layer(layer_in, w_gate_in, w_gate_rec, gate_bias, masks):
    hidden = w_gate_rec.shape[0]
    rows_in = low_back(layer_in)
    projected = jnp.einsum('btd,dg->tbg', rows_in, w_gate_in, precision=highest) + gate_bias

    def recur(carry, inputs_t):
        h_prev, c_prev = carry
        proj_t, mask_t = inputs_t
        gates = low_back(proj_t + jnp.dot(h_prev, w_gate_rec, precision=highest))
        in_gate = jax.nn.sigmoid(gates[:, :hidden])
        forget = jax.nn.sigmoid(gates[:, hidden:2 * hidden])
        candid = jnp.tanh(gates[:, 2 * hidden:3 * hidden])
        out_gate = jax.nn.sigmoid(gates[:, 3 * hidden:])
        c_new = forget * c_prev + in_gate * candid
        h_new = low(out_gate * jnp.tanh(c_new))
        return ((h_new, c_new), h_new * mask_t[:, None])
    batch = layer_in.shape[0]
    zeros = jnp.zeros((batch, hidden), jnp.float32)
    final_state, outputs = lax.scan(jax.checkpoint(recur), (zeros, zeros), (projected, masks.T))
    return jnp.transpose(outputs, (1, 0, 2))

def reference(inputs, lengths, w_in, w_rec, bias, cotangent):
    inputs_f = inputs.astype(jnp.float32)
    w_in_f = w_in.astype(jnp.float32)
    w_rec_f = w_rec.astype(jnp.float32)
    bias_f = bias.astype(jnp.float32)
    positions = jnp.arange(L, dtype=jnp.int32)
    sum_in = jnp.zeros_like(w_in_f)
    sum_rec = jnp.zeros_like(w_rec_f)
    sum_bias = jnp.zeros_like(bias_f)
    first_outs, second_outs, first_grads, second_grads = ([], [], [], [])
    for micro in range(M):
        masks = (positions[None, :] < lengths[micro][:, None]).astype(jnp.float32)

        def run_layer(layer_in, w_gate_in, w_gate_rec, gate_bias):
            return lstm_layer(layer_in, w_gate_in, w_gate_rec, gate_bias, masks)
        out_one, back_one = jax.vjp(run_layer, inputs_f[micro], w_in_f[0], w_rec_f[0], bias_f[0])
        out_two, back_two = jax.vjp(run_layer, out_one, w_in_f[1], w_rec_f[1], bias_f[1])
        grad_mid, gin_two, grec_two, gbias_two = back_two(cotangent[micro].astype(jnp.float32))
        grad_first, gin_one, grec_one, gbias_one = back_one(grad_mid)
        sum_in = sum_in + jnp.stack([gin_one, gin_two])
        sum_rec = sum_rec + jnp.stack([grec_one, grec_two])
        sum_bias = sum_bias + jnp.stack([gbias_one, gbias_two])
        first_outs.append(out_one)
        second_outs.append(out_two)
        first_grads.append(grad_first)
        second_grads.append(grad_mid)
    hidden_states = jnp.stack([jnp.stack(first_outs), jnp.stack(second_outs)]).astype(jnp.bfloat16)
    input_grads = jnp.stack([jnp.stack(first_grads), jnp.stack(second_grads)]).astype(jnp.bfloat16)
    return (hidden_states, input_grads, sum_in, sum_rec, sum_bias)
```

```python
import functools

import jax
import jax.numpy as jnp
from jax import lax
from jax.experimental import pallas as pl
from jax.experimental.pallas import tpu as pltpu
from jax.sharding import PartitionSpec as P

BF = jnp.bfloat16
F32 = jnp.float32
BLOCK = 4
PAD = 128
TILE = 256


def sigmoid(v):
    return 0.5 * jnp.tanh(0.5 * v) + 0.5


def rows_at(start, size):
    return pl.ds(pl.multiple_of(start, size), size)


def dot(a, b):
    return jnp.dot(a, b, preferred_element_type=F32)


def dot_t(a, b):
    return lax.dot_general(a, b, (((1,), (1,)), ((), ())), preferred_element_type=F32)


def padded(rows):
    lack = PAD - rows.shape[0]
    return jnp.concatenate([rows, jnp.zeros((lack, rows.shape[1]), rows.dtype)], axis=0) if lack > 0 else rows


def lstm_kernel(
    steps, seqs,
    x_ref, len_ref, win_ref, wrec_ref, bias_ref, ct_ref,
    hid_out, dx_out, u_out, hp_out, dz_out,
    raw, perm, u, hs, dy, dx, act, cs, dz, proj, win, wrec, wrt, wint, dr, dc, lens, bias,
    load_sem, store_sem, up_send, up_recv, down_send, down_recv,
):
    hidden = wrec.shape[0]
    gates = 4 * hidden
    total = steps * seqs
    blocks = steps // BLOCK
    brows = BLOCK * seqs
    section = lax.axis_index("section")
    first = section == 0
    second = section == 1
    other = {"section": 1 - section}

    barrier = pltpu.get_barrier_semaphore()
    pl.semaphore_signal(barrier, inc=1, device_id=other, device_id_type=pl.DeviceIdType.MESH)

    load_x = pltpu.make_async_copy(x_ref, raw, load_sem.at[0])
    load_ct = pltpu.make_async_copy(ct_ref, raw, load_sem.at[0])
    load_win = pltpu.make_async_copy(win_ref, win, load_sem.at[1])
    load_wrec = pltpu.make_async_copy(wrec_ref, wrec, load_sem.at[2])
    load_bias = pltpu.make_async_copy(bias_ref, bias, load_sem.at[3])
    pl.when(first)(lambda: load_x.start())
    pl.when(second)(lambda: load_ct.start())
    load_bias.start()
    load_win.start()
    load_wrec.start()

    micro, per = len_ref.shape
    row_id = lax.broadcasted_iota(jnp.int32, (per, per), 0)
    col_id = lax.broadcasted_iota(jnp.int32, (per, per), 1)
    for m in range(micro):
        row = jnp.broadcast_to(len_ref[m : m + 1, :].astype(F32), (per, per))
        column = jnp.sum(jnp.where(row_id == col_id, row, 0.0), axis=1, keepdims=True)
        lens[m * per : (m + 1) * per, :] = jnp.broadcast_to(column, (per, lens.shape[1]))

    hs[0:seqs, :] = jnp.zeros((seqs, hidden), BF)
    cs[0:seqs, :] = jnp.zeros((seqs, hidden), F32)
    dr[...] = jnp.zeros_like(dr)
    dc[...] = jnp.zeros_like(dc)

    q_id = lax.broadcasted_iota(jnp.int32, (total, total), 0)
    p_id = lax.broadcasted_iota(jnp.int32, (total, total), 1)
    perm[...] = jnp.where((q_id % seqs) * steps + q_id // seqs == p_id, 1.0, 0.0).astype(BF)
    load_x.wait()
    ordered = dot(perm[...], raw[...]).astype(BF)

    @pl.when(first)
    def _():
        u[...] = ordered

    @pl.when(second)
    def _():
        dy[...] = ordered

    load_bias.wait()
    load_win.wait()
    load_wrec.wait()

    eye = jnp.where(
        lax.broadcasted_iota(jnp.int32, (TILE, TILE), 0) == lax.broadcasted_iota(jnp.int32, (TILE, TILE), 1), 1.0, 0.0
    ).astype(BF)

    def turn_over(source, target):
        def piece(i, carry):
            at = rows_at(i * TILE, TILE)
            target[at, :] = dot_t(eye, source[:, at]).astype(BF)
            return carry

        lax.fori_loop(0, gates // TILE, piece, 0)

    @pl.when(second)
    def _():
        turn_over(wrec, wrt)
        turn_over(win, wint)

    pl.semaphore_wait(barrier, 1)

    def send_up(b):
        return pltpu.make_async_remote_copy(
            src_ref=hs.at[pl.ds(pl.multiple_of(b * brows + seqs, seqs), brows)],
            dst_ref=u.at[rows_at(b * brows, brows)],
            send_sem=up_send.at[b],
            recv_sem=up_recv.at[b],
            device_id=other,
            device_id_type=pl.DeviceIdType.MESH,
        )

    def send_down(b):
        return pltpu.make_async_remote_copy(
            src_ref=dx.at[rows_at(b * brows, brows)],
            dst_ref=dy.at[rows_at(b * brows, brows)],
            send_sem=down_send.at[b],
            recv_sem=down_recv.at[b],
            device_id=other,
            device_id_type=pl.DeviceIdType.MESH,
        )

    def forward_block(b, carry):
        pl.when(second)(lambda: send_up(b).wait_recv())

        def project(i, c):
            at = rows_at(i * TILE, TILE)
            proj[:, at] = dot(u[rows_at(b * brows, brows), :], win[:, at]) + bias[:, at]
            return c

        lax.fori_loop(0, gates // TILE, project, 0, unroll=4)

        def step(k, c):
            t = b * BLOCK + k
            here = rows_at(t * seqs, seqs)
            after = rows_at((t + 1) * seqs, seqs)
            part = rows_at(k * seqs, seqs)
            h_prev = padded(hs[here, :])
            mask = jnp.where(t.astype(F32) < lens[:, 0:1], 1.0, 0.0)
            for j in range(0, hidden, TILE):
                z = []
                for g in range(4):
                    cols = slice(g * hidden + j, g * hidden + j + TILE)
                    z.append(dot(h_prev, wrec[:, cols])[:seqs] + proj[part, cols])
                gi, gf, gg, go = sigmoid(z[0]), sigmoid(z[1]), jnp.tanh(z[2]), sigmoid(z[3])
                c_new = gf * cs[here, j : j + TILE] + gi * gg
                cs[after, j : j + TILE] = c_new
                act[here, j : j + TILE] = gi
                act[here, hidden + j : hidden + j + TILE] = gf
                act[here, 2 * hidden + j : 2 * hidden + j + TILE] = gg
                act[here, 3 * hidden + j : 3 * hidden + j + TILE] = go
                hs[after, j : j + TILE] = (go * jnp.tanh(c_new) * mask).astype(BF)
            return c

        lax.fori_loop(0, BLOCK, step, 0)
        pl.when(first)(lambda: send_up(b).start())
        return carry

    lax.fori_loop(0, blocks, forward_block, 0)

    @pl.when(first)
    def _():
        turn_over(wrec, wrt)
        turn_over(win, wint)

    def backward_block(i, carry):
        b = blocks - 1 - i
        pl.when(first)(lambda: send_down(b).wait_recv())

        def step(n, c):
            t = b * BLOCK + (BLOCK - 1 - n)
            here = rows_at(t * seqs, seqs)
            after = rows_at((t + 1) * seqs, seqs)
            mask = jnp.where(t.astype(F32) < lens[:, 0:1], 1.0, 0.0)
            for j in range(0, hidden, TILE):
                cols = slice(j, j + TILE)
                dh = dy[here, cols].astype(F32) * mask + dr[:, cols]
                gi = act[here, j : j + TILE]
                gf = act[here, hidden + j : hidden + j + TILE]
                gg = act[here, 2 * hidden + j : 2 * hidden + j + TILE]
                go = act[here, 3 * hidden + j : 3 * hidden + j + TILE]
                tc = jnp.tanh(cs[after, cols])
                e = dc[:, cols] + dh * go * (1.0 - tc * tc)
                dz[here, j : j + TILE] = (e * gg * gi * (1.0 - gi)).astype(BF)
                dz[here, hidden + j : hidden + j + TILE] = (e * cs[here, cols] * gf * (1.0 - gf)).astype(BF)
                dz[here, 2 * hidden + j : 2 * hidden + j + TILE] = (e * gi * (1.0 - gg * gg)).astype(BF)
                dz[here, 3 * hidden + j : 3 * hidden + j + TILE] = (dh * tc * go * (1.0 - go)).astype(BF)
                dc[:, cols] = e * gf
            dr[...] = dot(padded(dz[here, :]), wrt[...])[:seqs]
            return c

        lax.fori_loop(0, BLOCK, step, 0)
        block_rows = rows_at(b * brows, brows)
        dx[block_rows, :] = dot(padded(dz[block_rows, :]), wint[...])[:brows].astype(BF)
        pl.when(second)(lambda: send_down(b).start())
        return carry

    lax.fori_loop(0, blocks, backward_block, 0)

    perm[...] = jnp.where((q_id % steps) * seqs + q_id // steps == p_id, 1.0, 0.0).astype(BF)
    raw[...] = dot(perm[...], hs[seqs:, :]).astype(BF)
    stores = [
        pltpu.make_async_copy(raw, hid_out, store_sem.at[0]),
        pltpu.make_async_copy(u, u_out, store_sem.at[1]),
        pltpu.make_async_copy(hs.at[pl.ds(0, total)], hp_out, store_sem.at[2]),
        pltpu.make_async_copy(dz, dz_out, store_sem.at[3]),
    ]
    for copy in stores:
        copy.start()
    for b in range(blocks):
        pl.when(first)(lambda: send_up(b).wait_send())
        pl.when(second)(lambda: send_down(b).wait_send())
    dy[...] = dot(perm[...], dx[...]).astype(BF)
    last = pltpu.make_async_copy(dy, dx_out, store_sem.at[4])
    last.start()
    for copy in stores + [last]:
        copy.wait()


def on_device(inputs, lengths, w_in, w_rec, bias, cotangent):
    micro, per, steps, feats = inputs.shape
    hidden = w_rec.shape[1]
    seqs = micro * per
    total = steps * seqs
    vmem = pltpu.VMEM
    blocks = steps // BLOCK
    hid, dx, u, hp, dz = pl.pallas_call(
        functools.partial(lstm_kernel, steps, seqs),
        out_shape=(
            jax.ShapeDtypeStruct((total, hidden), BF),
            jax.ShapeDtypeStruct((total, feats), BF),
            jax.ShapeDtypeStruct((total, feats), BF),
            jax.ShapeDtypeStruct((total, hidden), BF),
            jax.ShapeDtypeStruct((total, 4 * hidden), BF),
        ),
        in_specs=[
            pl.BlockSpec(memory_space=pl.ANY),
            pl.BlockSpec(memory_space=pltpu.VMEM),
            pl.BlockSpec(memory_space=pl.ANY),
            pl.BlockSpec(memory_space=pl.ANY),
            pl.BlockSpec(memory_space=pl.ANY),
            pl.BlockSpec(memory_space=pl.ANY),
        ],
        out_specs=tuple(pl.BlockSpec(memory_space=pl.ANY) for _ in range(5)),
        scratch_shapes=[
            vmem((total, feats), BF),
            vmem((total, total), BF),
            vmem((total, feats), BF),
            vmem((total + seqs, hidden), BF),
            vmem((total, hidden), BF),
            vmem((total, feats), BF),
            vmem((total, 4 * hidden), F32),
            vmem((total + seqs, hidden), F32),
            vmem((total, 4 * hidden), BF),
            vmem((BLOCK * seqs, 4 * hidden), F32),
            vmem((feats, 4 * hidden), BF),
            vmem((hidden, 4 * hidden), BF),
            vmem((4 * hidden, hidden), BF),
            vmem((4 * hidden, feats), BF),
            vmem((seqs, hidden), F32),
            vmem((seqs, hidden), F32),
            vmem((seqs, 128), F32),
            vmem((1, 4 * hidden), F32),
            pltpu.SemaphoreType.DMA((4,)),
            pltpu.SemaphoreType.DMA((5,)),
            pltpu.SemaphoreType.DMA((blocks,)),
            pltpu.SemaphoreType.DMA((blocks,)),
            pltpu.SemaphoreType.DMA((blocks,)),
            pltpu.SemaphoreType.DMA((blocks,)),
        ],
        compiler_params=pltpu.CompilerParams(
            collective_id=0, has_side_effects=True, vmem_limit_bytes=62 * 2**20
        ),
        name="lstm_both_ways",
    )(
        inputs.reshape(total, feats),
        lengths,
        w_in[0],
        w_rec[0],
        bias,
        cotangent.reshape(total, hidden),
    )
    sum_in = lax.dot_general(u, dz, (((0,), (0,)), ((), ())), preferred_element_type=F32)
    sum_rec = lax.dot_general(hp, dz, (((0,), (0,)), ((), ())), preferred_element_type=F32)
    sum_bias = jnp.sum(dz, axis=0, dtype=F32)
    share_in = lax.psum_scatter(sum_in, "dp", scatter_dimension=0, tiled=True)
    share_rec = lax.psum_scatter(sum_rec, "dp", scatter_dimension=0, tiled=True)
    share_bias = lax.psum_scatter(sum_bias, "dp", scatter_dimension=0, tiled=True)
    shape = inputs.shape
    return (
        hid.reshape(shape)[None],
        dx.reshape(shape)[None],
        share_in[None],
        share_rec[None],
        share_bias[None],
    )


def solution(mesh):
    placed = (
        P(None, "dp", None, None),
        P(None, "dp"),
        P("section", None, None),
        P("section", None, None),
        P("section", None),
        P(None, "dp", None, None),
    )
    return jax.shard_map(
        on_device,
        mesh=mesh,
        in_specs=placed,
        out_specs=(
            P("section", None, "dp", None, None),
            P("section", None, "dp", None, None),
            P("section", "dp", None),
            P("section", "dp", None),
            P("section", "dp"),
        ),
        check_vma=False,
    )
```

```python
import functools

import jax
import jax.numpy as jnp
from jax import lax
from jax.experimental import pallas as pl
from jax.experimental.pallas import tpu as pltpu
from jax.sharding import PartitionSpec as P

BF = jnp.bfloat16
F32 = jnp.float32
MESH = pl.DeviceIdType.MESH
CHUNK = 256
BLOCK = 4
PAD = 128
TILE = 256


def sigmoid(v):
    return 0.5 * jnp.tanh(0.5 * v) + 0.5


def rows_at(start, size):
    return pl.ds(pl.multiple_of(start, size), size)


def dot(a, b):
    return jnp.dot(a, b, preferred_element_type=F32)


def dot_t(a, b):
    return lax.dot_general(a, b, (((1,), (1,)), ((), ())), preferred_element_type=F32)


def padded(rows):
    lack = PAD - rows.shape[0]
    return jnp.concatenate([rows, jnp.zeros((lack, rows.shape[1]), rows.dtype)], axis=0) if lack > 0 else rows


def lstm_kernel(
    steps, seqs, fused,
    x_ref, len_ref, win_ref, wrec_ref, bias_ref, ct_ref,
    hid_out, dx_out, out_a, out_b, out_c,
    u, hs, dy, dx, act, cs, dz, proj, win, wrec, wrt, wint, dr, dc, lens, bias,
    load_sem, store_sem, up_send, up_recv, down_send, down_recv, *more,
):
    hidden = wrec.shape[0]
    gates = 4 * hidden
    total = steps * seqs
    blocks = steps // BLOCK
    brows = BLOCK * seqs
    section = lax.axis_index("section")
    first = section == 0
    second = section == 1
    other = {"section": 1 - section}

    tail = Tail(section, hidden, act, win, wrec, proj, dz, *more) if fused else None

    barrier = pltpu.get_barrier_semaphore()
    pl.semaphore_signal(barrier, inc=1, device_id=other, device_id_type=MESH)
    if fused:
        for partner in tail.partners:
            pl.semaphore_signal(barrier, inc=1, device_id=partner, device_id_type=MESH)

    load_x = pltpu.make_async_copy(x_ref, dx, load_sem.at[0])
    load_ct = pltpu.make_async_copy(ct_ref, dx, load_sem.at[0])
    load_win = pltpu.make_async_copy(win_ref, win, load_sem.at[1])
    load_wrec = pltpu.make_async_copy(wrec_ref, wrec, load_sem.at[2])
    load_bias = pltpu.make_async_copy(bias_ref, bias, load_sem.at[3])
    pl.when(first)(lambda: load_x.start())
    pl.when(second)(lambda: load_ct.start())
    load_bias.start()
    load_win.start()
    load_wrec.start()

    micro, per = len_ref.shape
    row_id = lax.broadcasted_iota(jnp.int32, (per, per), 0)
    col_id = lax.broadcasted_iota(jnp.int32, (per, per), 1)
    for m in range(micro):
        row = jnp.broadcast_to(len_ref[m : m + 1, :].astype(F32), (per, per))
        column = jnp.sum(jnp.where(row_id == col_id, row, 0.0), axis=1, keepdims=True)
        lens[m * per : (m + 1) * per, :] = jnp.broadcast_to(column, (per, lens.shape[1]))

    hs[0:seqs, :] = jnp.zeros((seqs, hidden), BF)
    cs[0:seqs, :] = jnp.zeros((seqs, hidden), F32)
    dr[...] = jnp.zeros_like(dr)
    dc[...] = jnp.zeros_like(dc)

    perm = wrt.at[0:total, 0:total]

    def reorder(outer, inner, source, skip, write):
        to_id = lax.broadcasted_iota(jnp.int32, (inner, total), 0)
        from_id = lax.broadcasted_iota(jnp.int32, (inner, total), 1)
        for n in range(outer):
            perm[n * inner : (n + 1) * inner, :] = jnp.where(to_id * outer + n == from_id, 1.0, 0.0).astype(BF)
        for j in range(0, hidden, TILE):
            cols = slice(j, j + TILE)
            write(cols, dot(perm[...], source[skip : skip + total, cols]).astype(BF))

    def write_first(cols, value):
        @pl.when(first)
        def _():
            u[:, cols] = value

        @pl.when(second)
        def _():
            dy[:, cols] = value

    load_x.wait()
    reorder(steps, seqs, dx, 0, write_first)

    load_bias.wait()
    load_win.wait()
    load_wrec.wait()

    eye = jnp.where(
        lax.broadcasted_iota(jnp.int32, (TILE, TILE), 0) == lax.broadcasted_iota(jnp.int32, (TILE, TILE), 1), 1.0, 0.0
    ).astype(BF)

    def turn_over(source, target):
        def piece(i, carry):
            at = rows_at(i * TILE, TILE)
            target[at, :] = dot_t(eye, source[:, at]).astype(BF)
            return carry

        lax.fori_loop(0, gates // TILE, piece, 0)

    @pl.when(second)
    def _():
        turn_over(wrec, wrt)
        turn_over(win, wint)

    pl.semaphore_wait(barrier, 1 + len(tail.partners) if fused else 1)

    def send_up(b):
        return pltpu.make_async_remote_copy(
            src_ref=hs.at[pl.ds(pl.multiple_of(b * brows + seqs, seqs), brows)],
            dst_ref=u.at[rows_at(b * brows, brows)],
            send_sem=up_send.at[b],
            recv_sem=up_recv.at[b],
            device_id=other,
            device_id_type=MESH,
        )

    def send_down(b):
        return pltpu.make_async_remote_copy(
            src_ref=dx.at[rows_at(b * brows, brows)],
            dst_ref=dy.at[rows_at(b * brows, brows)],
            send_sem=down_send.at[b],
            recv_sem=down_recv.at[b],
            device_id=other,
            device_id_type=MESH,
        )

    def forward_block(b, carry):
        pl.when(second)(lambda: send_up(b).wait_recv())

        def project(i, c):
            at = rows_at(i * TILE, TILE)
            proj[:, at] = dot(u[rows_at(b * brows, brows), :], win[:, at]) + bias[:, at]
            return c

        lax.fori_loop(0, gates // TILE, project, 0, unroll=4)

        def step(k, c):
            t = b * BLOCK + k
            here = rows_at(t * seqs, seqs)
            after = rows_at((t + 1) * seqs, seqs)
            part = rows_at(k * seqs, seqs)
            h_prev = padded(hs[here, :])
            mask = jnp.where(t.astype(F32) < lens[:, 0:1], 1.0, 0.0)
            for j in range(0, hidden, TILE):
                z = []
                for g in range(4):
                    cols = slice(g * hidden + j, g * hidden + j + TILE)
                    z.append(dot(h_prev, wrec[:, cols])[:seqs] + proj[part, cols])
                gi, gf, gg, go = sigmoid(z[0]), sigmoid(z[1]), jnp.tanh(z[2]), sigmoid(z[3])
                c_new = gf * cs[here, j : j + TILE] + gi * gg
                cs[after, j : j + TILE] = c_new
                act[here, j : j + TILE] = gi
                act[here, hidden + j : hidden + j + TILE] = gf
                act[here, 2 * hidden + j : 2 * hidden + j + TILE] = gg
                act[here, 3 * hidden + j : 3 * hidden + j + TILE] = go
                hs[after, j : j + TILE] = (go * jnp.tanh(c_new) * mask).astype(BF)
            return c

        lax.fori_loop(0, BLOCK, step, 0)
        pl.when(first)(lambda: send_up(b).start())
        return carry

    lax.fori_loop(0, blocks, forward_block, 0)

    @pl.when(first)
    def _():
        turn_over(wrec, wrt)
        turn_over(win, wint)

    if fused:
        tail.send_factors(eye, u, hs)
        for partner in tail.partners:
            pl.semaphore_signal(tail.ready, inc=1, device_id=partner, device_id_type=MESH)

    def backward_block(i, carry):
        b = blocks - 1 - i
        pl.when(first)(lambda: send_down(b).wait_recv())

        def step(n, c):
            t = b * BLOCK + (BLOCK - 1 - n)
            here = rows_at(t * seqs, seqs)
            after = rows_at((t + 1) * seqs, seqs)
            mask = jnp.where(t.astype(F32) < lens[:, 0:1], 1.0, 0.0)
            for j in range(0, hidden, TILE):
                cols = slice(j, j + TILE)
                dh = dy[here, cols].astype(F32) * mask + dr[:, cols]
                gi = act[here, j : j + TILE]
                gf = act[here, hidden + j : hidden + j + TILE]
                gg = act[here, 2 * hidden + j : 2 * hidden + j + TILE]
                go = act[here, 3 * hidden + j : 3 * hidden + j + TILE]
                tc = jnp.tanh(cs[after, cols])
                e = dc[:, cols] + dh * go * (1.0 - tc * tc)
                dz[here, j : j + TILE] = (e * gg * gi * (1.0 - gi)).astype(BF)
                dz[here, hidden + j : hidden + j + TILE] = (e * cs[here, cols] * gf * (1.0 - gf)).astype(BF)
                dz[here, 2 * hidden + j : 2 * hidden + j + TILE] = (e * gi * (1.0 - gg * gg)).astype(BF)
                dz[here, 3 * hidden + j : 3 * hidden + j + TILE] = (dh * tc * go * (1.0 - go)).astype(BF)
                dc[:, cols] = e * gf
            dr[...] = dot(padded(dz[here, :]), wrt[...])[:seqs]
            return c

        lax.fori_loop(0, BLOCK, step, 0)
        block_rows = rows_at(b * brows, brows)
        if fused:
            tail.send_dz(b, brows)

        @pl.when(second)
        def _():
            dx[block_rows, :] = dot(dz[block_rows, :], wint[...]).astype(BF)
            send_down(b).start()

        return carry

    lax.fori_loop(0, blocks, backward_block, 0)

    def write_sequences():
        def write_u(cols, value):
            u[:, cols] = value

        def write_dy(cols, value):
            dy[:, cols] = value

        reorder(seqs, steps, hs, seqs, write_u)
        pltpu.make_async_copy(u, hid_out, store_sem.at[0]).start()

        @pl.when(first)
        def _():
            for j in range(0, hidden, TILE):
                dx[:, j : j + TILE] = dot(dz[...], wint[:, j : j + TILE]).astype(BF)

        reorder(seqs, steps, dx, 0, write_dy)
        pltpu.make_async_copy(dy, dx_out, store_sem.at[1]).start()

    if fused:
        tail.run(blocks, brows, write_sequences, out_a, out_b, out_c, store_sem)
    else:
        stores = [
            pltpu.make_async_copy(u, out_a, store_sem.at[2]),
            pltpu.make_async_copy(hs.at[pl.ds(0, total)], out_b, store_sem.at[3]),
            pltpu.make_async_copy(dz, out_c, store_sem.at[4]),
        ]
        for copy in stores:
            copy.start()
        for copy in stores:
            copy.wait()
        write_sequences()
    pltpu.make_async_copy(u, hid_out, store_sem.at[0]).wait()
    pltpu.make_async_copy(dy, dx_out, store_sem.at[1]).wait()
    for b in range(blocks):
        pl.when(first)(lambda: send_up(b).wait_send())
        pl.when(second)(lambda: send_down(b).wait_send())


class Tail:
    def __init__(self, section, hidden, act, win, wrec, proj, dz, fta, ftb, dza, dzb, bsum, brecv, ready,
                 ft_sems, dz_sems, a_sems, b_sems, z_sems, c_sems):
        self.s = section
        self.first, self.second = section == 0, section == 1
        self.hidden, self.half = hidden, 2 * hidden
        self.act, self.win, self.wrec, self.proj, self.dz = act, win, wrec, proj, dz
        self.fta, self.ftb, self.dza, self.dzb = fta, ftb, dza, dzb
        self.bsum, self.brecv, self.ready = bsum, brecv, ready
        self.ft_sems, self.dz_sems = ft_sems, dz_sems
        self.a_sems, self.b_sems, self.z_sems, self.c_sems = a_sems, b_sems, z_sems, c_sems
        j = lax.axis_index("dp")
        x, y, z = j % 2, (j // 2) % 2, j // 4
        s = section
        self.x, self.y, self.z = x, y, z
        self.ca = x * (1 - s) + y * s
        self.cb = y * (1 - s) + x * s
        self.zp = z % 2
        self.zin = z // 2
        self.kz = ((z + 1) // 2) % 2
        jx, jy = j + 1 - 2 * x, j + 2 - 4 * y
        self.to_x, self.to_y = {"dp": jx}, {"dp": jy}
        self.to_a = {"dp": jx * (1 - s) + jy * s}
        self.to_b = {"dp": jy * (1 - s) + jx * s}
        self.to_mate = {"dp": j + 4 - 8 * self.zp}
        self.to_across = {"dp": j + 4 * (3 - 2 * z)}
        self.to_z = [{"dp": j - 4 * z + 4 * ((z + 3 - i) % 4)} for i in range(3)]
        self.partners = [self.to_x, self.to_y] + self.to_z
        self.rows = dz.shape[0]
        self.chunks = self.half // CHUNK
        self.unit = hidden // 16

    def remote(self, src, dst, send, recv, to):
        return pltpu.make_async_remote_copy(
            src_ref=src, dst_ref=dst, send_sem=send, recv_sem=recv, device_id=to, device_id_type=MESH
        )


    def build(self, eye, source, target, place):
        unit = self.unit
        for f in range(self.hidden // TILE):
            turned = dot_t(eye, source[0 : self.rows, f * TILE : (f + 1) * TILE]).astype(BF)
            for i in range(TILE // unit):
                at = place(f * (TILE // unit) + i) * unit
                target[at : at + unit, 0 : self.rows] = turned[i * unit : (i + 1) * unit, :]

    def factor_copy(self, i):
        own, theirs = pl.ds(0, self.rows), pl.ds(self.rows, self.rows)
        ref, to = ((self.fta, self.to_a), (self.ftb, self.to_mate))[i]
        return self.remote(ref.at[:, own], ref.at[:, theirs], self.ft_sems.at[0, i], self.ft_sems.at[1, i], to)

    def send_factors(self, eye, u, hs):
        def z_place(z):
            return 2 * (((z + 1) // 2) % 2) + z // 2

        def place_a(j, a_is_x):
            x, y, z = j % 2, (j // 2) % 2, j // 4
            a, b = (x, y) if a_is_x else (y, x)
            return b * 8 + z_place(z) * 2 + a

        def place_b(j, a_is_x):
            x, y, z = j % 2, (j // 2) % 2, j // 4
            a, b = (x, y) if a_is_x else (y, x)
            return a * 8 + b * 4 + z

        @pl.when(self.first)
        def _():
            self.build(eye, u, self.fta, lambda j: place_a(j, True))
            self.build(eye, hs, self.ftb, lambda j: place_b(j, True))

        @pl.when(self.second)
        def _():
            self.build(eye, hs, self.fta, lambda j: place_a(j, False))
            self.build(eye, u, self.ftb, lambda j: place_b(j, False))

        for i in range(2):
            self.factor_copy(i).start()

    def dz_copy(self, i, b, brows):
        at = pl.ds(pl.multiple_of(b * brows, brows), brows)
        their = pl.ds(pl.multiple_of((1 - (self.ca, self.zp)[i]) * self.half, self.half), self.half)
        return self.remote(
            self.dz.at[at, their],
            (self.dza, self.dzb)[i].at[at],
            self.dz_sems.at[2 * i, b],
            self.dz_sems.at[2 * i + 1, b],
            (self.to_a, self.to_mate)[i],
        )

    def send_dz(self, b, brows):
        for i in range(2):
            self.dz_copy(i, b, brows).start()


    def region(self, ref, row, size, base, k):
        return ref.at[pl.ds(row, size), pl.ds(pl.multiple_of(base + k * CHUNK, CHUNK), CHUNK)]

    def moved(self, row, size, base, k, send, recv, to):
        return self.remote(
            self.region(self.wrec, row, size, base, k), self.region(self.win, row, size, base, k), send, recv, to
        )

    def a1(self, k):
        return self.moved(0, 512, 0, k, self.a_sems.at[0, k], self.a_sems.at[1, k], self.to_b)

    def a2(self, k):
        return self.moved(512, 256, 0, k, self.a_sems.at[2, k], self.a_sems.at[3, k], self.to_mate)

    def a3(self, k):
        return self.moved(768, 128, 0, k, self.a_sems.at[4, k], self.a_sems.at[5, k], self.to_across)

    def a4(self, k):
        return self.moved(896, 64, 0, k, self.a_sems.at[6, k], self.a_sems.at[7, k], self.to_a)

    def b1(self, k):
        return self.moved(0, 512, self.half, k, self.b_sems.at[0, k], self.b_sems.at[1, k], self.to_a)

    def b2(self, k):
        return self.moved(512, 256, self.half, k, self.b_sems.at[2, k], self.b_sems.at[3, k], self.to_b)

    def b3(self, k, i):
        return self.moved(
            768 + 64 * i, 64, self.half, k, self.z_sems.at[0, i, k], self.z_sems.at[1, i, k], self.to_z[i]
        )

    def cols(self, base, k):
        return pl.ds(pl.multiple_of(base + k * CHUNK, CHUNK), CHUNK)

    def span(self, start, size):
        return pl.ds(pl.multiple_of(start, size), size)

    def product(self, ft, dz_theirs, mine, row, k):
        rows = self.span(row, 512)
        one = dot(ft[rows, 0 : self.rows], self.dz[:, self.cols(mine * self.half, k)])
        two = dot(ft[rows, self.rows : 2 * self.rows], dz_theirs[:, self.cols(0, k)])
        return one + two

    def bias_plan(self, i):
        base_x, base_y = self.x * 8, self.x * 8 + self.y * 4
        base_z = base_y + self.kz * 2
        return (
            ((1 - self.x) * 8, base_x, 8, 0, self.to_x),
            (base_x + (1 - self.y) * 4, base_y, 4, 8, self.to_y),
            (base_y + (1 - self.kz) * 2, base_z, 2, 12, self.to_mate),
            (base_z + 1 - self.zin, base_z + self.zin, 1, 14, self.to_across),
        )[i]

    def bias_copy(self, i):
        start, _, size, land, to = self.bias_plan(i)
        return self.remote(
            self.bsum.at[pl.ds(start, size)],
            self.brecv.at[pl.ds(land, size)],
            self.c_sems.at[0, i],
            self.c_sems.at[1, i],
            to,
        )

    def bias_start(self):
        ones = jnp.where(lax.broadcasted_iota(jnp.int32, (PAD, self.rows), 0) == 0, 1.0, 0.0).astype(BF)
        width = 4 * self.hidden // 16
        for j in range(16):
            x, y, z = j % 2, (j // 2) % 2, j // 4
            place = x * 8 + y * 4 + 2 * (((z + 1) // 2) % 2) + z // 2
            self.bsum[place] = dot(ones, self.dz[:, j * width : (j + 1) * width])[0:8]
        self.bias_copy(0).start()

    def bias_step(self, i):
        self.bias_copy(i).wait_recv()
        _, start, size, land, _ = self.bias_plan(i)
        mine = pl.ds(start, size)
        self.bsum[mine] = self.bsum[mine] + self.brecv[land : land + size]
        if i < 3:
            self.bias_copy(i + 1).start()

    def run(self, blocks, brows, write_sequences, out_in, out_rec, out_bias, store_sem):
        act, win, wrec, proj = self.act, self.win, self.wrec, self.proj
        half, chunks = self.half, self.chunks

        def loop(body):
            def wrapped(k, carry):
                body(k)
                return carry

            lax.fori_loop(0, chunks, wrapped, 0)

        pl.semaphore_wait(self.ready, len(self.partners))
        self.bias_start()
        self.factor_copy(0).wait_recv()
        for b in range(blocks):
            self.dz_copy(0, b, brows).wait_recv()

        def other_a(k):
            at = self.cols(0, k)
            wrec[0:512, at] = self.product(self.fta, self.dza, self.ca, (1 - self.cb) * 512, k).astype(BF)
            self.a1(k).start()

        loop(other_a)
        self.bias_step(0)

        self.factor_copy(1).wait_recv()
        for b in range(blocks):
            self.dz_copy(1, b, brows).wait_recv()

        def other_b(k):
            at = self.cols(half, k)
            wrec[0:512, at] = self.product(self.ftb, self.dzb, self.zp, (1 - self.ca) * 512, k).astype(BF)
            self.b1(k).start()

        loop(other_b)
        self.bias_step(1)

        def own(k):
            act[:, self.cols(0, k)] = self.product(self.fta, self.dza, self.ca, self.cb * 512, k)
            act[:, self.cols(half, k)] = self.product(self.ftb, self.dzb, self.zp, self.ca * 512, k)

        loop(own)
        self.bias_step(2)

        def after_a1(k):
            at = self.cols(0, k)
            self.a1(k).wait_recv()
            away, mine = self.span((1 - self.kz) * 256, 256), self.span(self.kz * 256, 256)
            wrec[512:768, at] = (act[away, at] + win[away, at].astype(F32)).astype(BF)
            self.a2(k).start()
            act[mine, at] = act[mine, at] + win[mine, at].astype(F32)

        def after_a2(k):
            at = self.cols(0, k)
            self.a2(k).wait_recv()
            base = self.kz * 256
            away, mine = (1 - self.zin) * 128, self.zin * 128
            wrec[768:896, at] = (
                act[self.span(base + away, 128), at] + win[self.span(512 + away, 128), at].astype(F32)
            ).astype(BF)
            self.a3(k).start()
            kept = self.span(base + mine, 128)
            act[kept, at] = act[kept, at] + win[self.span(512 + mine, 128), at].astype(F32)

        def after_a3(k):
            at = self.cols(0, k)
            self.a3(k).wait_recv()
            base = self.kz * 256 + self.zin * 128
            away, mine = (1 - self.ca) * 64, self.ca * 64
            wrec[896:960, at] = (
                act[self.span(base + away, 64), at] + win[self.span(768 + away, 64), at].astype(F32)
            ).astype(BF)
            self.a4(k).start()
            proj[0:64, self.cols(self.ca * half, k)] = (
                act[self.span(base + mine, 64), at] + win[self.span(768 + mine, 64), at].astype(F32)
            )

        def after_a4(k):
            self.a4(k).wait_recv()
            proj[0:64, self.cols((1 - self.ca) * half, k)] = win[896:960, self.cols(0, k)].astype(F32)

        def after_b1(k):
            at = self.cols(half, k)
            self.b1(k).wait_recv()
            away, mine = self.span((1 - self.cb) * 256, 256), self.span(self.cb * 256, 256)
            wrec[512:768, at] = (act[away, at] + win[away, at].astype(F32)).astype(BF)
            self.b2(k).start()
            act[mine, at] = act[mine, at] + win[mine, at].astype(F32)

        def after_b2(k):
            at = self.cols(half, k)
            self.b2(k).wait_recv()
            base = self.cb * 256
            for i in range(3):
                block = ((self.z + 3 - i) % 4) * 64
                wrec[768 + 64 * i : 832 + 64 * i, at] = (
                    act[self.span(base + block, 64), at] + win[self.span(512 + block, 64), at].astype(F32)
                ).astype(BF)
                self.b3(k, i).start()
            block = self.z * 64
            kept = self.span(base + block, 64)
            act[kept, at] = act[kept, at] + win[self.span(512 + block, 64), at].astype(F32)

        def after_b3(k):
            at = self.cols(half, k)
            for i in range(3):
                self.b3(k, i).wait_recv()
            kept = self.span(self.cb * 256 + self.z * 64, 64)
            proj[64:128, self.cols(self.zp * half, k)] = act[kept, at] + win[832:896, at].astype(F32)
            proj[64:128, self.cols((1 - self.zp) * half, k)] = win[768:832, at].astype(F32) + win[
                896:960, at
            ].astype(F32)

        stages = ((after_a1, 0), (after_b1, 0), (after_a2, 1), (after_b2, 1), (after_a3, 2), (after_b3, 2), (after_a4, 3))
        write_sequences()

        def turn(n, carry):
            for work, lag in stages:
                k = n - lag
                pl.when((k >= 0) & (k < chunks))(lambda: work(k))
            return carry

        lax.fori_loop(0, chunks + 3, turn, 0)
        self.bias_step(3)

        mine = self.x * 8 + self.y * 4 + self.kz * 2 + self.zin
        self.brecv[0, 0:1, :] = jnp.sum(self.bsum[mine], axis=0, keepdims=True)
        bias_copy = pltpu.make_async_copy(self.brecv.at[0, pl.ds(0, 1)], out_bias, store_sem.at[4])
        bias_copy.start()

        def results(top, bottom):
            return (
                pltpu.make_async_copy(proj.at[pl.ds(0, 64)], top, store_sem.at[2]),
                pltpu.make_async_copy(proj.at[pl.ds(64, 64)], bottom, store_sem.at[3]),
            )

        @pl.when(self.first)
        def _():
            for copy in results(out_in, out_rec):
                copy.start()

        @pl.when(self.second)
        def _():
            for copy in results(out_rec, out_in):
                copy.start()

        for i in range(2):
            self.factor_copy(i).wait_send()
            for b in range(blocks):
                self.dz_copy(i, b, brows).wait_send()
        for i in range(4):
            self.bias_copy(i).wait_send()

        def sent(k):
            for part in (self.a1, self.a2, self.a3, self.a4, self.b1, self.b2):
                part(k).wait_send()
            for i in range(3):
                self.b3(k, i).wait_send()

        loop(sent)
        bias_copy.wait()
        for copy in results(out_in, out_rec):
            copy.wait()


def on_device(inputs, lengths, w_in, w_rec, bias, cotangent):
    micro, per, steps, feats = inputs.shape
    hidden = w_rec.shape[1]
    seqs = micro * per
    total = steps * seqs
    vmem = pltpu.VMEM
    blocks = steps // BLOCK
    shards = lax.axis_size("dp")
    fused = shards == 16
    if fused:
        last_three = (
            jax.ShapeDtypeStruct((feats // shards, 4 * hidden), F32),
            jax.ShapeDtypeStruct((hidden // shards, 4 * hidden), F32),
            jax.ShapeDtypeStruct((1, 4 * hidden // shards), F32),
        )
        chunks = 2 * hidden // CHUNK
        dma = pltpu.SemaphoreType.DMA
        more = [
            vmem((feats, 2 * total), BF),
            vmem((hidden, 2 * total), BF),
            vmem((total, 2 * hidden), BF),
            vmem((total, 2 * hidden), BF),
            vmem((16, 8, 4 * hidden // 16), F32),
            vmem((15, 8, 4 * hidden // 16), F32),
            pltpu.SemaphoreType.REGULAR,
            dma((2, 2)),
            dma((4, blocks)),
            dma((8, chunks)),
            dma((4, chunks)),
            dma((2, 3, chunks)),
            dma((2, 4)),
        ]
    else:
        last_three = (
            jax.ShapeDtypeStruct((total, feats), BF),
            jax.ShapeDtypeStruct((total, hidden), BF),
            jax.ShapeDtypeStruct((total, 4 * hidden), BF),
        )
        more = []
    hid, dx, *rest = pl.pallas_call(
        functools.partial(lstm_kernel, steps, seqs, fused),
        out_shape=(
            jax.ShapeDtypeStruct((total, hidden), BF),
            jax.ShapeDtypeStruct((total, feats), BF),
            *last_three,
        ),
        in_specs=[
            pl.BlockSpec(memory_space=pl.ANY),
            pl.BlockSpec(memory_space=pltpu.VMEM),
            pl.BlockSpec(memory_space=pl.ANY),
            pl.BlockSpec(memory_space=pl.ANY),
            pl.BlockSpec(memory_space=pl.ANY),
            pl.BlockSpec(memory_space=pl.ANY),
        ],
        out_specs=tuple(pl.BlockSpec(memory_space=pl.ANY) for _ in range(5)),
        scratch_shapes=[
            vmem((total, feats), BF),
            vmem((total + seqs, hidden), BF),
            vmem((total, hidden), BF),
            vmem((total, feats), BF),
            vmem((total, 4 * hidden), F32),
            vmem((total + seqs, hidden), F32),
            vmem((total, 4 * hidden), BF),
            vmem((BLOCK * seqs, 4 * hidden), F32),
            vmem((feats, 4 * hidden), BF),
            vmem((hidden, 4 * hidden), BF),
            vmem((4 * hidden, hidden), BF),
            vmem((4 * hidden, feats), BF),
            vmem((seqs, hidden), F32),
            vmem((seqs, hidden), F32),
            vmem((seqs, 128), F32),
            vmem((1, 4 * hidden), F32),
            pltpu.SemaphoreType.DMA((4,)),
            pltpu.SemaphoreType.DMA((5,)),
            pltpu.SemaphoreType.DMA((blocks,)),
            pltpu.SemaphoreType.DMA((blocks,)),
            pltpu.SemaphoreType.DMA((blocks,)),
            pltpu.SemaphoreType.DMA((blocks,)),
            *more,
        ],
        compiler_params=pltpu.CompilerParams(
            collective_id=0, has_side_effects=True, vmem_limit_bytes=63 * 2**20
        ),
        name="lstm_both_ways",
    )(
        inputs.reshape(total, feats),
        lengths,
        w_in[0],
        w_rec[0],
        bias,
        cotangent.reshape(total, hidden),
    )
    if fused:
        share_in, share_rec, share_bias = rest
    else:
        u, hp, dz = rest
        sum_in = lax.dot_general(u, dz, (((0,), (0,)), ((), ())), preferred_element_type=F32)
        sum_rec = lax.dot_general(hp, dz, (((0,), (0,)), ((), ())), preferred_element_type=F32)
        sum_bias = jnp.sum(dz, axis=0, dtype=F32)
        share_in = lax.psum_scatter(sum_in, "dp", scatter_dimension=0, tiled=True)
        share_rec = lax.psum_scatter(sum_rec, "dp", scatter_dimension=0, tiled=True)
        share_bias = lax.psum_scatter(sum_bias, "dp", scatter_dimension=0, tiled=True)[None]
    shape = inputs.shape
    return (
        hid.reshape(shape)[None],
        dx.reshape(shape)[None],
        share_in[None],
        share_rec[None],
        share_bias,
    )


def solution(mesh):
    placed = (
        P(None, "dp", None, None),
        P(None, "dp"),
        P("section", None, None),
        P("section", None, None),
        P("section", None),
        P(None, "dp", None, None),
    )
    return jax.shard_map(
        on_device,
        mesh=mesh,
        in_specs=placed,
        out_specs=(
            P("section", None, "dp", None, None),
            P("section", None, "dp", None, None),
            P("section", "dp", None),
            P("section", "dp", None),
            P("section", "dp"),
        ),
        check_vma=False,
    )
```

```python
import functools

import jax
import jax.numpy as jnp
from jax import lax
from jax.experimental import pallas as pl
from jax.experimental.pallas import tpu as pltpu
from jax.sharding import PartitionSpec as P

BF = jnp.bfloat16
F32 = jnp.float32
MESH = pl.DeviceIdType.MESH
BLOCK = 4
PAD = 128
TILE = 256
CHUNK = 256
PAIR = 2 * CHUNK


def sigmoid(v):
    return 0.5 * jnp.tanh(0.5 * v) + 0.5


def rows_at(start, size):
    return pl.ds(pl.multiple_of(start, size), size)


def dot(a, b):
    return jnp.dot(a, b, preferred_element_type=F32)


def dot_t(a, b):
    return lax.dot_general(a, b, (((1,), (1,)), ((), ())), preferred_element_type=F32)


def padded(rows):
    lack = PAD - rows.shape[0]
    return jnp.concatenate([rows, jnp.zeros((lack, rows.shape[1]), rows.dtype)], axis=0) if lack > 0 else rows


def z_place(z):
    return 2 * (((z + 1) // 2) % 2) + z // 2


def lstm_kernel(
    steps, seqs, fused,
    x_ref, len_ref, win_ref, wrec_ref, bias_ref, ct_ref,
    hid_out, dx_out, out_a, out_b, out_c,
    u, hs, dy, dx, act, cs, dz, win, wrec, wrt, wint, dr, dc, lens, bias,
    load_sem, store_sem, up_send, up_recv, down_send, down_recv, *more,
):
    hidden = wrec.shape[0]
    gates = 4 * hidden
    total = steps * seqs
    blocks = steps // BLOCK
    brows = BLOCK * seqs
    section = lax.axis_index("section")
    first = section == 0
    second = section == 1
    other = {"section": 1 - section}

    tail = Tail(section, seqs, brows, u, hs, act, cs, dz, win, wrec, wrt, *more) if fused else None

    barrier = pltpu.get_barrier_semaphore()
    pl.semaphore_signal(barrier, inc=1, device_id=other, device_id_type=MESH)
    if fused:
        for partner in tail.partners:
            pl.semaphore_signal(barrier, inc=1, device_id=partner, device_id_type=MESH)

    load_x = pltpu.make_async_copy(x_ref, dx, load_sem.at[0])
    load_ct = pltpu.make_async_copy(ct_ref, dx, load_sem.at[0])
    load_win = pltpu.make_async_copy(win_ref, win, load_sem.at[1])
    load_wrec = pltpu.make_async_copy(wrec_ref, wrec, load_sem.at[2])
    load_bias = pltpu.make_async_copy(bias_ref, bias, load_sem.at[3])
    pl.when(first)(lambda: load_x.start())
    pl.when(second)(lambda: load_ct.start())
    load_bias.start()
    load_win.start()
    load_wrec.start()

    micro, per = len_ref.shape
    row_id = lax.broadcasted_iota(jnp.int32, (per, per), 0)
    col_id = lax.broadcasted_iota(jnp.int32, (per, per), 1)
    for m in range(micro):
        row = jnp.broadcast_to(len_ref[m : m + 1, :].astype(F32), (per, per))
        column = jnp.sum(jnp.where(row_id == col_id, row, 0.0), axis=1, keepdims=True)
        lens[m * per : (m + 1) * per, :] = jnp.broadcast_to(column, (per, lens.shape[1]))

    hs[0:seqs, :] = jnp.zeros((seqs, hidden), BF)
    cs[0:seqs, :] = jnp.zeros((seqs, hidden), F32)
    dr[...] = jnp.zeros_like(dr)
    dc[...] = jnp.zeros_like(dc)
    if fused:
        tail.clear()

    def reorder(outer, inner, source, skip, perm, write):
        to_id = lax.broadcasted_iota(jnp.int32, (inner, total), 0)
        from_id = lax.broadcasted_iota(jnp.int32, (inner, total), 1)
        for n in range(outer):
            perm[n * inner : (n + 1) * inner, :] = jnp.where(to_id * outer + n == from_id, 1.0, 0.0).astype(BF)
        for j in range(0, hidden, TILE):
            cols = slice(j, j + TILE)
            write(cols, dot(perm[...], source[skip : skip + total, cols]).astype(BF))

    def write_first(cols, value):
        @pl.when(first)
        def _():
            u[:, cols] = value

        @pl.when(second)
        def _():
            dy[:, cols] = value

    load_x.wait()
    reorder(steps, seqs, dx, 0, wrt.at[0:total, 0:total], write_first)

    load_bias.wait()
    load_win.wait()

    eye = jnp.where(
        lax.broadcasted_iota(jnp.int32, (TILE, TILE), 0) == lax.broadcasted_iota(jnp.int32, (TILE, TILE), 1), 1.0, 0.0
    ).astype(BF)

    def turn_over(source, target):
        def piece(i, carry):
            at = rows_at(i * TILE, TILE)
            target[at, :] = dot_t(eye, source[:, at]).astype(BF)
            return carry

        lax.fori_loop(0, gates // TILE, piece, 0)

    @pl.when(second)
    def _():
        turn_over(win, wint)
        load_wrec.wait()
        turn_over(wrec, wrt)

    def arrived():
        pl.semaphore_wait(barrier, 1 + len(tail.partners) if fused else 1)

    def send_up(b):
        return pltpu.make_async_remote_copy(
            src_ref=hs.at[pl.ds(pl.multiple_of(b * brows + seqs, seqs), brows)],
            dst_ref=u.at[rows_at(b * brows, brows)],
            send_sem=up_send.at[b],
            recv_sem=up_recv.at[b],
            device_id=other,
            device_id_type=MESH,
        )

    def send_down(b):
        return pltpu.make_async_remote_copy(
            src_ref=dx.at[rows_at(b * brows, brows)],
            dst_ref=dy.at[rows_at(b * brows, brows)],
            send_sem=down_send.at[b],
            recv_sem=down_recv.at[b],
            device_id=other,
            device_id_type=MESH,
        )

    def forward_block(b, carry):
        pl.when(second)(lambda: send_up(b).wait_recv())
        block_rows = rows_at(b * brows, brows)

        def project(i, c):
            at = rows_at(i * TILE, TILE)
            act[block_rows, at] = dot(u[block_rows, :], win[:, at]) + bias[:, at]
            return c

        lax.fori_loop(0, gates // TILE, project, 0, unroll=4)
        pl.when(first & (b == 0))(lambda: load_wrec.wait())

        def step(k, c):
            t = b * BLOCK + k
            here = rows_at(t * seqs, seqs)
            after = rows_at((t + 1) * seqs, seqs)
            h_prev = padded(hs[here, :])
            mask = jnp.where(t.astype(F32) < lens[:, 0:1], 1.0, 0.0)
            for j in range(0, hidden, TILE):
                z = []
                for g in range(4):
                    cols = slice(g * hidden + j, g * hidden + j + TILE)
                    z.append(dot(h_prev, wrec[:, cols])[:seqs] + act[here, cols])
                gi, gf, gg, go = sigmoid(z[0]), sigmoid(z[1]), jnp.tanh(z[2]), sigmoid(z[3])
                c_new = gf * cs[here, j : j + TILE] + gi * gg
                cs[after, j : j + TILE] = c_new
                act[here, j : j + TILE] = gi
                act[here, hidden + j : hidden + j + TILE] = gf
                act[here, 2 * hidden + j : 2 * hidden + j + TILE] = gg
                act[here, 3 * hidden + j : 3 * hidden + j + TILE] = go
                hs[after, j : j + TILE] = (go * jnp.tanh(c_new) * mask).astype(BF)
            return c

        lax.fori_loop(0, BLOCK, step, 0)
        pl.when(b == 0)(arrived)
        pl.when(first)(lambda: send_up(b).start())
        if fused:
            tail.send_factors(b)
        return carry

    lax.fori_loop(0, blocks, forward_block, 0)

    @pl.when(first)
    def _():
        turn_over(wrec, wrt)
        turn_over(win, wint)

    if fused:
        pl.when(first)(lambda: tail.build_own(eye))
        tail.say_ready()

    def backward_block(i, carry):
        b = blocks - 1 - i
        pl.when(first)(lambda: send_down(b).wait_recv())

        def step(n, c):
            t = b * BLOCK + (BLOCK - 1 - n)
            here = rows_at(t * seqs, seqs)
            after = rows_at((t + 1) * seqs, seqs)
            mask = jnp.where(t.astype(F32) < lens[:, 0:1], 1.0, 0.0)
            for j in range(0, hidden, TILE):
                cols = slice(j, j + TILE)
                dh = dy[here, cols].astype(F32) * mask + dr[:, cols]
                gi = act[here, j : j + TILE]
                gf = act[here, hidden + j : hidden + j + TILE]
                gg = act[here, 2 * hidden + j : 2 * hidden + j + TILE]
                go = act[here, 3 * hidden + j : 3 * hidden + j + TILE]
                tc = jnp.tanh(cs[after, cols])
                e = dc[:, cols] + dh * go * (1.0 - tc * tc)
                dz[here, j : j + TILE] = (e * gg * gi * (1.0 - gi)).astype(BF)
                dz[here, hidden + j : hidden + j + TILE] = (e * cs[here, cols] * gf * (1.0 - gf)).astype(BF)
                dz[here, 2 * hidden + j : 2 * hidden + j + TILE] = (e * gi * (1.0 - gg * gg)).astype(BF)
                dz[here, 3 * hidden + j : 3 * hidden + j + TILE] = (dh * tc * go * (1.0 - go)).astype(BF)
                dc[:, cols] = e * gf
            dr[...] = dot(padded(dz[here, :]), wrt[...])[:seqs]
            return c

        lax.fori_loop(0, BLOCK, step, 0)
        block_rows = rows_at(b * brows, brows)
        if fused:
            pl.when(i == 0)(lambda: tail.wait_ready())
            tail.send_dz(b)

        @pl.when(second)
        def _():
            dx[block_rows, :] = dot(dz[block_rows, :], wint[...]).astype(BF)
            send_down(b).start()

        return carry

    lax.fori_loop(0, blocks, backward_block, 0)

    def write_hidden(perm):
        def write_u(cols, value):
            u[:, cols] = value

        reorder(seqs, steps, hs, seqs, perm, write_u)
        pltpu.make_async_copy(u, hid_out, store_sem.at[0]).start()

    def write_grads(perm):
        def write_dy(cols, value):
            dy[:, cols] = value

        @pl.when(first)
        def _():
            for j in range(0, hidden, TILE):
                dx[:, j : j + TILE] = dot(dz[...], wint[:, j : j + TILE]).astype(BF)

        reorder(seqs, steps, dx, 0, perm, write_dy)
        pltpu.make_async_copy(dy, dx_out, store_sem.at[1]).start()

    if fused:
        pl.when(second)(lambda: tail.build_own(eye))
        tail.run(eye, blocks, write_hidden, write_grads, out_a, out_b, out_c, store_sem)
    else:
        stores = [
            pltpu.make_async_copy(u, out_a, store_sem.at[2]),
            pltpu.make_async_copy(hs.at[pl.ds(0, total)], out_b, store_sem.at[3]),
            pltpu.make_async_copy(dz, out_c, store_sem.at[4]),
        ]
        for copy in stores:
            copy.start()
        for copy in stores:
            copy.wait()
        write_hidden(wrt.at[0:total, 0:total])
        write_grads(wrt.at[0:total, 0:total])
    pltpu.make_async_copy(u, hid_out, store_sem.at[0]).wait()
    pltpu.make_async_copy(dy, dx_out, store_sem.at[1]).wait()
    for b in range(blocks):
        pl.when(first)(lambda: send_up(b).wait_send())
        pl.when(second)(lambda: send_down(b).wait_send())


class Tail:
    def __init__(self, section, seqs, brows, u, hs, act, cs, dz, win, wrec, wrt,
                 u_a, h_a, u_z, h_z, bsum, brecv, ready,
                 f_sems, dz_sems, p_sems, z_sems, all_sems, c_sems):
        self.s, self.seqs, self.brows = section, seqs, brows
        self.first, self.second = section == 0, section == 1
        self.hidden = wrec.shape[0]
        self.quarter = self.hidden
        self.u, self.hs, self.act, self.cs, self.dz = u, hs, act, cs, dz
        self.win, self.wrec, self.wrt = win, wrec, wrt
        self.u_a, self.h_a, self.u_z, self.h_z = u_a, h_a, u_z, h_z
        self.bsum, self.brecv, self.ready = bsum, brecv, ready
        self.f_sems, self.dz_sems, self.p_sems = f_sems, dz_sems, p_sems
        self.z_sems, self.all_sems, self.c_sems = z_sems, all_sems, c_sems
        j = lax.axis_index("dp")
        x, y, z = j % 2, (j // 2) % 2, j // 4
        s = section
        self.x, self.y, self.z = x, y, z
        self.ca = x * (1 - s) + y * s
        self.cb = y * (1 - s) + x * s
        self.zp, self.zin, self.kz = z % 2, z // 2, ((z + 1) // 2) % 2
        jx, jy = j + 1 - 2 * x, j + 2 - 4 * y
        self.to_x, self.to_y = {"dp": jx}, {"dp": jy}
        self.to_a = {"dp": jx * (1 - s) + jy * s}
        self.to_b = {"dp": jy * (1 - s) + jx * s}
        self.to_mate = {"dp": j + 4 - 8 * self.zp}
        self.to_across = {"dp": j + 4 * (3 - 2 * z)}
        self.to_z = [{"dp": j - 4 * z + 4 * ((z + 3 - i) % 4)} for i in range(3)]
        self.partners = [self.to_x, self.to_y] + self.to_z
        self.rows = dz.shape[0]
        self.chunks = self.quarter // CHUNK
        self.unit = self.hidden // 16
        rows = self.rows
        self.ut = win.at[:, 0 : 3 * rows]
        self.ht = win.at[:, 3 * rows : 6 * rows]
        self.dz_theirs = (
            win.at[0:rows, 6 * rows : 6 * rows + self.quarter],
            win.at[rows : 2 * rows, 6 * rows : 6 * rows + self.quarter],
        )

    def remote(self, src, dst, send, recv, to):
        return pltpu.make_async_remote_copy(
            src_ref=src, dst_ref=dst, send_sem=send, recv_sem=recv, device_id=to, device_id_type=MESH
        )

    def clear(self):
        zeros = jnp.zeros((self.seqs, self.hidden), BF)
        self.h_a[0 : self.seqs, :] = zeros
        self.h_z[0 : self.seqs, :] = zeros


    def factor(self, i, b):
        at_u = pl.ds(pl.multiple_of(b * self.brows, self.brows), self.brows)
        at_h = pl.ds(pl.multiple_of(b * self.brows + self.seqs, self.seqs), self.brows)
        src, dst, at, to = (
            (self.u, self.u_a, at_u, self.to_a),
            (self.hs, self.h_a, at_h, self.to_a),
            (self.u, self.u_z, at_u, self.to_mate),
            (self.hs, self.h_z, at_h, self.to_mate),
        )[i]
        return self.remote(src.at[at], dst.at[at], self.f_sems.at[0, i, b], self.f_sems.at[1, i, b], to)

    def send_factors(self, b):
        for i in range(4):
            self.factor(i, b).start()

    def say_ready(self):
        for partner in self.partners:
            pl.semaphore_signal(self.ready, inc=1, device_id=partner, device_id_type=MESH)

    def wait_ready(self):
        pl.semaphore_wait(self.ready, len(self.partners))

    def dz_copy(self, i, b):
        at = pl.ds(pl.multiple_of(b * self.brows, self.brows), self.brows)
        start = (1 - self.ca) * self.quarter if i == 0 else (3 - self.zp) * self.quarter
        cols = pl.ds(pl.multiple_of(start, self.quarter), self.quarter)
        return self.remote(
            self.dz.at[at, cols],
            self.dz_theirs[i].at[at],
            self.dz_sems.at[2 * i, b],
            self.dz_sems.at[2 * i + 1, b],
            (self.to_a, self.to_mate)[i],
        )

    def send_dz(self, b):
        for i in range(2):
            self.dz_copy(i, b).start()

    def build_own(self, eye):
        self.build(eye, self.u, self.ut, 0)
        self.build(eye, self.hs, self.ht, 0)

    def build(self, eye, source, target, part):
        unit, rows = self.unit, self.rows

        def place(j):
            x, y, z = j % 2, (j // 2) % 2, j // 4
            a = x * (1 - self.s) + y * self.s
            b = y * (1 - self.s) + x * self.s
            return b * 8 + z_place(z) * 2 + a

        for f in range(self.hidden // TILE):
            turned = dot_t(eye, source[0:rows, f * TILE : (f + 1) * TILE]).astype(BF)
            for i in range(TILE // unit):
                at = pl.ds(pl.multiple_of(place(f * (TILE // unit) + i) * unit, unit), unit)
                target[at, part * rows : (part + 1) * rows] = turned[i * unit : (i + 1) * unit, :]


    def cols(self, c):
        return pl.ds(pl.multiple_of(c * PAIR, PAIR), PAIR)

    def staged(self, c, row, size):
        wide = self.hidden // PAIR
        return (
            pl.ds(pl.multiple_of((c // wide) * self.hidden + row, 64), size),
            pl.ds(pl.multiple_of((c % wide) * PAIR, PAIR), PAIR),
        )

    def moved(self, c, row, size, sems, to):
        return self.remote(
            self.wrt.at[self.staged(c, row, size)], self.wrec.at[pl.ds(row, size), self.cols(c)], *sems, to
        )

    def along_b(self, c):
        return self.moved(c, 0, 512, (self.p_sems.at[0, c], self.p_sems.at[1, c]), self.to_b)

    def p_mate(self, c):
        return self.moved(c, 512, 256, (self.p_sems.at[2, c], self.p_sems.at[3, c]), self.to_mate)

    def p_across(self, c):
        return self.moved(c, 768, 128, (self.p_sems.at[4, c], self.p_sems.at[5, c]), self.to_across)

    def p_swap(self, c):
        return self.moved(c, 896, 64, (self.p_sems.at[6, c], self.p_sems.at[7, c]), self.to_a)

    def z_along_a(self, c):
        n = c - self.chunks
        return self.moved(c, 512, 256, (self.z_sems.at[0, n], self.z_sems.at[1, n]), self.to_a)

    def z_all(self, c, i):
        n = c - self.chunks
        sems = (self.all_sems.at[0, i, n], self.all_sems.at[1, i, n])
        return self.moved(c, 768 + 64 * i, 64, sems, self.to_z[i])

    def product(self, c, part, mine, row):
        rows = self.rows
        at = pl.ds(pl.multiple_of(row, 512), 512)
        n = c - (part - 1) * self.chunks
        own = self.dz[:, pl.ds(pl.multiple_of(mine * self.quarter + n * CHUNK, CHUNK), CHUNK)]
        theirs = self.dz_theirs[part - 1][:, pl.ds(pl.multiple_of(n * CHUNK, CHUNK), CHUNK)]
        return [
            dot(ref[at, 0:rows], own) + dot(ref[at, part * rows : (part + 1) * rows], theirs)
            for ref in (self.ut, self.ht)
        ]

    def bias_plan(self, i):
        one = self.kz * 8
        two = one + self.zin * 4
        three = two + self.ca * 2
        return (
            ((1 - self.kz) * 8, one, 8, 0, self.to_mate),
            (one + (1 - self.zin) * 4, two, 4, 8, self.to_across),
            (two + (1 - self.ca) * 2, three, 2, 12, self.to_a),
            (three + 1 - self.cb, three + self.cb, 1, 14, self.to_b),
        )[i]

    def bias_copy(self, i):
        start, _, size, land, to = self.bias_plan(i)
        return self.remote(
            self.bsum.at[pl.ds(start, size)],
            self.brecv.at[pl.ds(land, size)],
            self.c_sems.at[0, i],
            self.c_sems.at[1, i],
            to,
        )

    def bias_start(self):
        ones = jnp.where(lax.broadcasted_iota(jnp.int32, (PAD, self.rows), 0) == 0, 1.0, 0.0).astype(BF)
        width = 4 * self.hidden // 16
        for j in range(16):
            x, y, z = j % 2, (j // 2) % 2, j // 4
            a = x * (1 - self.s) + y * self.s
            b = y * (1 - self.s) + x * self.s
            self.bsum[z_place(z) * 4 + a * 2 + b] = dot(ones, self.dz[:, j * width : (j + 1) * width])[0:8]
        self.bias_copy(0).start()

    def bias_step(self, i):
        self.bias_copy(i).wait_recv()
        _, start, size, land, _ = self.bias_plan(i)
        mine = pl.ds(start, size)
        self.bsum[mine] = self.bsum[mine] + self.brecv[land : land + size]
        if i < 3:
            self.bias_copy(i + 1).start()

    def put(self, q, c, value):
        n = c % self.chunks
        at = pl.ds(pl.multiple_of(n * CHUNK, CHUNK), CHUNK)
        for g in range(2):
            rows = pl.ds(pl.multiple_of((g * 4 + q) * self.unit, self.unit), self.unit)
            self.cs[rows, at] = value[:, g * CHUNK : (g + 1) * CHUNK]

    def run(self, eye, blocks, write_hidden, write_grads, out_in, out_rec, out_bias, store_sem):
        act, wrec, wrt = self.act, self.wrec, self.wrt
        chunks = self.chunks

        def loop(start, stop, body):
            def wrapped(c, carry):
                body(c)
                return carry

            lax.fori_loop(start, stop, wrapped, 0)

        def span(start, size):
            return pl.ds(pl.multiple_of(start, size), size)

        def arrive(i):
            for b in range(blocks):
                self.factor(i, b).wait_recv()

        self.bias_start()
        arrive(0)
        arrive(1)
        self.build(eye, self.u_a, self.ut, 1)
        self.build(eye, self.h_a, self.ht, 1)
        for b in range(blocks):
            self.dz_copy(0, b).wait_recv()

        def away(part, mine):
            def body(c):
                for g, value in enumerate(self.product(c, part, mine, (1 - self.cb) * 512)):
                    rows, cols = self.staged(c, 0, 512)
                    wide = self.hidden // PAIR
                    cols = pl.ds(pl.multiple_of((c % wide) * PAIR + g * CHUNK, CHUNK), CHUNK)
                    wrt[rows, cols] = value.astype(BF)
                self.along_b(c).start()

            return body

        def kept(part, mine):
            def body(c):
                for g, value in enumerate(self.product(c, part, mine, self.cb * 512)):
                    act[:, pl.ds(pl.multiple_of(c * PAIR + g * CHUNK, CHUNK), CHUNK)] = value

            return body

        loop(0, chunks, away(1, self.ca))
        loop(0, chunks, kept(1, self.ca))

        def z_away():
            arrive(2)
            arrive(3)
            self.build(eye, self.u_z, self.ut, 2)
            self.build(eye, self.h_z, self.ht, 2)
            for b in range(blocks):
                self.dz_copy(1, b).wait_recv()
            loop(chunks, 2 * chunks, away(2, 2 + self.zp))

        def sequences():
            for b in range(blocks):
                for i in range(4):
                    self.factor(i, b).wait_send()
            write_hidden(self.u_a.at[:, 0 : self.rows])
            write_grads(self.u_a.at[:, 0 : self.rows])

        extra = {
            0: z_away,
            1: lambda: loop(chunks, 2 * chunks, kept(2, 2 + self.zp)),
            2: lambda: self.bias_step(0),
            3: sequences,
            4: lambda: self.bias_step(1),
            6: lambda: self.bias_step(2),
        }

        def add(kept_rows, landed, at):
            act[kept_rows, at] = act[kept_rows, at] + wrec[landed, at].astype(F32)

        def send_sum(c, row, size, from_rows, landed):
            at = self.cols(c)
            wrt[self.staged(c, row, size)] = (act[from_rows, at] + wrec[landed, at].astype(F32)).astype(BF)

        def p_after_b(c):
            self.along_b(c).wait_recv()
            theirs, mine = span((1 - self.kz) * 256, 256), span(self.kz * 256, 256)
            send_sum(c, 512, 256, theirs, theirs)
            self.p_mate(c).start()
            add(mine, mine, self.cols(c))

        def p_after_mate(c):
            self.p_mate(c).wait_recv()
            base = self.kz * 256
            theirs, mine = (1 - self.zin) * 128, self.zin * 128
            send_sum(c, 768, 128, span(base + theirs, 128), span(512 + theirs, 128))
            self.p_across(c).start()
            add(span(base + mine, 128), span(512 + mine, 128), self.cols(c))

        def p_after_across(c):
            self.p_across(c).wait_recv()
            at = self.cols(c)
            base = self.kz * 256 + self.zin * 128
            theirs, mine = (1 - self.ca) * 64, self.ca * 64
            send_sum(c, 896, 64, span(base + theirs, 64), span(768 + theirs, 64))
            self.p_swap(c).start()
            self.put(self.ca, c, act[span(base + mine, 64), at] + wrec[span(768 + mine, 64), at].astype(F32))

        def p_after_swap(c):
            self.p_swap(c).wait_recv()
            self.put(1 - self.ca, c, wrec[896:960, self.cols(c)].astype(F32))

        def z_after_b(c):
            self.along_b(c).wait_recv()
            for i in range(4):
                theirs, mine = (2 * i + 1 - self.ca) * 64, (2 * i + self.ca) * 64
                send_sum(c, 512 + 64 * i, 64, span(theirs, 64), span(theirs, 64))
                add(span(mine, 64), span(mine, 64), self.cols(c))
            self.z_along_a(c).start()

        def z_after_a(c):
            self.z_along_a(c).wait_recv()
            for i in range(3):
                place = z_place((self.z + 3 - i) % 4)
                send_sum(c, 768 + 64 * i, 64, span((2 * place + self.ca) * 64, 64), span(512 + place * 64, 64))
                self.z_all(c, i).start()
            place = z_place(self.z)
            add(span((2 * place + self.ca) * 64, 64), span(512 + place * 64, 64), self.cols(c))

        def z_after_all(c):
            for i in range(3):
                self.z_all(c, i).wait_recv()
            at = self.cols(c)
            mine = span((2 * z_place(self.z) + self.ca) * 64, 64)
            self.put(2 + self.zp, c, act[mine, at] + wrec[832:896, at].astype(F32))
            self.put(3 - self.zp, c, wrec[768:832, at].astype(F32) + wrec[896:960, at].astype(F32))

        stages = (
            (p_after_b, 0, 0), (p_after_mate, 0, 1), (p_after_across, 0, 2), (p_after_swap, 0, 3),
            (z_after_b, chunks, 0), (z_after_a, chunks, 1), (z_after_all, chunks, 2),
        )

        def turn(n, carry):
            for work, start, lag in stages:
                c = n - lag
                pl.when((c >= start) & (c < start + chunks))(lambda: work(c))
            for at, work in extra.items():
                pl.when(n == at)(work)
            return carry

        lax.fori_loop(0, 2 * chunks + 2, turn, 0)
        self.bias_step(3)

        mine = self.bias_plan(3)[1]
        self.brecv[0, 0:1, :] = jnp.sum(self.bsum[mine], axis=0, keepdims=True)
        bias_store = pltpu.make_async_copy(self.brecv.at[0, pl.ds(0, 1)], out_bias, store_sem.at[2])
        bias_store.start()

        def result(n):
            g, q = n // 4, n % 4
            out = (out_in, out_rec)[g]
            rows = pl.ds(n * self.unit, self.unit)
            return pltpu.make_async_copy(
                self.cs.at[rows], out.at[:, pl.ds(q * self.quarter, self.quarter)], store_sem.at[3 + n]
            )

        for n in range(8):
            result(n).start()

        for b in range(blocks):
            for i in range(2):
                self.dz_copy(i, b).wait_send()
        for i in range(4):
            self.bias_copy(i).wait_send()

        def p_sent(c):
            for part in (self.along_b, self.p_mate, self.p_across, self.p_swap):
                part(c).wait_send()

        def z_sent(c):
            self.along_b(c).wait_send()
            self.z_along_a(c).wait_send()
            for i in range(3):
                self.z_all(c, i).wait_send()

        loop(0, chunks, p_sent)
        loop(chunks, 2 * chunks, z_sent)
        bias_store.wait()
        for n in range(8):
            result(n).wait()


def deliver_kernel(count, *refs):
    sources, targets, held, sems = refs[:count], refs[count : 2 * count], refs[2 * count : 3 * count], refs[3 * count]
    loads = [pltpu.make_async_copy(sources[i], held[i], sems.at[0, i]) for i in range(count)]
    stores = [pltpu.make_async_copy(held[i], targets[i], sems.at[1, i]) for i in range(count)]
    for copy in loads:
        copy.start()
    for load, store in zip(loads, stores):
        load.wait()
        store.start()
    for copy in stores:
        copy.wait()


def deliver(arrays):
    anywhere = [pl.BlockSpec(memory_space=pl.ANY)] * len(arrays)
    return pl.pallas_call(
        functools.partial(deliver_kernel, len(arrays)),
        out_shape=tuple(jax.ShapeDtypeStruct(a.shape, a.dtype) for a in arrays),
        in_specs=anywhere,
        out_specs=tuple(anywhere),
        scratch_shapes=[pltpu.VMEM(a.shape, a.dtype) for a in arrays] + [pltpu.SemaphoreType.DMA((2, len(arrays)))],
        compiler_params=pltpu.CompilerParams(vmem_limit_bytes=16 * 2**20),
        name="deliver",
    )(*arrays)


def on_device(inputs, lengths, w_in, w_rec, bias, cotangent):
    micro, per, steps, feats = inputs.shape
    hidden = w_rec.shape[1]
    seqs = micro * per
    total = steps * seqs
    vmem = pltpu.VMEM
    dma = pltpu.SemaphoreType.DMA
    blocks = steps // BLOCK
    shards = lax.axis_size("dp")
    fused = shards == 16
    if fused:
        last_three = (
            jax.ShapeDtypeStruct((feats // shards, 4 * hidden), F32),
            jax.ShapeDtypeStruct((hidden // shards, 4 * hidden), F32),
            jax.ShapeDtypeStruct((1, 4 * hidden // shards), F32),
        )
        chunks = hidden // CHUNK
        more = [
            vmem((total, feats), BF),
            vmem((total + seqs, hidden), BF),
            vmem((total, feats), BF),
            vmem((total + seqs, hidden), BF),
            vmem((16, 8, 4 * hidden // 16), F32),
            vmem((15, 8, 4 * hidden // 16), F32),
            pltpu.SemaphoreType.REGULAR,
            dma((2, 4, blocks)),
            dma((4, blocks)),
            dma((8, 2 * chunks)),
            dma((2, chunks)),
            dma((2, 3, chunks)),
            dma((2, 4)),
        ]
    else:
        last_three = (
            jax.ShapeDtypeStruct((total, feats), BF),
            jax.ShapeDtypeStruct((total, hidden), BF),
            jax.ShapeDtypeStruct((total, 4 * hidden), BF),
        )
        more = []
    anywhere = pl.BlockSpec(memory_space=pl.ANY)
    results = pl.pallas_call(
        functools.partial(lstm_kernel, steps, seqs, fused),
        out_shape=(
            jax.ShapeDtypeStruct((total, hidden), BF),
            jax.ShapeDtypeStruct((total, feats), BF),
            *last_three,
        ),
        in_specs=[anywhere, pl.BlockSpec(memory_space=pltpu.VMEM)] + [anywhere] * 4,
        out_specs=(anywhere,) * 5,
        scratch_shapes=[
            vmem((total, feats), BF),
            vmem((total + seqs, hidden), BF),
            vmem((total, hidden), BF),
            vmem((total, feats), BF),
            vmem((total, 4 * hidden), F32),
            vmem((total + seqs, hidden), F32),
            vmem((total, 4 * hidden), BF),
            vmem((feats, 4 * hidden), BF),
            vmem((hidden, 4 * hidden), BF),
            vmem((4 * hidden, hidden), BF),
            vmem((4 * hidden, feats), BF),
            vmem((seqs, hidden), F32),
            vmem((seqs, hidden), F32),
            vmem((seqs, 128), F32),
            vmem((1, 4 * hidden), F32),
            dma((4,)),
            dma((11,)),
            dma((blocks,)),
            dma((blocks,)),
            dma((blocks,)),
            dma((blocks,)),
            *more,
        ],
        compiler_params=pltpu.CompilerParams(
            collective_id=0, has_side_effects=True, vmem_limit_bytes=62 * 2**20
        ),
        name="lstm_both_ways",
    )(
        inputs.reshape(total, feats),
        lengths,
        w_in[0],
        w_rec[0],
        bias,
        cotangent.reshape(total, hidden),
    )
    if fused:
        hid, dx, share_in, share_rec, share_bias = deliver(results)
    else:
        hid, dx, u, hp, dz = results
        sum_in = lax.dot_general(u, dz, (((0,), (0,)), ((), ())), preferred_element_type=F32)
        sum_rec = lax.dot_general(hp, dz, (((0,), (0,)), ((), ())), preferred_element_type=F32)
        sum_bias = jnp.sum(dz, axis=0, dtype=F32)
        share_in = lax.psum_scatter(sum_in, "dp", scatter_dimension=0, tiled=True)
        share_rec = lax.psum_scatter(sum_rec, "dp", scatter_dimension=0, tiled=True)
        share_bias = lax.psum_scatter(sum_bias, "dp", scatter_dimension=0, tiled=True)[None]
    shape = inputs.shape
    return (
        hid.reshape(shape)[None],
        dx.reshape(shape)[None],
        share_in[None],
        share_rec[None],
        share_bias,
    )


def solution(mesh):
    placed = (
        P(None, "dp", None, None),
        P(None, "dp"),
        P("section", None, None),
        P("section", None, None),
        P("section", None),
        P(None, "dp", None, None),
    )
    return jax.shard_map(
        on_device,
        mesh=mesh,
        in_specs=placed,
        out_specs=(
            P("section", None, "dp", None, None),
            P("section", None, "dp", None, None),
            P("section", "dp", None),
            P("section", "dp", None),
            P("section", "dp"),
        ),
        check_vma=False,
    )
```

```python
import functools

import jax
import jax.numpy as jnp
from jax import lax
from jax.experimental import pallas as pl
from jax.experimental.pallas import tpu as pltpu
from jax.sharding import PartitionSpec as P

BF = jnp.bfloat16
F32 = jnp.float32
MESH = pl.DeviceIdType.MESH
BLOCK = 4
EDGE = 2
PAD = 128
TILE = 256
CHUNK = 256
SOON = True
AHEAD = 2
LATER = 0


def sigmoid(v):
    return 0.5 * jnp.tanh(0.5 * v) + 0.5


def rows_at(start, size):
    return pl.ds(pl.multiple_of(start, size), size)


def dot(a, b):
    return jnp.dot(a, b, preferred_element_type=F32)


def dot_t(a, b):
    return lax.dot_general(a, b, (((1,), (1,)), ((), ())), preferred_element_type=F32)


def padded(rows):
    lack = PAD - rows.shape[0]
    return jnp.concatenate([rows, jnp.zeros((lack, rows.shape[1]), rows.dtype)], axis=0) if lack > 0 else rows


def block_count(steps):
    return 2 + (steps - 2 * EDGE) // BLOCK


def block_span(steps, b):
    if isinstance(b, int):
        if b == 0:
            return 0, EDGE
        if b == block_count(steps) - 1:
            return steps - EDGE, EDGE
    return EDGE + (b - 1) * BLOCK, BLOCK


def z_place(z):
    return 2 * (((z + 1) // 2) % 2) + z // 2


def lstm_kernel(
    steps, seqs, fused,
    x_ref, len_ref, win_ref, wrec_ref, bias_ref, ct_ref,
    hid_out, dx_out, out_a, out_b, out_c,
    u, hs, dy, dx, act, cs, dz, win, wrec, wrt, wint, dr, dc, lens, bias,
    load_sem, store_sem, up_send, up_recv, down_send, down_recv, *more,
):
    hidden = wrec.shape[0]
    gates = 4 * hidden
    total = steps * seqs
    blocks = block_count(steps)
    section = lax.axis_index("section")
    first = section == 0
    second = section == 1
    other = {"section": 1 - section}

    tail = Tail(section, seqs, steps, u, hs, act, cs, dz, win, wrec, wrt, *more) if fused else None

    barrier = pltpu.get_barrier_semaphore()
    pl.semaphore_signal(barrier, inc=1, device_id=other, device_id_type=MESH)
    if fused:
        for partner in tail.partners:
            pl.semaphore_signal(barrier, inc=1, device_id=partner, device_id_type=MESH)

    load_x = pltpu.make_async_copy(x_ref, dx, load_sem.at[0])
    load_ct = pltpu.make_async_copy(ct_ref, dx, load_sem.at[0])
    load_win = pltpu.make_async_copy(win_ref, win, load_sem.at[1])
    load_wrec = pltpu.make_async_copy(wrec_ref, wrec, load_sem.at[2])
    load_bias = pltpu.make_async_copy(bias_ref, bias, load_sem.at[3])
    pl.when(first)(lambda: load_x.start())
    pl.when(second)(lambda: load_ct.start())
    load_bias.start()
    load_win.start()
    load_wrec.start()

    micro, per = len_ref.shape
    row_id = lax.broadcasted_iota(jnp.int32, (per, per), 0)
    col_id = lax.broadcasted_iota(jnp.int32, (per, per), 1)
    for m in range(micro):
        row = jnp.broadcast_to(len_ref[m : m + 1, :].astype(F32), (per, per))
        column = jnp.sum(jnp.where(row_id == col_id, row, 0.0), axis=1, keepdims=True)
        lens[m * per : (m + 1) * per, :] = jnp.broadcast_to(column, (per, lens.shape[1]))

    hs[0:seqs, :] = jnp.zeros((seqs, hidden), BF)
    cs[0:seqs, :] = jnp.zeros((seqs, hidden), F32)
    dr[...] = jnp.zeros_like(dr)
    dc[...] = jnp.zeros_like(dc)
    if fused:
        tail.clear()

    def reorder(outer, inner, source, skip, perm, write):
        to_id = lax.broadcasted_iota(jnp.int32, (inner, total), 0)
        from_id = lax.broadcasted_iota(jnp.int32, (inner, total), 1)
        for n in range(outer):
            perm[n * inner : (n + 1) * inner, :] = jnp.where(to_id * outer + n == from_id, 1.0, 0.0).astype(BF)
        for j in range(0, hidden, TILE):
            cols = slice(j, j + TILE)
            write(cols, dot(perm[...], source[skip : skip + total, cols]).astype(BF))

    def write_first(cols, value):
        @pl.when(first)
        def _():
            u[:, cols] = value

        @pl.when(second)
        def _():
            dy[:, cols] = value

    load_x.wait()
    reorder(steps, seqs, dx, 0, wrt.at[0:total, 0:total], write_first)

    load_bias.wait()
    load_win.wait()

    eye = jnp.where(
        lax.broadcasted_iota(jnp.int32, (TILE, TILE), 0) == lax.broadcasted_iota(jnp.int32, (TILE, TILE), 1), 1.0, 0.0
    ).astype(BF)

    def turn_over(source, target):
        def piece(i, carry):
            at = rows_at(i * TILE, TILE)
            target[at, :] = dot_t(eye, source[:, at]).astype(BF)
            return carry

        lax.fori_loop(0, gates // TILE, piece, 0)

    @pl.when(second)
    def _():
        turn_over(win, wint)
        load_wrec.wait()
        turn_over(wrec, wrt)

    def arrived():
        pl.semaphore_wait(barrier, 1 + len(tail.partners) if fused else 1)

    def rows_of(b, shift=0):
        start, length = block_span(steps, b)
        return pl.ds(pl.multiple_of((start + shift) * seqs, seqs), length * seqs)

    def send_up(b):
        return pltpu.make_async_remote_copy(
            src_ref=hs.at[rows_of(b, 1)],
            dst_ref=u.at[rows_of(b)],
            send_sem=up_send.at[b],
            recv_sem=up_recv.at[b],
            device_id=other,
            device_id_type=MESH,
        )

    def send_down(b):
        return pltpu.make_async_remote_copy(
            src_ref=dx.at[rows_of(b)],
            dst_ref=dy.at[rows_of(b)],
            send_sem=down_send.at[b],
            recv_sem=down_recv.at[b],
            device_id=other,
            device_id_type=MESH,
        )

    def cell(t, recur):
        here = rows_at(t * seqs, seqs)
        after = rows_at((t + 1) * seqs, seqs)
        h_prev = padded(hs[here, :]) if recur else None
        mask = jnp.where(jnp.float32(t) < lens[:, 0:1], 1.0, 0.0)
        for j in range(0, hidden, TILE):
            z = []
            for g in range(4):
                cols = slice(g * hidden + j, g * hidden + j + TILE)
                z.append(act[here, cols] + dot(h_prev, wrec[:, cols])[:seqs] if recur else act[here, cols])
            gi, gf, gg, go = sigmoid(z[0]), sigmoid(z[1]), jnp.tanh(z[2]), sigmoid(z[3])
            c_new = gf * cs[here, j : j + TILE] + gi * gg if recur else gi * gg
            cs[after, j : j + TILE] = c_new
            act[here, j : j + TILE] = gi
            act[here, hidden + j : hidden + j + TILE] = gf
            act[here, 2 * hidden + j : 2 * hidden + j + TILE] = gg
            act[here, 3 * hidden + j : 3 * hidden + j + TILE] = go
            hs[after, j : j + TILE] = (go * jnp.tanh(c_new) * mask).astype(BF)

    def forward_block(b):
        pl.when(second)(lambda: send_up(b).wait_recv())
        start, length = block_span(steps, b)
        here = rows_of(b)
        given = u[here, :]
        given = padded(given)
        for j in range(0, gates, TILE):
            act[here, j : j + TILE] = dot(given, win[:, j : j + TILE])[: length * seqs] + bias[:, j : j + TILE]
        for k in range(length):
            at_zero = isinstance(b, int) and b == 0 and k == 0
            cell(start + k, not at_zero)
            if at_zero:
                pl.when(first)(lambda: load_wrec.wait())
        if isinstance(b, int) and b == 0:
            arrived()
        pl.when(first)(lambda: send_up(b).start())
        if fused:
            tail.send_factors(b)

    def each_inner(body):
        def wrapped(b, carry):
            body(b)
            return carry

        lax.fori_loop(1, blocks - 1, wrapped, 0)

    forward_block(0)
    each_inner(forward_block)
    forward_block(blocks - 1)

    @pl.when(first)
    def _():
        turn_over(wrec, wrt)
        turn_over(win, wint)

    if fused:
        pl.when(first)(lambda: tail.build_own(eye))
        tail.say_ready()

    def cell_back(t, more_to_come):
        here = rows_at(t * seqs, seqs)
        after = rows_at((t + 1) * seqs, seqs)
        mask = jnp.where(jnp.float32(t) < lens[:, 0:1], 1.0, 0.0)
        for j in range(0, hidden, TILE):
            cols = slice(j, j + TILE)
            dh = dy[here, cols].astype(F32) * mask + dr[:, cols]
            gi = act[here, j : j + TILE]
            gf = act[here, hidden + j : hidden + j + TILE]
            gg = act[here, 2 * hidden + j : 2 * hidden + j + TILE]
            go = act[here, 3 * hidden + j : 3 * hidden + j + TILE]
            tc = jnp.tanh(cs[after, cols])
            e = dc[:, cols] + dh * go * (1.0 - tc * tc)
            dz[here, j : j + TILE] = (e * gg * gi * (1.0 - gi)).astype(BF)
            dz[here, hidden + j : hidden + j + TILE] = (e * cs[here, cols] * gf * (1.0 - gf)).astype(BF)
            dz[here, 2 * hidden + j : 2 * hidden + j + TILE] = (e * gi * (1.0 - gg * gg)).astype(BF)
            dz[here, 3 * hidden + j : 3 * hidden + j + TILE] = (dh * tc * go * (1.0 - go)).astype(BF)
            dc[:, cols] = e * gf
        if fused and SOON:
            tail.send_dz(t)
        if more_to_come:
            dr[...] = dot(padded(dz[here, :]), wrt[...])[:seqs]

    def backward_block(b):
        pl.when(first)(lambda: send_down(b).wait_recv())
        start, length = block_span(steps, b)
        for k in reversed(range(length)):
            cell_back(start + k, not (isinstance(b, int) and b == 0 and k == 0))
        if fused and not SOON:
            for k in range(length):
                tail.send_dz(start + k)
        here = rows_of(b)

        @pl.when(second)
        def _():
            dx[here, :] = dot(padded(dz[here, :]), wint[...])[: length * seqs].astype(BF)
            send_down(b).start()

    backward_block(blocks - 1)
    if fused:
        pl.when(first)(lambda: tail.hand_over_all())
    each_inner(lambda n: backward_block(blocks - 1 - n))
    backward_block(0)

    def write_hidden(perm):
        def write_u(cols, value):
            u[:, cols] = value

        reorder(seqs, steps, hs, seqs, perm, write_u)
        pltpu.make_async_copy(u, hid_out, store_sem.at[0]).start()

    def write_grads(perm):
        def write_dy(cols, value):
            dy[:, cols] = value

        @pl.when(first)
        def _():
            for j in range(0, hidden, TILE):
                dx[:, j : j + TILE] = dot(dz[...], wint[:, j : j + TILE]).astype(BF)

        reorder(seqs, steps, dx, 0, perm, write_dy)
        pltpu.make_async_copy(dy, dx_out, store_sem.at[1]).start()

    if fused:
        pl.when(second)(lambda: tail.build_own(eye))
        tail.run(eye, write_hidden, write_grads, out_a, out_b, out_c, store_sem)
    else:
        stores = [
            pltpu.make_async_copy(u, out_a, store_sem.at[2]),
            pltpu.make_async_copy(hs.at[pl.ds(0, total)], out_b, store_sem.at[3]),
            pltpu.make_async_copy(dz, out_c, store_sem.at[4]),
        ]
        for copy in stores:
            copy.start()
        for copy in stores:
            copy.wait()
        write_hidden(wrt.at[0:total, 0:total])
        write_grads(wrt.at[0:total, 0:total])
    pltpu.make_async_copy(u, hid_out, store_sem.at[0]).wait()
    pltpu.make_async_copy(dy, dx_out, store_sem.at[1]).wait()
    for b in range(blocks):
        pl.when(first)(lambda: send_up(b).wait_send())
        pl.when(second)(lambda: send_down(b).wait_send())


class Tail:
    def __init__(self, section, seqs, steps, u, hs, act, cs, dz, win, wrec, wrt,
                 u_a, h_a, u_z, h_z, dz_a, dz_z, bsum, brecv, ready,
                 f_sems, o_sems, dz_sems, p_sems, z_sems, all_sems, c_sems):
        self.s, self.seqs, self.steps, self.blocks = section, seqs, steps, block_count(steps)
        self.first, self.second = section == 0, section == 1
        self.hidden = wrec.shape[0]
        self.quarter = self.hidden
        self.u, self.hs, self.act, self.cs, self.dz = u, hs, act, cs, dz
        self.win, self.wrec, self.wrt = win, wrec, wrt
        self.u_a, self.h_a, self.u_z, self.h_z = u_a, h_a, u_z, h_z
        self.dz_theirs = (dz_a, dz_z)
        self.bsum, self.brecv, self.ready = bsum, brecv, ready
        self.f_sems, self.o_sems, self.dz_sems, self.p_sems = f_sems, o_sems, dz_sems, p_sems
        self.z_sems, self.all_sems, self.c_sems = z_sems, all_sems, c_sems
        j = lax.axis_index("dp")
        x, y, z = j % 2, (j // 2) % 2, j // 4
        s = section
        self.x, self.y, self.z = x, y, z
        self.ca = x * (1 - s) + y * s
        self.cb = y * (1 - s) + x * s
        self.zp, self.zin, self.kz = z % 2, z // 2, ((z + 1) // 2) % 2
        jx, jy = j + 1 - 2 * x, j + 2 - 4 * y
        self.to_a = {"dp": jx * (1 - s) + jy * s}
        self.to_b = {"dp": jy * (1 - s) + jx * s}
        self.to_mate = {"dp": j + 4 - 8 * self.zp}
        self.to_across = {"dp": j + 4 * (3 - 2 * z)}
        self.to_z = [{"dp": j - 4 * z + 4 * ((z + 3 - i) % 4)} for i in range(3)]
        self.partners = [{"dp": jx}, {"dp": jy}] + self.to_z
        self.rows = dz.shape[0]
        self.chunks = 2 * (self.quarter // CHUNK)
        self.unit = self.hidden // 16

    def remote(self, src, dst, send, recv, to):
        return pltpu.make_async_remote_copy(
            src_ref=src, dst_ref=dst, send_sem=send, recv_sem=recv, device_id=to, device_id_type=MESH
        )

    def clear(self):
        zeros = jnp.zeros((self.seqs, self.hidden), BF)
        self.h_a[0 : self.seqs, :] = zeros
        self.h_z[0 : self.seqs, :] = zeros


    def rows_of(self, b, shift=0):
        start, length = block_span(self.steps, b)
        return pl.ds(pl.multiple_of((start + shift) * self.seqs, self.seqs), length * self.seqs)

    def factor(self, i, b):
        at_u, at_h = self.rows_of(b), self.rows_of(b, 1)
        src, dst, at, to = (
            (self.u, self.u_a, at_u, self.to_a),
            (self.hs, self.h_a, at_h, self.to_a),
            (self.u, self.u_z, at_u, self.to_mate),
            (self.hs, self.h_z, at_h, self.to_mate),
        )[i]
        return self.remote(src.at[at], dst.at[at], self.f_sems.at[0, i, b], self.f_sems.at[1, i, b], to)

    def send_factors(self, b):
        if isinstance(b, int) and b == 0:

            @pl.when(self.first)
            def _():
                for n in range(self.blocks):
                    self.factor(0, n).start()
                    self.factor(2, n).start()

        pl.when(self.second)(lambda: self.factor(0, b).start())
        self.factor(1, b).start()
        self.factor(3, b).start()

    def hand_over(self, b):
        return self.remote(
            self.h_z.at[self.rows_of(b, 1)],
            self.u_z.at[self.rows_of(b)],
            self.o_sems.at[0, b],
            self.o_sems.at[1, b],
            {"section": 1 - self.s},
        )

    def hand_over_all(self):
        for b in range(self.blocks):
            self.factor(3, b).wait_recv()
            self.hand_over(b).start()

    def say_ready(self):
        for partner in self.partners:
            pl.semaphore_signal(self.ready, inc=1, device_id=partner, device_id_type=MESH)

    def wait_ready(self):
        pl.semaphore_wait(self.ready, len(self.partners))

    def dz_copy(self, i, t):
        at = pl.ds(pl.multiple_of(t * self.seqs, self.seqs), self.seqs)
        start = (1 - self.ca) * self.quarter if i == 0 else (3 - self.zp) * self.quarter
        cols = pl.ds(pl.multiple_of(start, self.quarter), self.quarter)
        return self.remote(
            self.dz.at[at, cols],
            self.dz_theirs[i].at[at],
            self.dz_sems.at[2 * i, t],
            self.dz_sems.at[2 * i + 1, t],
            (self.to_a, self.to_mate)[i],
        )

    def send_dz(self, t):
        for i in range(2):
            self.dz_copy(i, t).start()

    def place(self, part, j):
        x, y, z = j % 2, (j // 2) % 2, j // 4
        a = x * (1 - self.s) + y * self.s
        b = y * (1 - self.s) + x * self.s
        return b * 8 + z_place(z) * 2 + a if part == 0 else a * 8 + b * 4 + z

    def build(self, eye, source, g, spots):
        unit, rows = self.unit, self.rows
        for f in range(self.hidden // TILE):
            turned = dot_t(eye, source[0:rows, f * TILE : (f + 1) * TILE]).astype(BF)
            for i in range(TILE // unit):
                for part, half in spots:
                    row = self.place(part, f * (TILE // unit) + i) * unit
                    left = (part * 2 + g) * 2 * rows + half * rows
                    at = pl.ds(pl.multiple_of(row, unit), unit)
                    self.win[at, left : left + rows] = turned[i * unit : (i + 1) * unit, :]

    def build_own(self, eye):
        self.build(eye, self.u, 0, ((0, 0), (1, 0)))
        self.build(eye, self.hs, 1, ((0, 0), (1, 0)))


    def cols(self, c):
        return pl.ds(pl.multiple_of(c * CHUNK, CHUNK), CHUNK)

    def staged(self, c, row, size):
        wide = self.hidden // CHUNK
        return (
            pl.ds(pl.multiple_of((c // wide) * self.hidden + row, 64), size),
            pl.ds(pl.multiple_of((c % wide) * CHUNK, CHUNK), CHUNK),
        )

    def moved(self, c, row, size, sems, to):
        return self.remote(
            self.wrt.at[self.staged(c, row, size)], self.wrec.at[pl.ds(row, size), self.cols(c)], *sems, to
        )

    def p_along_b(self, c):
        return self.moved(c, 0, 512, (self.p_sems.at[0, c], self.p_sems.at[1, c]), self.to_b)

    def p_mate(self, c):
        return self.moved(c, 512, 256, (self.p_sems.at[2, c], self.p_sems.at[3, c]), self.to_mate)

    def p_across(self, c):
        return self.moved(c, 768, 128, (self.p_sems.at[4, c], self.p_sems.at[5, c]), self.to_across)

    def p_swap(self, c):
        return self.moved(c, 896, 64, (self.p_sems.at[6, c], self.p_sems.at[7, c]), self.to_a)

    def z_along_a(self, c):
        n = c - self.chunks
        return self.moved(c, 0, 512, (self.z_sems.at[0, n], self.z_sems.at[1, n]), self.to_a)

    def z_along_b(self, c):
        n = c - self.chunks
        return self.moved(c, 512, 256, (self.z_sems.at[2, n], self.z_sems.at[3, n]), self.to_b)

    def z_all(self, c, i):
        n = c - self.chunks
        sems = (self.all_sems.at[0, i, n], self.all_sems.at[1, i, n])
        return self.moved(c, 768 + 64 * i, 64, sems, self.to_z[i])

    def product(self, c, part, mine, half):
        rows = self.rows
        at = pl.ds(pl.multiple_of(half * 512, 512), 512)
        n = (c - part * self.chunks) // 2
        left = (part * 2 + c % 2) * 2 * rows
        own = self.dz[:, pl.ds(pl.multiple_of(mine * self.quarter + n * CHUNK, CHUNK), CHUNK)]
        theirs = self.dz_theirs[part][:, self.cols(n)]
        return dot(self.win[at, pl.ds(pl.multiple_of(left, rows), rows)], own) + dot(
            self.win[at, pl.ds(pl.multiple_of(left + rows, rows), rows)], theirs
        )

    def bias_plan(self, i):
        one = self.kz * 8
        two = one + self.zin * 4
        three = two + self.ca * 2
        return (
            ((1 - self.kz) * 8, one, 8, 0, self.to_mate),
            (one + (1 - self.zin) * 4, two, 4, 8, self.to_across),
            (two + (1 - self.ca) * 2, three, 2, 12, self.to_a),
            (three + 1 - self.cb, three + self.cb, 1, 14, self.to_b),
        )[i]

    def bias_copy(self, i):
        start, _, size, land, to = self.bias_plan(i)
        return self.remote(
            self.bsum.at[pl.ds(start, size)],
            self.brecv.at[pl.ds(land, size)],
            self.c_sems.at[0, i],
            self.c_sems.at[1, i],
            to,
        )

    def bias_start(self):
        ones = jnp.where(lax.broadcasted_iota(jnp.int32, (PAD, self.rows), 0) == 0, 1.0, 0.0).astype(BF)
        width = 4 * self.hidden // 16
        for j in range(16):
            x, y, z = j % 2, (j // 2) % 2, j // 4
            a = x * (1 - self.s) + y * self.s
            b = y * (1 - self.s) + x * self.s
            self.bsum[z_place(z) * 4 + a * 2 + b] = dot(ones, self.dz[:, j * width : (j + 1) * width])[0:8]
        self.bias_copy(0).start()

    def bias_step(self, i):
        self.bias_copy(i).wait_recv()
        _, start, size, land, _ = self.bias_plan(i)
        mine = pl.ds(start, size)
        self.bsum[mine] = self.bsum[mine] + self.brecv[land : land + size]
        if i < 3:
            self.bias_copy(i + 1).start()

    def put(self, q, c, value):
        n = (c % self.chunks) // 2
        rows = pl.ds(pl.multiple_of(((c % 2) * 4 + q) * self.unit, self.unit), self.unit)
        self.cs[rows, self.cols(n)] = value

    def run(self, eye, write_hidden, write_grads, out_in, out_rec, out_bias, store_sem):
        act, wrec, wrt = self.act, self.wrec, self.wrt
        chunks, blocks, steps = self.chunks, self.blocks, self.steps

        def loop(start, stop, body):
            def wrapped(c, carry):
                body(c)
                return carry

            lax.fori_loop(start, stop, wrapped, 0)

        def span(start, size):
            return pl.ds(pl.multiple_of(start, size), size)

        def arrive(i):
            for b in range(blocks):
                self.factor(i, b).wait_recv()

        def p_make(c):
            wrt[self.staged(c, 0, 512)] = self.product(c, 0, self.ca, 1 - self.cb).astype(BF)
            act[:, self.cols(c)] = self.product(c, 0, self.ca, self.cb)
            self.p_along_b(c).start()

        def z_make(c):
            wrt[self.staged(c, 0, 512)] = self.product(c, 1, 2 + self.zp, 1 - self.ca).astype(BF)
            act[:, self.cols(c)] = self.product(c, 1, 2 + self.zp, self.ca)
            self.z_along_a(c).start()

        def dz_arrived(i):
            def one(t):
                self.dz_copy(i, t).wait_recv()

            loop(0, steps, one)

        self.bias_start()
        arrive(0)
        arrive(1)
        self.build(eye, self.u_a, 0, ((0, 1),))
        self.build(eye, self.h_a, 1, ((0, 1),))
        dz_arrived(0)
        self.wait_ready()
        loop(0, AHEAD, p_make)

        @pl.when(self.first)
        def _():
            arrive(2)

        @pl.when(self.second)
        def _():
            arrive(3)
            for b in range(blocks):
                self.hand_over(b).wait_recv()

        self.build(eye, self.u_z, 0, ((1, 1),))
        self.build(eye, self.h_z, 1, ((1, 1),))
        dz_arrived(1)
        loop(chunks, chunks + AHEAD - LATER, z_make)

        def hidden_out():
            for b in range(blocks):
                for i in (0, 1, 3):
                    self.factor(i, b).wait_send()

            @pl.when(self.first)
            def _():
                for b in range(blocks):
                    self.factor(2, b).wait_send()
                    self.hand_over(b).wait_send()

            write_hidden(self.u_a.at[:, 0 : self.rows])

        extra = {
            1: lambda: self.bias_step(0),
            2: hidden_out,
            3: lambda: write_grads(self.u_a.at[:, 0 : self.rows]),
            4: lambda: self.bias_step(1),
            6: lambda: self.bias_step(2),
        }

        def add(kept_rows, landed, at):
            act[kept_rows, at] = act[kept_rows, at] + wrec[landed, at].astype(F32)

        def send_sum(c, row, size, from_rows, landed):
            at = self.cols(c)
            wrt[self.staged(c, row, size)] = (act[from_rows, at] + wrec[landed, at].astype(F32)).astype(BF)

        def p_after_b(c):
            self.p_along_b(c).wait_recv()
            theirs, mine = span((1 - self.kz) * 256, 256), span(self.kz * 256, 256)
            send_sum(c, 512, 256, theirs, theirs)
            self.p_mate(c).start()
            add(mine, mine, self.cols(c))

        def p_after_mate(c):
            self.p_mate(c).wait_recv()
            base = self.kz * 256
            theirs, mine = (1 - self.zin) * 128, self.zin * 128
            send_sum(c, 768, 128, span(base + theirs, 128), span(512 + theirs, 128))
            self.p_across(c).start()
            add(span(base + mine, 128), span(512 + mine, 128), self.cols(c))

        def p_after_across(c):
            self.p_across(c).wait_recv()
            at = self.cols(c)
            base = self.kz * 256 + self.zin * 128
            theirs, mine = (1 - self.ca) * 64, self.ca * 64
            send_sum(c, 896, 64, span(base + theirs, 64), span(768 + theirs, 64))
            self.p_swap(c).start()
            self.put(self.ca, c, act[span(base + mine, 64), at] + wrec[span(768 + mine, 64), at].astype(F32))

        def p_after_swap(c):
            self.p_swap(c).wait_recv()
            self.put(1 - self.ca, c, wrec[896:960, self.cols(c)].astype(F32))

        def z_after_a(c):
            self.z_along_a(c).wait_recv()
            theirs, mine = span((1 - self.cb) * 256, 256), span(self.cb * 256, 256)
            send_sum(c, 512, 256, theirs, theirs)
            self.z_along_b(c).start()
            add(mine, mine, self.cols(c))

        def z_after_b(c):
            self.z_along_b(c).wait_recv()
            base = self.cb * 256
            for i in range(3):
                block = ((self.z + 3 - i) % 4) * 64
                send_sum(c, 768 + 64 * i, 64, span(base + block, 64), span(512 + block, 64))
                self.z_all(c, i).start()
            block = self.z * 64
            add(span(base + block, 64), span(512 + block, 64), self.cols(c))

        def z_after_all(c):
            for i in range(3):
                self.z_all(c, i).wait_recv()
            at = self.cols(c)
            mine = span(self.cb * 256 + self.z * 64, 64)
            self.put(2 + self.zp, c, act[mine, at] + wrec[832:896, at].astype(F32))
            self.put(3 - self.zp, c, wrec[768:832, at].astype(F32) + wrec[896:960, at].astype(F32))

        p_stages = ((p_make, -AHEAD), (p_after_b, 0), (p_after_mate, 1), (p_after_across, 2), (p_after_swap, 3))
        z_stages = ((z_make, LATER - AHEAD), (z_after_a, LATER), (z_after_b, LATER + 1), (z_after_all, LATER + 2))

        def turn(n, carry):
            for work, lag in p_stages:
                pl.when((n >= lag) & (n < lag + chunks))(lambda: work(n - lag))
            for at, work in extra.items():
                pl.when(n == at)(work)
            for work, lag in z_stages:
                pl.when((n >= lag) & (n < lag + chunks))(lambda: work(chunks + n - lag))
            return carry

        lax.fori_loop(0, chunks + max(3, LATER + 2), turn, 0)
        self.bias_step(3)

        mine = self.bias_plan(3)[1]
        self.brecv[0, 0:1, :] = jnp.sum(self.bsum[mine], axis=0, keepdims=True)
        bias_store = pltpu.make_async_copy(self.brecv.at[0, pl.ds(0, 1)], out_bias, store_sem.at[2])
        bias_store.start()

        def result(n):
            g, q = n // 4, n % 4
            out = (out_in, out_rec)[g]
            rows = pl.ds(n * self.unit, self.unit)
            return pltpu.make_async_copy(
                self.cs.at[rows], out.at[:, pl.ds(q * self.quarter, self.quarter)], store_sem.at[3 + n]
            )

        for n in range(8):
            result(n).start()

        def dz_sent(t):
            for i in range(2):
                self.dz_copy(i, t).wait_send()

        loop(0, steps, dz_sent)
        for i in range(4):
            self.bias_copy(i).wait_send()

        def sent(c):
            for part in (self.p_along_b, self.p_mate, self.p_across, self.p_swap):
                part(c).wait_send()
            self.z_along_a(chunks + c).wait_send()
            self.z_along_b(chunks + c).wait_send()
            for i in range(3):
                self.z_all(chunks + c, i).wait_send()

        loop(0, chunks, sent)
        bias_store.wait()
        for n in range(8):
            result(n).wait()


def deliver_kernel(count, *refs):
    sources, targets, held, sems = refs[:count], refs[count : 2 * count], refs[2 * count : 3 * count], refs[3 * count]
    loads = [pltpu.make_async_copy(sources[i], held[i], sems.at[0, i]) for i in range(count)]
    stores = [pltpu.make_async_copy(held[i], targets[i], sems.at[1, i]) for i in range(count)]
    for copy in loads:
        copy.start()
    for load, store in zip(loads, stores):
        load.wait()
        store.start()
    for copy in stores:
        copy.wait()


def deliver(arrays):
    anywhere = [pl.BlockSpec(memory_space=pl.ANY)] * len(arrays)
    return pl.pallas_call(
        functools.partial(deliver_kernel, len(arrays)),
        out_shape=tuple(jax.ShapeDtypeStruct(a.shape, a.dtype) for a in arrays),
        in_specs=anywhere,
        out_specs=tuple(anywhere),
        scratch_shapes=[pltpu.VMEM(a.shape, a.dtype) for a in arrays] + [pltpu.SemaphoreType.DMA((2, len(arrays)))],
        compiler_params=pltpu.CompilerParams(vmem_limit_bytes=62 * 2**20),
        name="deliver",
    )(*arrays)


def on_device(inputs, lengths, w_in, w_rec, bias, cotangent):
    micro, per, steps, feats = inputs.shape
    hidden = w_rec.shape[1]
    seqs = micro * per
    total = steps * seqs
    vmem = pltpu.VMEM
    dma = pltpu.SemaphoreType.DMA
    blocks = block_count(steps)
    shards = lax.axis_size("dp")
    fused = shards == 16
    if fused:
        last_three = (
            jax.ShapeDtypeStruct((feats // shards, 4 * hidden), F32),
            jax.ShapeDtypeStruct((hidden // shards, 4 * hidden), F32),
            jax.ShapeDtypeStruct((1, 4 * hidden // shards), F32),
        )
        chunks = 2 * hidden // CHUNK
        more = [
            vmem((total, feats), BF),
            vmem((total + seqs, hidden), BF),
            vmem((total, feats), BF),
            vmem((total + seqs, hidden), BF),
            vmem((total, hidden), BF),
            vmem((total, hidden), BF),
            vmem((16, 8, 4 * hidden // 16), F32),
            vmem((15, 8, 4 * hidden // 16), F32),
            pltpu.SemaphoreType.REGULAR,
            dma((2, 4, blocks)),
            dma((2, blocks)),
            dma((4, steps)),
            dma((8, chunks)),
            dma((4, chunks)),
            dma((2, 3, chunks)),
            dma((2, 4)),
        ]
    else:
        last_three = (
            jax.ShapeDtypeStruct((total, feats), BF),
            jax.ShapeDtypeStruct((total, hidden), BF),
            jax.ShapeDtypeStruct((total, 4 * hidden), BF),
        )
        more = []
    anywhere = pl.BlockSpec(memory_space=pl.ANY)
    results = pl.pallas_call(
        functools.partial(lstm_kernel, steps, seqs, fused),
        out_shape=(
            jax.ShapeDtypeStruct((total, hidden), BF),
            jax.ShapeDtypeStruct((total, feats), BF),
            *last_three,
        ),
        in_specs=[anywhere, pl.BlockSpec(memory_space=pltpu.VMEM)] + [anywhere] * 4,
        out_specs=(anywhere,) * 5,
        scratch_shapes=[
            vmem((total, feats), BF),
            vmem((total + seqs, hidden), BF),
            vmem((total, hidden), BF),
            vmem((total, feats), BF),
            vmem((total, 4 * hidden), F32),
            vmem((total + seqs, hidden), F32),
            vmem((total, 4 * hidden), BF),
            vmem((feats, 4 * hidden), BF),
            vmem((hidden, 4 * hidden), BF),
            vmem((4 * hidden, hidden), BF),
            vmem((4 * hidden, feats), BF),
            vmem((seqs, hidden), F32),
            vmem((seqs, hidden), F32),
            vmem((seqs, 128), F32),
            vmem((1, 4 * hidden), F32),
            dma((4,)),
            dma((11,)),
            dma((blocks,)),
            dma((blocks,)),
            dma((blocks,)),
            dma((blocks,)),
            *more,
        ],
        compiler_params=pltpu.CompilerParams(
            collective_id=0, has_side_effects=True, vmem_limit_bytes=62 * 2**20
        ),
        name="lstm_both_ways",
    )(
        inputs.reshape(total, feats),
        lengths,
        w_in[0],
        w_rec[0],
        bias,
        cotangent.reshape(total, hidden),
    )
    if fused:
        hid, dx, share_in, share_rec, share_bias = deliver(results)
    else:
        hid, dx, u, hp, dz = results
        sum_in = lax.dot_general(u, dz, (((0,), (0,)), ((), ())), preferred_element_type=F32)
        sum_rec = lax.dot_general(hp, dz, (((0,), (0,)), ((), ())), preferred_element_type=F32)
        sum_bias = jnp.sum(dz, axis=0, dtype=F32)
        share_in = lax.psum_scatter(sum_in, "dp", scatter_dimension=0, tiled=True)
        share_rec = lax.psum_scatter(sum_rec, "dp", scatter_dimension=0, tiled=True)
        share_bias = lax.psum_scatter(sum_bias, "dp", scatter_dimension=0, tiled=True)[None]
    shape = inputs.shape
    return (
        hid.reshape(shape)[None],
        dx.reshape(shape)[None],
        share_in[None],
        share_rec[None],
        share_bias,
    )


def solution(mesh):
    placed = (
        P(None, "dp", None, None),
        P(None, "dp"),
        P("section", None, None),
        P("section", None, None),
        P("section", None),
        P(None, "dp", None, None),
    )
    return jax.shard_map(
        on_device,
        mesh=mesh,
        in_specs=placed,
        out_specs=(
            P("section", None, "dp", None, None),
            P("section", None, "dp", None, None),
            P("section", "dp", None),
            P("section", "dp", None),
            P("section", "dp"),
        ),
        check_vma=False,
    )
```

```python
import functools

import jax
import jax.numpy as jnp
from jax import lax
from jax.experimental import pallas as pl
from jax.experimental.pallas import tpu as pltpu
from jax.sharding import PartitionSpec as P

BF = jnp.bfloat16
F32 = jnp.float32
MESH = pl.DeviceIdType.MESH
BLOCK = 4
EDGE = 2
PAD = 128
TILE = 256
CHUNK = 128
WIDE = 256
SOON = True
P_AHEAD = 3
Z_AHEAD = 3
HAND_AFTER = 2
P_LAGS = (2, 4)
Z_LAGS = (2, 4)


def sigmoid(v):
    return 0.5 * jnp.tanh(0.5 * v) + 0.5


def rows_at(start, size):
    return pl.ds(pl.multiple_of(start, size), size)


def dot(a, b):
    return jnp.dot(a, b, preferred_element_type=F32)


def dot_t(a, b):
    return lax.dot_general(a, b, (((1,), (1,)), ((), ())), preferred_element_type=F32)


def padded(rows):
    lack = PAD - rows.shape[0]
    return jnp.concatenate([rows, jnp.zeros((lack, rows.shape[1]), rows.dtype)], axis=0) if lack > 0 else rows


def block_count(steps):
    return 2 + (steps - 2 * EDGE) // BLOCK


def block_span(steps, b):
    if isinstance(b, int):
        if b == 0:
            return 0, EDGE
        if b == block_count(steps) - 1:
            return steps - EDGE, EDGE
    return EDGE + (b - 1) * BLOCK, BLOCK


def z_place(z):
    return 2 * (((z + 1) // 2) % 2) + z // 2


def lstm_kernel(
    steps, seqs, fused,
    x_ref, len_ref, win_ref, wrec_ref, bias_ref, ct_ref,
    hid_out, dx_out, out_a, out_b, out_c,
    u, hs, dy, dx, act, cs, dz, win, wrec, wrt, wint, dr, dc, lens, bias,
    load_sem, store_sem, up_send, up_recv, down_send, down_recv, *more,
):
    hidden = wrec.shape[0]
    gates = 4 * hidden
    total = steps * seqs
    blocks = block_count(steps)
    section = lax.axis_index("section")
    first = section == 0
    second = section == 1
    other = {"section": 1 - section}

    tail = Tail(section, seqs, steps, u, hs, act, cs, dz, win, wrec, wrt, *more) if fused else None

    barrier = pltpu.get_barrier_semaphore()
    pl.semaphore_signal(barrier, inc=1, device_id=other, device_id_type=MESH)
    if fused:
        for partner in tail.partners:
            pl.semaphore_signal(barrier, inc=1, device_id=partner, device_id_type=MESH)

    load_x = pltpu.make_async_copy(x_ref, dx, load_sem.at[0])
    load_ct = pltpu.make_async_copy(ct_ref, dx, load_sem.at[0])
    load_wrec = pltpu.make_async_copy(wrec_ref, wrec, load_sem.at[1])

    def load_win(g):
        part = pl.ds(g * hidden, hidden)
        return pltpu.make_async_copy(win_ref.at[:, part], win.at[:, part], load_sem.at[2 + g])

    load_bias = pltpu.make_async_copy(bias_ref, bias, load_sem.at[6])
    pl.when(first)(lambda: load_x.start())
    pl.when(second)(lambda: load_ct.start())
    load_bias.start()
    for g in range(4):
        load_win(g).start()
    load_wrec.start()

    micro, per = len_ref.shape
    row_id = lax.broadcasted_iota(jnp.int32, (per, per), 0)
    col_id = lax.broadcasted_iota(jnp.int32, (per, per), 1)
    for m in range(micro):
        row = jnp.broadcast_to(len_ref[m : m + 1, :].astype(F32), (per, per))
        column = jnp.sum(jnp.where(row_id == col_id, row, 0.0), axis=1, keepdims=True)
        lens[m * per : (m + 1) * per, :] = jnp.broadcast_to(column, (per, lens.shape[1]))

    hs[0:seqs, :] = jnp.zeros((seqs, hidden), BF)
    cs[0:seqs, :] = jnp.zeros((seqs, hidden), F32)
    dr[...] = jnp.zeros_like(dr)
    dc[...] = jnp.zeros_like(dc)
    if fused:
        tail.clear()

    def order(outer, inner, perm):
        to_id = lax.broadcasted_iota(jnp.int32, (inner, total), 0)
        from_id = lax.broadcasted_iota(jnp.int32, (inner, total), 1)
        for n in range(outer):
            perm[n * inner : (n + 1) * inner, :] = jnp.where(to_id * outer + n == from_id, 1.0, 0.0).astype(BF)

    def reorder(perm, source, skip, columns, write):
        for j in columns:
            cols = slice(j, j + TILE)
            write(cols, dot(perm[...], source[skip : skip + total, cols]).astype(BF))

    def write_first(cols, value):
        @pl.when(first)
        def _():
            u[:, cols] = value

        @pl.when(second)
        def _():
            dy[:, cols] = value

    load_x.wait()
    order(steps, seqs, wrt.at[0:total, 0:total])
    reorder(wrt.at[0:total, 0:total], dx, 0, range(0, hidden, TILE), write_first)

    load_bias.wait()

    eye = jnp.where(
        lax.broadcasted_iota(jnp.int32, (TILE, TILE), 0) == lax.broadcasted_iota(jnp.int32, (TILE, TILE), 1), 1.0, 0.0
    ).astype(BF)

    def turn_over(source, target):
        def piece(i, carry):
            at = rows_at(i * TILE, TILE)
            target[at, :] = dot_t(eye, source[:, at]).astype(BF)
            return carry

        lax.fori_loop(0, gates // TILE, piece, 0)

    @pl.when(second)
    def _():
        for g in range(4):
            load_win(g).wait()
        turn_over(win, wint)
        load_wrec.wait()
        turn_over(wrec, wrt)

    def arrived():
        pl.semaphore_wait(barrier, 1 + len(tail.partners) if fused else 1)

    def rows_of(b, shift=0):
        start, length = block_span(steps, b)
        return pl.ds(pl.multiple_of((start + shift) * seqs, seqs), length * seqs)

    def send_up(b):
        return pltpu.make_async_remote_copy(
            src_ref=hs.at[rows_of(b, 1)],
            dst_ref=u.at[rows_of(b)],
            send_sem=up_send.at[b],
            recv_sem=up_recv.at[b],
            device_id=other,
            device_id_type=MESH,
        )

    def send_down(b):
        return pltpu.make_async_remote_copy(
            src_ref=dx.at[rows_of(b)],
            dst_ref=dy.at[rows_of(b)],
            send_sem=down_send.at[b],
            recv_sem=down_recv.at[b],
            device_id=other,
            device_id_type=MESH,
        )

    def cell(t, recur):
        here = rows_at(t * seqs, seqs)
        after = rows_at((t + 1) * seqs, seqs)
        h_prev = padded(hs[here, :]) if recur else None
        mask = jnp.where(jnp.float32(t) < lens[:, 0:1], 1.0, 0.0)
        for j in range(0, hidden, TILE):
            z = []
            for g in range(4):
                cols = slice(g * hidden + j, g * hidden + j + TILE)
                z.append(act[here, cols] + dot(h_prev, wrec[:, cols])[:seqs] if recur else act[here, cols])
            gi, gf, gg, go = sigmoid(z[0]), sigmoid(z[1]), jnp.tanh(z[2]), sigmoid(z[3])
            c_new = gf * cs[here, j : j + TILE] + gi * gg if recur else gi * gg
            cs[after, j : j + TILE] = c_new
            act[here, j : j + TILE] = gi
            act[here, hidden + j : hidden + j + TILE] = gf
            act[here, 2 * hidden + j : 2 * hidden + j + TILE] = gg
            act[here, 3 * hidden + j : 3 * hidden + j + TILE] = go
            hs[after, j : j + TILE] = (go * jnp.tanh(c_new) * mask).astype(BF)

    def forward_block(b):
        pl.when(second)(lambda: send_up(b).wait_recv())
        start, length = block_span(steps, b)
        here = rows_of(b)
        given = u[here, :]
        given = padded(given)
        for j in range(0, gates, TILE):
            if isinstance(b, int) and b == 0 and j % hidden == 0:
                pl.when(first)(lambda: load_win(j // hidden).wait())
            act[here, j : j + TILE] = dot(given, win[:, j : j + TILE])[: length * seqs] + bias[:, j : j + TILE]
        for k in range(length):
            at_zero = isinstance(b, int) and b == 0 and k == 0
            cell(start + k, not at_zero)
            if at_zero:
                pl.when(first)(lambda: load_wrec.wait())
        if isinstance(b, int) and b == 0:
            arrived()
        pl.when(first)(lambda: send_up(b).start())
        if fused:
            tail.send_factors(b)

    def each_inner(body):
        def wrapped(b, carry):
            body(b)
            return carry

        lax.fori_loop(1, blocks - 1, wrapped, 0)

    forward_block(0)
    each_inner(forward_block)
    forward_block(blocks - 1)

    @pl.when(first)
    def _():
        turn_over(wrec, wrt)
        turn_over(win, wint)

    if fused:
        @pl.when(first)
        def _():
            tail.build_own(eye)
            tail.build_a(eye)

        tail.say_ready()

    def cell_back(t, more_to_come):
        here = rows_at(t * seqs, seqs)
        after = rows_at((t + 1) * seqs, seqs)
        mask = jnp.where(jnp.float32(t) < lens[:, 0:1], 1.0, 0.0)
        for j in range(0, hidden, TILE):
            cols = slice(j, j + TILE)
            dh = dy[here, cols].astype(F32) * mask + dr[:, cols]
            gi = act[here, j : j + TILE]
            gf = act[here, hidden + j : hidden + j + TILE]
            gg = act[here, 2 * hidden + j : 2 * hidden + j + TILE]
            go = act[here, 3 * hidden + j : 3 * hidden + j + TILE]
            tc = jnp.tanh(cs[after, cols])
            e = dc[:, cols] + dh * go * (1.0 - tc * tc)
            dz[here, j : j + TILE] = (e * gg * gi * (1.0 - gi)).astype(BF)
            dz[here, hidden + j : hidden + j + TILE] = (e * cs[here, cols] * gf * (1.0 - gf)).astype(BF)
            dz[here, 2 * hidden + j : 2 * hidden + j + TILE] = (e * gi * (1.0 - gg * gg)).astype(BF)
            dz[here, 3 * hidden + j : 3 * hidden + j + TILE] = (dh * tc * go * (1.0 - go)).astype(BF)
            dc[:, cols] = e * gf
        if fused and SOON:
            tail.send_dz(t)
        if more_to_come:
            dr[...] = dot(padded(dz[here, :]), wrt[...])[:seqs]

    def backward_block(b):
        pl.when(first)(lambda: send_down(b).wait_recv())
        start, length = block_span(steps, b)
        for k in reversed(range(length)):
            cell_back(start + k, not (isinstance(b, int) and b == 0 and k == 0))
        if fused and not SOON:
            for k in range(length):
                tail.send_dz(start + k)
        here = rows_of(b)

        @pl.when(second)
        def _():
            dx[here, :] = dot(padded(dz[here, :]), wint[...])[: length * seqs].astype(BF)
            send_down(b).start()

    def backward_inner(n):
        backward_block(blocks - 1 - n)
        if fused:
            pl.when(first & (n == HAND_AFTER))(lambda: tail.take_from_mate())

    backward_block(blocks - 1)
    each_inner(backward_inner)
    backward_block(0)

    def write_u(cols, value):
        u[:, cols] = value

    def write_dy(cols, value):
        dy[:, cols] = value

    def write_pieces(perm):
        middle = hidden // 2
        left, right = range(0, middle, TILE), range(middle, hidden, TILE)

        def hidden_left():
            order(seqs, steps, perm)
            reorder(perm, hs, seqs, left, write_u)

        def hidden_right():
            reorder(perm, hs, seqs, right, write_u)
            pltpu.make_async_copy(u, hid_out, store_sem.at[0]).start()

        def late_dx(columns):
            @pl.when(first)
            def _():
                for j in columns:
                    dx[:, j : j + TILE] = dot(dz[...], wint[:, j : j + TILE]).astype(BF)

        def grads_right():
            reorder(perm, dx, 0, right, write_dy)
            pltpu.make_async_copy(dy, dx_out, store_sem.at[1]).start()

        return (
            hidden_left, hidden_right, lambda: late_dx(left), lambda: late_dx(right),
            lambda: reorder(perm, dx, 0, left, write_dy), grads_right,
        )

    if fused:
        @pl.when(second)
        def _():
            tail.build_own(eye)
            tail.build_a(eye)

        tail.run(eye, write_pieces, out_a, out_b, out_c, store_sem)
    else:
        stores = [
            pltpu.make_async_copy(u, out_a, store_sem.at[2]),
            pltpu.make_async_copy(hs.at[pl.ds(0, total)], out_b, store_sem.at[3]),
            pltpu.make_async_copy(dz, out_c, store_sem.at[4]),
        ]
        for copy in stores:
            copy.start()
        for copy in stores:
            copy.wait()
        for piece in write_pieces(wrt.at[0:total, 0:total]):
            piece()
    pltpu.make_async_copy(u, hid_out, store_sem.at[0]).wait()
    pltpu.make_async_copy(dy, dx_out, store_sem.at[1]).wait()
    for b in range(blocks):
        pl.when(first)(lambda: send_up(b).wait_send())
        pl.when(second)(lambda: send_down(b).wait_send())


class Tail:
    def __init__(self, section, seqs, steps, u, hs, act, cs, dz, win, wrec, wrt,
                 u_a, h_a, u_z, h_z, dz_a, dz_z, bsum, brecv, ready,
                 f_sems, o_sems, dz_sems, p_sems, z_sems, c_sems):
        self.s, self.seqs, self.steps, self.blocks = section, seqs, steps, block_count(steps)
        self.first, self.second = section == 0, section == 1
        self.hidden = wrec.shape[0]
        self.quarter = self.hidden
        self.u, self.hs, self.act, self.cs, self.dz = u, hs, act, cs, dz
        self.win, self.wrec, self.wrt = win, wrec, wrt
        self.u_a, self.h_a, self.u_z, self.h_z = u_a, h_a, u_z, h_z
        self.dz_theirs = (dz_a, dz_z)
        self.bsum, self.brecv, self.ready = bsum, brecv, ready
        self.f_sems, self.o_sems, self.dz_sems, self.p_sems = f_sems, o_sems, dz_sems, p_sems
        self.z_sems, self.c_sems = z_sems, c_sems
        j = lax.axis_index("dp")
        x, y, z = j % 2, (j // 2) % 2, j // 4
        s = section
        self.x, self.y, self.z = x, y, z
        self.ca = x * (1 - s) + y * s
        self.cb = y * (1 - s) + x * s
        self.zp, self.zin, self.kz = z % 2, z // 2, ((z + 1) // 2) % 2
        jx, jy = j + 1 - 2 * x, j + 2 - 4 * y
        self.to_a = {"dp": jx * (1 - s) + jy * s}
        self.to_b = {"dp": jy * (1 - s) + jx * s}
        self.to_mate = {"dp": j + 4 - 8 * self.zp}
        self.to_across = {"dp": j + 4 * (3 - 2 * z)}
        self.to_z = [{"dp": j - 4 * z + 4 * ((z + 3 - i) % 4)} for i in range(3)]
        self.partners = [{"dp": jx}, {"dp": jy}] + self.to_z
        self.rows = dz.shape[0]
        self.chunks = 2 * (self.quarter // CHUNK)
        self.unit = self.hidden // 16

    def remote(self, src, dst, send, recv, to):
        return pltpu.make_async_remote_copy(
            src_ref=src, dst_ref=dst, send_sem=send, recv_sem=recv, device_id=to, device_id_type=MESH
        )

    def clear(self):
        zeros = jnp.zeros((self.seqs, self.hidden), BF)
        self.h_a[0 : self.seqs, :] = zeros
        self.h_z[0 : self.seqs, :] = zeros


    def rows_of(self, b, shift=0):
        start, length = block_span(self.steps, b)
        return pl.ds(pl.multiple_of((start + shift) * self.seqs, self.seqs), length * self.seqs)

    def factor(self, i, b):
        at_u, at_h = self.rows_of(b), self.rows_of(b, 1)
        src, dst, at, to = (
            (self.u, self.u_a, at_u, self.to_a),
            (self.hs, self.h_a, at_h, self.to_a),
            (self.u, self.u_z, at_u, self.to_mate),
            (self.hs, self.h_z, at_h, self.to_mate),
        )[i]
        return self.remote(src.at[at], dst.at[at], self.f_sems.at[0, i, b], self.f_sems.at[1, i, b], to)

    def send_factors(self, b):
        if isinstance(b, int) and b == 0:

            @pl.when(self.first)
            def _():
                for n in range(self.blocks):
                    self.factor(0, n).start()
                    self.factor(2, n).start()

        pl.when(self.second)(lambda: self.factor(0, b).start())
        self.factor(1, b).start()
        self.factor(3, b).start()

    def hand_over(self, b):
        return self.remote(
            self.h_z.at[self.rows_of(b, 1)],
            self.u_z.at[self.rows_of(b)],
            self.o_sems.at[0, b],
            self.o_sems.at[1, b],
            {"section": 1 - self.s},
        )

    def build_z(self, eye):
        self.build(eye, self.u_z, 0, 2)
        self.build(eye, self.h_z, 1, 2)

    def take_from_mate(self):
        for b in range(self.blocks):
            self.factor(3, b).wait_recv()
            self.hand_over(b).start()
    def say_ready(self):
        for partner in self.partners:
            pl.semaphore_signal(self.ready, inc=1, device_id=partner, device_id_type=MESH)

    def wait_ready(self):
        pl.semaphore_wait(self.ready, len(self.partners))

    def dz_copy(self, i, t):
        at = pl.ds(pl.multiple_of(t * self.seqs, self.seqs), self.seqs)
        cols = pl.ds(0, 2 * self.quarter)
        if i == 1:
            cols = pl.ds(pl.multiple_of((3 - self.zp) * self.quarter, self.quarter), self.quarter)
        return self.remote(
            self.dz.at[at, cols],
            self.dz_theirs[i].at[at],
            self.dz_sems.at[2 * i, t],
            self.dz_sems.at[2 * i + 1, t],
            (self.to_a, self.to_mate)[i],
        )

    def send_dz(self, t):
        for i in range(2):
            self.dz_copy(i, t).start()

    def place(self, j):
        x, y, z = j % 2, (j // 2) % 2, j // 4
        a = x * (1 - self.s) + y * self.s
        b = y * (1 - self.s) + x * self.s
        return a * 8 + b * 4 + z_place(z)

    def build(self, eye, source, g, origin):
        unit, rows = self.unit, self.rows
        left = (g * 3 + origin) * rows
        for f in range(self.hidden // TILE):
            turned = dot_t(eye, source[0:rows, f * TILE : (f + 1) * TILE]).astype(BF)
            for i in range(TILE // unit):
                row = self.place(f * (TILE // unit) + i) * unit
                at = pl.ds(pl.multiple_of(row, unit), unit)
                self.win[at, left : left + rows] = turned[i * unit : (i + 1) * unit, :]

    def build_own(self, eye):
        self.build(eye, self.u, 0, 0)
        self.build(eye, self.hs, 1, 0)

    def build_a(self, eye):
        for b in range(self.blocks):
            self.factor(0, b).wait_recv()
            self.factor(1, b).wait_recv()
        self.build(eye, self.u_a, 0, 1)
        self.build(eye, self.h_a, 1, 1)


    def p_out(self, c, row, size):
        return (
            pl.ds(pl.multiple_of((c // (self.hidden // WIDE)) * 512 + row, 64), size),
            pl.ds(pl.multiple_of((c % (self.hidden // WIDE)) * WIDE, WIDE), WIDE),
        )

    def p_in(self, c, row, size):
        return (
            pl.ds(pl.multiple_of((c // (2 * self.hidden // WIDE)) * 512 + row, 64), size),
            pl.ds(pl.multiple_of((c % (2 * self.hidden // WIDE)) * WIDE, WIDE), WIDE),
        )

    def p_kept(self, c, row, size):
        return (
            pl.ds(pl.multiple_of((c // (2 * self.hidden // WIDE)) * 256 + row, 64), size),
            pl.ds(pl.multiple_of((c % (2 * self.hidden // WIDE)) * WIDE, WIDE), WIDE),
        )

    def z_out(self, c, row, size):
        wide = self.hidden // CHUNK
        return (
            pl.ds(pl.multiple_of(2 * self.hidden + (c // wide) * self.hidden + row, 64), size),
            pl.ds(pl.multiple_of((c % wide) * CHUNK, CHUNK), CHUNK),
        )

    def z_in(self, c, row, size):
        return (
            pl.ds(pl.multiple_of(row, 64), size),
            pl.ds(pl.multiple_of(2 * self.hidden + c * CHUNK, CHUNK), CHUNK),
        )

    def p_moved(self, c, i, row, size, to):
        return self.remote(
            self.wrt.at[self.p_out(c, row, size)], self.wrec.at[self.p_in(c, row, size)],
            self.p_sems.at[2 * i, c], self.p_sems.at[2 * i + 1, c], to,
        )

    def z_moved(self, c, i, row, size, to):
        return self.remote(
            self.wrt.at[self.z_out(c, row, size)], self.wrec.at[self.z_in(c, row, size)],
            self.z_sems.at[2 * i, c], self.z_sems.at[2 * i + 1, c], to,
        )

    def p_along_b(self, c):
        return self.p_moved(c, 0, 0, 256, self.to_b)

    def p_mate(self, c):
        return self.p_moved(c, 1, 256, 128, self.to_mate)

    def p_across(self, c):
        return self.p_moved(c, 2, 384, 64, self.to_across)

    def z_along_a(self, c):
        return self.z_moved(c, 0, 0, 512, self.to_a)

    def z_along_b(self, c):
        return self.z_moved(c, 1, 512, 256, self.to_b)

    def z_all(self, c, i):
        return self.z_moved(c, 2 + i, 768 + 64 * i, 64, self.to_z[i])

    def product(self, c, row, size, origin, own, theirs):
        rows = self.rows
        at = pl.ds(pl.multiple_of(row, size), size)
        left = (c % 2) * 3 * rows
        one = dot(self.win[at, pl.ds(pl.multiple_of(left, rows), rows)], own)
        two = dot(self.win[at, pl.ds(pl.multiple_of(left + origin * rows, rows), rows)], theirs)
        return one + two

    def p_make(self, c):
        at = pl.ds(pl.multiple_of((c // 2) * WIDE, WIDE), WIDE)
        own, theirs = self.dz[:, at], self.dz_theirs[0][:, at]
        base = self.ca * 512
        self.wrt[self.p_out(c, 0, 256)] = self.product(c, base + (1 - self.cb) * 256, 256, 1, own, theirs).astype(BF)
        self.act[self.p_kept(c, 0, 256)] = self.product(c, base + self.cb * 256, 256, 1, own, theirs)
        self.p_along_b(c).start()

    def z_make(self, c):
        own = self.dz[:, pl.ds(pl.multiple_of((2 + self.zp) * self.quarter + (c // 2) * CHUNK, CHUNK), CHUNK)]
        theirs = self.dz_theirs[1][:, pl.ds(pl.multiple_of((c // 2) * CHUNK, CHUNK), CHUNK)]
        self.wrt[self.z_out(c, 0, 512)] = self.product(c, (1 - self.ca) * 512, 512, 2, own, theirs).astype(BF)
        self.act[self.z_in(c, 0, 512)] = self.product(c, self.ca * 512, 512, 2, own, theirs)
        self.z_along_a(c).start()

    def bias_plan(self, i):
        one = self.kz * 8
        two = one + self.zin * 4
        three = two + self.ca * 2
        return (
            ((1 - self.kz) * 8, one, 8, 0, self.to_mate),
            (one + (1 - self.zin) * 4, two, 4, 8, self.to_across),
            (two + (1 - self.ca) * 2, three, 2, 12, self.to_a),
            (three + 1 - self.cb, three + self.cb, 1, 14, self.to_b),
        )[i]

    def bias_copy(self, i):
        start, _, size, land, to = self.bias_plan(i)
        return self.remote(
            self.bsum.at[pl.ds(start, size)],
            self.brecv.at[pl.ds(land, size)],
            self.c_sems.at[0, i],
            self.c_sems.at[1, i],
            to,
        )

    def bias_start(self):
        ones = jnp.where(lax.broadcasted_iota(jnp.int32, (PAD, self.rows), 0) == 0, 1.0, 0.0).astype(BF)
        width = 4 * self.hidden // 16
        for j in range(16):
            x, y, z = j % 2, (j // 2) % 2, j // 4
            a = x * (1 - self.s) + y * self.s
            b = y * (1 - self.s) + x * self.s
            self.bsum[z_place(z) * 4 + a * 2 + b] = dot(ones, self.dz[:, j * width : (j + 1) * width])[0:8]
        self.bias_copy(0).start()

    def bias_step(self, i):
        self.bias_copy(i).wait_recv()
        _, start, size, land, _ = self.bias_plan(i)
        mine = pl.ds(start, size)
        self.bsum[mine] = self.bsum[mine] + self.brecv[land : land + size]
        if i < 3:
            self.bias_copy(i + 1).start()

    def put(self, c, column, value):
        quarter, width = self.quarter, value.shape[1]
        rows = pl.ds(pl.multiple_of(((c % 2) * 4 + column // quarter) * self.unit, self.unit), self.unit)
        self.cs[rows, pl.ds(pl.multiple_of(column % quarter, width), width)] = value

    def run(self, eye, write_pieces, out_in, out_rec, out_bias, store_sem):
        act, wrec, wrt = self.act, self.wrec, self.wrt
        chunks, blocks, steps = self.chunks, self.blocks, self.steps

        def loop(start, stop, body):
            def wrapped(c, carry):
                body(c)
                return carry

            lax.fori_loop(start, stop, wrapped, 0)

        def span(start, size):
            return pl.ds(pl.multiple_of(start, size), size)

        def dz_arrived(i):
            def one(t):
                self.dz_copy(i, t).wait_recv()

            loop(0, steps, one)

        dz_arrived(0)
        self.wait_ready()
        loop(0, P_AHEAD, self.p_make)

        @pl.when(self.first)
        def _():
            for b in range(blocks):
                self.factor(2, b).wait_recv()

        @pl.when(self.second)
        def _():
            for b in range(blocks):
                self.factor(3, b).wait_recv()
                self.hand_over(b).wait_recv()

        self.build_z(eye)
        dz_arrived(1)
        loop(0, Z_AHEAD, self.z_make)

        pieces = write_pieces(self.u_a.at[:, 0 : self.rows])

        def first_piece():
            for b in range(blocks):
                for i in (0, 1, 3):
                    self.factor(i, b).wait_send()

            @pl.when(self.first)
            def _():
                for b in range(blocks):
                    self.factor(2, b).wait_send()
                    self.hand_over(b).wait_send()

            pieces[0]()

        extra = (
            (1, self.bias_start), (2, first_piece), (4, pieces[1]), (5, lambda: self.bias_step(0)), (6, pieces[2]),
            (8, pieces[3]), (9, lambda: self.bias_step(1)), (10, pieces[4]), (12, pieces[5]), (13, lambda: self.bias_step(2)),
        )

        def total(kept, landed):
            return act[kept] + wrec[landed].astype(F32)

        def p_after_b(c):
            self.p_along_b(c).wait_recv()
            theirs, mine = (1 - self.kz) * 128, self.kz * 128
            wrt[self.p_out(c, 256, 128)] = total(self.p_kept(c, theirs, 128), self.p_in(c, theirs, 128)).astype(BF)
            self.p_mate(c).start()
            kept = self.p_kept(c, mine, 128)
            act[kept] = total(kept, self.p_in(c, mine, 128))

        def p_after_mate(c):
            self.p_mate(c).wait_recv()
            base = self.kz * 128
            theirs, mine = (1 - self.zin) * 64, self.zin * 64
            wrt[self.p_out(c, 384, 64)] = total(
                self.p_kept(c, base + theirs, 64), self.p_in(c, 256 + theirs, 64)
            ).astype(BF)
            self.p_across(c).start()
            kept = self.p_kept(c, base + mine, 64)
            act[kept] = total(kept, self.p_in(c, 256 + mine, 64))

        def p_after_across(c):
            self.p_across(c).wait_recv()
            kept = self.p_kept(c, self.kz * 128 + self.zin * 64, 64)
            self.put(c, (c // 2) * WIDE, total(kept, self.p_in(c, 384, 64)))

        def z_after_a(c):
            self.z_along_a(c).wait_recv()
            theirs, mine = (1 - self.cb) * 256, self.cb * 256
            wrt[self.z_out(c, 512, 256)] = total(self.z_in(c, theirs, 256), self.z_in(c, theirs, 256)).astype(BF)
            self.z_along_b(c).start()
            kept = self.z_in(c, mine, 256)
            act[kept] = total(kept, kept)

        def z_after_b(c):
            self.z_along_b(c).wait_recv()
            base = self.cb * 256
            for i in range(3):
                row = z_place((self.z + 3 - i) % 4) * 64
                wrt[self.z_out(c, 768 + 64 * i, 64)] = total(
                    self.z_in(c, base + row, 64), self.z_in(c, 512 + row, 64)
                ).astype(BF)
                self.z_all(c, i).start()
            row = z_place(self.z) * 64
            kept = self.z_in(c, base + row, 64)
            act[kept] = total(kept, self.z_in(c, 512 + row, 64))

        def z_after_all(c):
            for i in range(3):
                self.z_all(c, i).wait_recv()
            column = 2 * self.quarter + (c // 2) * CHUNK
            kept = self.z_in(c, self.cb * 256 + z_place(self.z) * 64, 64)
            self.put(c, column + self.zp * self.quarter, total(kept, self.z_in(c, 832, 64)))
            opposite = wrec[self.z_in(c, 768, 64)].astype(F32) + wrec[self.z_in(c, 896, 64)].astype(F32)
            self.put(c, column + (1 - self.zp) * self.quarter, opposite)

        stages = (
            (p_after_b, 0), (z_after_a, 0), (self.p_make, -P_AHEAD), (self.z_make, -Z_AHEAD),
            (p_after_mate, P_LAGS[0]), (z_after_b, Z_LAGS[0]),
            (p_after_across, P_LAGS[1]), (z_after_all, Z_LAGS[1]),
        )

        def turn(n, carry):
            for work, lag in stages:
                c = n - lag
                pl.when((c >= 0) & (c < chunks))(lambda: work(c))
            for at, work in extra:
                pl.when(n == at)(work)
            return carry

        lax.fori_loop(0, chunks + max(P_LAGS[1], Z_LAGS[1]), turn, 0)
        self.bias_step(3)

        mine = self.bias_plan(3)[1]
        self.brecv[0, 0:1, :] = jnp.sum(self.bsum[mine], axis=0, keepdims=True)
        bias_store = pltpu.make_async_copy(self.brecv.at[0, pl.ds(0, 1)], out_bias, store_sem.at[2])
        bias_store.start()

        def result(n):
            g, q = n // 4, n % 4
            out = (out_in, out_rec)[g]
            rows = pl.ds(n * self.unit, self.unit)
            return pltpu.make_async_copy(
                self.cs.at[rows], out.at[:, pl.ds(q * self.quarter, self.quarter)], store_sem.at[3 + n]
            )

        for n in range(8):
            result(n).start()

        def dz_sent(t):
            for i in range(2):
                self.dz_copy(i, t).wait_send()

        loop(0, steps, dz_sent)
        for i in range(4):
            self.bias_copy(i).wait_send()

        def sent(c):
            for part in (self.p_along_b, self.p_mate, self.p_across, self.z_along_a, self.z_along_b):
                part(c).wait_send()
            for i in range(3):
                self.z_all(c, i).wait_send()

        loop(0, chunks, sent)
        bias_store.wait()
        for n in range(8):
            result(n).wait()


def deliver_kernel(count, *refs):
    sources, targets, held, sems = refs[:count], refs[count : 2 * count], refs[2 * count : 3 * count], refs[3 * count]
    loads = [pltpu.make_async_copy(sources[i], held[i], sems.at[0, i]) for i in range(count)]
    stores = [pltpu.make_async_copy(held[i], targets[i], sems.at[1, i]) for i in range(count)]
    for copy in loads:
        copy.start()
    for load, store in zip(loads, stores):
        load.wait()
        store.start()
    for copy in stores:
        copy.wait()


def deliver(arrays):
    anywhere = [pl.BlockSpec(memory_space=pl.ANY)] * len(arrays)
    return pl.pallas_call(
        functools.partial(deliver_kernel, len(arrays)),
        out_shape=tuple(jax.ShapeDtypeStruct(a.shape, a.dtype) for a in arrays),
        in_specs=anywhere,
        out_specs=tuple(anywhere),
        scratch_shapes=[pltpu.VMEM(a.shape, a.dtype) for a in arrays] + [pltpu.SemaphoreType.DMA((2, len(arrays)))],
        compiler_params=pltpu.CompilerParams(vmem_limit_bytes=62 * 2**20),
        name="deliver",
    )(*arrays)


def on_device(inputs, lengths, w_in, w_rec, bias, cotangent):
    micro, per, steps, feats = inputs.shape
    hidden = w_rec.shape[1]
    seqs = micro * per
    total = steps * seqs
    vmem = pltpu.VMEM
    dma = pltpu.SemaphoreType.DMA
    blocks = block_count(steps)
    shards = lax.axis_size("dp")
    fused = shards == 16
    if fused:
        last_three = (
            jax.ShapeDtypeStruct((feats // shards, 4 * hidden), F32),
            jax.ShapeDtypeStruct((hidden // shards, 4 * hidden), F32),
            jax.ShapeDtypeStruct((1, 4 * hidden // shards), F32),
        )
        chunks = 2 * hidden // CHUNK
        more = [
            vmem((total, feats), BF),
            vmem((total + seqs, hidden), BF),
            vmem((total, feats), BF),
            vmem((total + seqs, hidden), BF),
            vmem((total, 2 * hidden), BF),
            vmem((total, hidden), BF),
            vmem((16, 8, 4 * hidden // 16), F32),
            vmem((15, 8, 4 * hidden // 16), F32),
            pltpu.SemaphoreType.REGULAR,
            dma((2, 4, blocks)),
            dma((2, blocks)),
            dma((4, steps)),
            dma((6, chunks)),
            dma((10, chunks)),
            dma((2, 4)),
        ]
    else:
        last_three = (
            jax.ShapeDtypeStruct((total, feats), BF),
            jax.ShapeDtypeStruct((total, hidden), BF),
            jax.ShapeDtypeStruct((total, 4 * hidden), BF),
        )
        more = []
    anywhere = pl.BlockSpec(memory_space=pl.ANY)
    results = pl.pallas_call(
        functools.partial(lstm_kernel, steps, seqs, fused),
        out_shape=(
            jax.ShapeDtypeStruct((total, hidden), BF),
            jax.ShapeDtypeStruct((total, feats), BF),
            *last_three,
        ),
        in_specs=[anywhere, pl.BlockSpec(memory_space=pltpu.VMEM)] + [anywhere] * 4,
        out_specs=(anywhere,) * 5,
        scratch_shapes=[
            vmem((total, feats), BF),
            vmem((total + seqs, hidden), BF),
            vmem((total, hidden), BF),
            vmem((total, feats), BF),
            vmem((total, 4 * hidden), F32),
            vmem((total + seqs, hidden), F32),
            vmem((total, 4 * hidden), BF),
            vmem((feats, 4 * hidden), BF),
            vmem((hidden, 4 * hidden), BF),
            vmem((4 * hidden, hidden), BF),
            vmem((4 * hidden, feats), BF),
            vmem((seqs, hidden), F32),
            vmem((seqs, hidden), F32),
            vmem((seqs, 128), F32),
            vmem((1, 4 * hidden), F32),
            dma((7,)),
            dma((11,)),
            dma((blocks,)),
            dma((blocks,)),
            dma((blocks,)),
            dma((blocks,)),
            *more,
        ],
        compiler_params=pltpu.CompilerParams(
            collective_id=0, has_side_effects=True, vmem_limit_bytes=62 * 2**20
        ),
        name="lstm_both_ways",
    )(
        inputs.reshape(total, feats),
        lengths,
        w_in[0],
        w_rec[0],
        bias,
        cotangent.reshape(total, hidden),
    )
    if fused:
        hid, dx, share_in, share_rec, share_bias = deliver(results)
    else:
        hid, dx, u, hp, dz = results
        sum_in = lax.dot_general(u, dz, (((0,), (0,)), ((), ())), preferred_element_type=F32)
        sum_rec = lax.dot_general(hp, dz, (((0,), (0,)), ((), ())), preferred_element_type=F32)
        sum_bias = jnp.sum(dz, axis=0, dtype=F32)
        share_in = lax.psum_scatter(sum_in, "dp", scatter_dimension=0, tiled=True)
        share_rec = lax.psum_scatter(sum_rec, "dp", scatter_dimension=0, tiled=True)
        share_bias = lax.psum_scatter(sum_bias, "dp", scatter_dimension=0, tiled=True)[None]
    shape = inputs.shape
    return (
        hid.reshape(shape)[None],
        dx.reshape(shape)[None],
        share_in[None],
        share_rec[None],
        share_bias,
    )


def solution(mesh):
    placed = (
        P(None, "dp", None, None),
        P(None, "dp"),
        P("section", None, None),
        P("section", None, None),
        P("section", None),
        P(None, "dp", None, None),
    )
    return jax.shard_map(
        on_device,
        mesh=mesh,
        in_specs=placed,
        out_specs=(
            P("section", None, "dp", None, None),
            P("section", None, "dp", None, None),
            P("section", "dp", None),
            P("section", "dp", None),
            P("section", "dp"),
        ),
        check_vma=False,
    )
```

```python
import functools

import jax
import jax.numpy as jnp
from jax import lax
from jax.experimental import pallas as pl
from jax.experimental.pallas import tpu as pltpu
from jax.sharding import PartitionSpec as P

BF = jnp.bfloat16
F32 = jnp.float32
MESH = pl.DeviceIdType.MESH
BLOCK = 4
EDGE = 2
PAD = 128
TILE = 256
CHUNK = 128
WIDE = 256
SOON = True
P_AHEAD = 3
Z_AHEAD = 3
HAND_AFTER = 2
P_LAGS = (2, 4)
Z_LAGS = (2, 4)


def sigmoid(v):
    return 0.5 * jnp.tanh(0.5 * v) + 0.5


def rows_at(start, size):
    return pl.ds(pl.multiple_of(start, size), size)


def dot(a, b):
    return jnp.dot(a, b, preferred_element_type=F32)


def dot_t(a, b):
    return lax.dot_general(a, b, (((1,), (1,)), ((), ())), preferred_element_type=F32)


def padded(rows):
    lack = PAD - rows.shape[0]
    return jnp.concatenate([rows, jnp.zeros((lack, rows.shape[1]), rows.dtype)], axis=0) if lack > 0 else rows


def block_count(steps):
    return 2 + (steps - 2 * EDGE) // BLOCK


def block_span(steps, b):
    if isinstance(b, int):
        if b == 0:
            return 0, EDGE
        if b == block_count(steps) - 1:
            return steps - EDGE, EDGE
    return EDGE + (b - 1) * BLOCK, BLOCK


def z_place(z):
    return 2 * (((z + 1) // 2) % 2) + z // 2


def lstm_kernel(
    steps, seqs, fused,
    x_ref, len_ref, win_ref, wrec_ref, bias_ref, ct_ref,
    hid_out, dx_out, out_a, out_b, out_c,
    u, hs, dy, dx, act, cs, dz, win, wrec, wrt, wint, dr, dc, lens, bias,
    load_sem, store_sem, up_send, up_recv, down_send, down_recv, *more,
):
    hidden = wrec.shape[0]
    gates = 4 * hidden
    total = steps * seqs
    blocks = block_count(steps)
    section = lax.axis_index("section")
    first = section == 0
    second = section == 1
    other = {"section": 1 - section}

    tail = Tail(section, seqs, steps, u, hs, act, cs, dz, win, wrec, wrt, *more) if fused else None

    barrier = pltpu.get_barrier_semaphore()
    pl.semaphore_signal(barrier, inc=1, device_id=other, device_id_type=MESH)
    if fused:
        for partner in tail.partners:
            pl.semaphore_signal(barrier, inc=1, device_id=partner, device_id_type=MESH)

    load_x = pltpu.make_async_copy(x_ref, dx, load_sem.at[0])
    load_ct = pltpu.make_async_copy(ct_ref, dx, load_sem.at[0])
    load_wrec = pltpu.make_async_copy(wrec_ref, wrec, load_sem.at[1])

    def load_win(g):
        part = pl.ds(g * hidden, hidden)
        return pltpu.make_async_copy(win_ref.at[:, part], win.at[:, part], load_sem.at[2 + g])

    load_bias = pltpu.make_async_copy(bias_ref, bias, load_sem.at[6])
    pl.when(first)(lambda: load_x.start())
    pl.when(second)(lambda: load_ct.start())
    load_bias.start()
    for g in range(4):
        load_win(g).start()
    load_wrec.start()

    micro, per = len_ref.shape
    row_id = lax.broadcasted_iota(jnp.int32, (per, per), 0)
    col_id = lax.broadcasted_iota(jnp.int32, (per, per), 1)
    for m in range(micro):
        row = jnp.broadcast_to(len_ref[m : m + 1, :].astype(F32), (per, per))
        column = jnp.sum(jnp.where(row_id == col_id, row, 0.0), axis=1, keepdims=True)
        lens[m * per : (m + 1) * per, :] = jnp.broadcast_to(column, (per, lens.shape[1]))

    hs[0:seqs, :] = jnp.zeros((seqs, hidden), BF)
    cs[0:seqs, :] = jnp.zeros((seqs, hidden), F32)
    dr[...] = jnp.zeros_like(dr)
    dc[...] = jnp.zeros_like(dc)
    if fused:
        tail.clear()

    def order(outer, inner, perm):
        to_id = lax.broadcasted_iota(jnp.int32, (inner, total), 0)
        from_id = lax.broadcasted_iota(jnp.int32, (inner, total), 1)
        for n in range(outer):
            perm[n * inner : (n + 1) * inner, :] = jnp.where(to_id * outer + n == from_id, 1.0, 0.0).astype(BF)

    def reorder(perm, source, skip, columns, write):
        for j in columns:
            cols = slice(j, j + TILE)
            write(cols, dot(perm[...], source[skip : skip + total, cols]).astype(BF))

    def write_first(cols, value):
        @pl.when(first)
        def _():
            u[:, cols] = value

        @pl.when(second)
        def _():
            dy[:, cols] = value

    load_x.wait()
    order(steps, seqs, wrt.at[0:total, 0:total])
    reorder(wrt.at[0:total, 0:total], dx, 0, range(0, hidden, TILE), write_first)

    load_bias.wait()

    eye = jnp.where(
        lax.broadcasted_iota(jnp.int32, (TILE, TILE), 0) == lax.broadcasted_iota(jnp.int32, (TILE, TILE), 1), 1.0, 0.0
    ).astype(BF)

    def turn_over(source, target):
        def piece(i, carry):
            at = rows_at(i * TILE, TILE)
            target[at, :] = dot_t(eye, source[:, at]).astype(BF)
            return carry

        lax.fori_loop(0, gates // TILE, piece, 0)

    @pl.when(second)
    def _():
        for g in range(4):
            load_win(g).wait()
        turn_over(win, wint)
        load_wrec.wait()
        turn_over(wrec, wrt)

    def arrived():
        pl.semaphore_wait(barrier, 1 + len(tail.partners) if fused else 1)

    def rows_of(b, shift=0):
        start, length = block_span(steps, b)
        return pl.ds(pl.multiple_of((start + shift) * seqs, seqs), length * seqs)

    def send_up(b):
        return pltpu.make_async_remote_copy(
            src_ref=hs.at[rows_of(b, 1)],
            dst_ref=u.at[rows_of(b)],
            send_sem=up_send.at[b],
            recv_sem=up_recv.at[b],
            device_id=other,
            device_id_type=MESH,
        )

    def send_down(b):
        return pltpu.make_async_remote_copy(
            src_ref=dx.at[rows_of(b)],
            dst_ref=dy.at[rows_of(b)],
            send_sem=down_send.at[b],
            recv_sem=down_recv.at[b],
            device_id=other,
            device_id_type=MESH,
        )

    def cell(t, recur):
        here = rows_at(t * seqs, seqs)
        after = rows_at((t + 1) * seqs, seqs)
        h_prev = padded(hs[here, :]) if recur else None
        mask = jnp.where(jnp.float32(t) < lens[:, 0:1], 1.0, 0.0)
        for j in range(0, hidden, TILE):
            z = []
            for g in range(4):
                cols = slice(g * hidden + j, g * hidden + j + TILE)
                z.append(act[here, cols] + dot(h_prev, wrec[:, cols])[:seqs] if recur else act[here, cols])
            gi, gf, gg, go = sigmoid(z[0]), sigmoid(z[1]), jnp.tanh(z[2]), sigmoid(z[3])
            c_new = gf * cs[here, j : j + TILE] + gi * gg if recur else gi * gg
            cs[after, j : j + TILE] = c_new
            act[here, j : j + TILE] = gi
            act[here, hidden + j : hidden + j + TILE] = gf
            act[here, 2 * hidden + j : 2 * hidden + j + TILE] = gg
            act[here, 3 * hidden + j : 3 * hidden + j + TILE] = go
            hs[after, j : j + TILE] = (go * jnp.tanh(c_new) * mask).astype(BF)

    def forward_block(b):
        pl.when(second)(lambda: send_up(b).wait_recv())
        start, length = block_span(steps, b)
        here = rows_of(b)
        given = u[here, :]
        given = padded(given)
        for j in range(0, gates, TILE):
            if isinstance(b, int) and b == 0 and j % hidden == 0:
                pl.when(first)(lambda: load_win(j // hidden).wait())
            act[here, j : j + TILE] = dot(given, win[:, j : j + TILE])[: length * seqs] + bias[:, j : j + TILE]
        for k in range(length):
            at_zero = isinstance(b, int) and b == 0 and k == 0
            cell(start + k, not at_zero)
            if at_zero:
                pl.when(first)(lambda: load_wrec.wait())
        if isinstance(b, int) and b == 0:
            arrived()
        pl.when(first)(lambda: send_up(b).start())
        if fused:
            tail.send_factors(b)

    def each_inner(body):
        def wrapped(b, carry):
            body(b)
            return carry

        lax.fori_loop(1, blocks - 1, wrapped, 0)

    forward_block(0)
    each_inner(forward_block)
    forward_block(blocks - 1)

    @pl.when(first)
    def _():
        turn_over(wrec, wrt)
        turn_over(win, wint)

    if fused:
        @pl.when(first)
        def _():
            tail.build_own(eye)
            tail.build_a(eye)

        tail.say_ready()

    def cell_back(t, more_to_come):
        here = rows_at(t * seqs, seqs)
        after = rows_at((t + 1) * seqs, seqs)
        mask = jnp.where(jnp.float32(t) < lens[:, 0:1], 1.0, 0.0)
        for j in range(0, hidden, TILE):
            cols = slice(j, j + TILE)
            dh = dy[here, cols].astype(F32) * mask + dr[:, cols]
            gi = act[here, j : j + TILE]
            gf = act[here, hidden + j : hidden + j + TILE]
            gg = act[here, 2 * hidden + j : 2 * hidden + j + TILE]
            go = act[here, 3 * hidden + j : 3 * hidden + j + TILE]
            tc = jnp.tanh(cs[after, cols])
            e = dc[:, cols] + dh * go * (1.0 - tc * tc)
            dz[here, j : j + TILE] = (e * gg * gi * (1.0 - gi)).astype(BF)
            dz[here, hidden + j : hidden + j + TILE] = (e * cs[here, cols] * gf * (1.0 - gf)).astype(BF)
            dz[here, 2 * hidden + j : 2 * hidden + j + TILE] = (e * gi * (1.0 - gg * gg)).astype(BF)
            dz[here, 3 * hidden + j : 3 * hidden + j + TILE] = (dh * tc * go * (1.0 - go)).astype(BF)
            dc[:, cols] = e * gf
        if fused and SOON:
            tail.send_dz(t)
        if more_to_come:
            dr[...] = dot(padded(dz[here, :]), wrt[...])[:seqs]

    def backward_block(b):
        pl.when(first)(lambda: send_down(b).wait_recv())
        start, length = block_span(steps, b)
        for k in reversed(range(length)):
            cell_back(start + k, not (isinstance(b, int) and b == 0 and k == 0))
        if fused and not SOON:
            for k in range(length):
                tail.send_dz(start + k)
        here = rows_of(b)

        @pl.when(second)
        def _():
            dx[here, :] = dot(padded(dz[here, :]), wint[...])[: length * seqs].astype(BF)
            send_down(b).start()

    def backward_inner(n):
        backward_block(blocks - 1 - n)
        if fused:
            pl.when(first & (n == HAND_AFTER))(lambda: tail.take_from_mate())

    backward_block(blocks - 1)
    each_inner(backward_inner)
    backward_block(0)

    def write_u(cols, value):
        u[:, cols] = value

    def write_dy(cols, value):
        dy[:, cols] = value

    def write_pieces(perm):
        middle = hidden // 2
        left, right = range(0, middle, TILE), range(middle, hidden, TILE)

        def hidden_left():
            order(seqs, steps, perm)
            reorder(perm, hs, seqs, left, write_u)

        def hidden_right():
            reorder(perm, hs, seqs, right, write_u)
            pltpu.make_async_copy(u, hid_out, store_sem.at[0]).start()

        def late_dx(columns):
            @pl.when(first)
            def _():
                for j in columns:
                    dx[:, j : j + TILE] = dot(dz[...], wint[:, j : j + TILE]).astype(BF)

        def grads_right():
            reorder(perm, dx, 0, right, write_dy)
            pltpu.make_async_copy(dy, dx_out, store_sem.at[1]).start()

        return (
            hidden_left, hidden_right, lambda: late_dx(left), lambda: late_dx(right),
            lambda: reorder(perm, dx, 0, left, write_dy), grads_right,
        )

    if fused:
        @pl.when(second)
        def _():
            tail.build_own(eye)
            tail.build_a(eye)

        tail.run(eye, write_pieces, out_a, out_b, out_c, store_sem)
    else:
        stores = [
            pltpu.make_async_copy(u, out_a, store_sem.at[2]),
            pltpu.make_async_copy(hs.at[pl.ds(0, total)], out_b, store_sem.at[3]),
            pltpu.make_async_copy(dz, out_c, store_sem.at[4]),
        ]
        for copy in stores:
            copy.start()
        for copy in stores:
            copy.wait()
        for piece in write_pieces(wrt.at[0:total, 0:total]):
            piece()
    pltpu.make_async_copy(u, hid_out, store_sem.at[0]).wait()
    pltpu.make_async_copy(dy, dx_out, store_sem.at[1]).wait()
    for b in range(blocks):
        pl.when(first)(lambda: send_up(b).wait_send())
        pl.when(second)(lambda: send_down(b).wait_send())


class Tail:
    def __init__(self, section, seqs, steps, u, hs, act, cs, dz, win, wrec, wrt,
                 u_a, h_a, u_z, h_z, dz_a, dz_z, bsum, brecv, ready,
                 f_sems, o_sems, dz_sems, p_sems, z_sems, c_sems):
        self.s, self.seqs, self.steps, self.blocks = section, seqs, steps, block_count(steps)
        self.first, self.second = section == 0, section == 1
        self.hidden = wrec.shape[0]
        self.quarter = self.hidden
        self.u, self.hs, self.act, self.cs, self.dz = u, hs, act, cs, dz
        self.win, self.wrec, self.wrt = win, wrec, wrt
        self.u_a, self.h_a, self.u_z, self.h_z = u_a, h_a, u_z, h_z
        self.dz_theirs = (dz_a, dz_z)
        self.bsum, self.brecv, self.ready = bsum, brecv, ready
        self.f_sems, self.o_sems, self.dz_sems, self.p_sems = f_sems, o_sems, dz_sems, p_sems
        self.z_sems, self.c_sems = z_sems, c_sems
        j = lax.axis_index("dp")
        x, y, z = j % 2, (j // 2) % 2, j // 4
        s = section
        self.x, self.y, self.z = x, y, z
        self.ca = x * (1 - s) + y * s
        self.cb = y * (1 - s) + x * s
        self.zp, self.zin, self.kz = z % 2, z // 2, ((z + 1) // 2) % 2
        jx, jy = j + 1 - 2 * x, j + 2 - 4 * y
        self.to_a = {"dp": jx * (1 - s) + jy * s}
        self.to_b = {"dp": jy * (1 - s) + jx * s}
        self.to_mate = {"dp": j + 4 - 8 * self.zp}
        self.to_across = {"dp": j + 4 * (3 - 2 * z)}
        self.to_z = [{"dp": j - 4 * z + 4 * ((z + 3 - i) % 4)} for i in range(3)]
        self.partners = [{"dp": jx}, {"dp": jy}] + self.to_z
        self.rows = dz.shape[0]
        self.chunks = 2 * (self.quarter // CHUNK)
        self.unit = self.hidden // 16

    def remote(self, src, dst, send, recv, to):
        return pltpu.make_async_remote_copy(
            src_ref=src, dst_ref=dst, send_sem=send, recv_sem=recv, device_id=to, device_id_type=MESH
        )

    def clear(self):
        zeros = jnp.zeros((self.seqs, self.hidden), BF)
        self.h_a[0 : self.seqs, :] = zeros
        self.h_z[0 : self.seqs, :] = zeros


    def rows_of(self, b, shift=0):
        start, length = block_span(self.steps, b)
        return pl.ds(pl.multiple_of((start + shift) * self.seqs, self.seqs), length * self.seqs)

    def factor(self, i, b):
        at_u, at_h = self.rows_of(b), self.rows_of(b, 1)
        src, dst, at, to = (
            (self.u, self.u_a, at_u, self.to_a),
            (self.hs, self.h_a, at_h, self.to_a),
            (self.u, self.u_z, at_u, self.to_mate),
            (self.hs, self.h_z, at_h, self.to_mate),
        )[i]
        return self.remote(src.at[at], dst.at[at], self.f_sems.at[0, i, b], self.f_sems.at[1, i, b], to)

    def send_factors(self, b):
        if isinstance(b, int) and b == 0:

            @pl.when(self.first)
            def _():
                for n in range(self.blocks):
                    self.factor(0, n).start()
                    self.factor(2, n).start()

        pl.when(self.second)(lambda: self.factor(0, b).start())
        self.factor(1, b).start()
        self.factor(3, b).start()

    def hand_over(self, b):
        return self.remote(
            self.h_z.at[self.rows_of(b, 1)],
            self.u_z.at[self.rows_of(b)],
            self.o_sems.at[0, b],
            self.o_sems.at[1, b],
            {"section": 1 - self.s},
        )

    def build_z(self, eye):
        self.build(eye, self.u_z, 0, 2)
        self.build(eye, self.h_z, 1, 2)

    def take_from_mate(self):
        for b in range(self.blocks):
            self.factor(3, b).wait_recv()
            self.hand_over(b).start()
    def say_ready(self):
        for partner in self.partners:
            pl.semaphore_signal(self.ready, inc=1, device_id=partner, device_id_type=MESH)

    def wait_ready(self):
        pl.semaphore_wait(self.ready, len(self.partners))

    def dz_copy(self, i, t):
        at = pl.ds(pl.multiple_of(t * self.seqs, self.seqs), self.seqs)
        cols = pl.ds(0, 2 * self.quarter)
        if i == 1:
            cols = pl.ds(pl.multiple_of((3 - self.zp) * self.quarter, self.quarter), self.quarter)
        return self.remote(
            self.dz.at[at, cols],
            self.dz_theirs[i].at[at],
            self.dz_sems.at[2 * i, t],
            self.dz_sems.at[2 * i + 1, t],
            (self.to_a, self.to_mate)[i],
        )

    def send_dz(self, t):
        for i in range(2):
            self.dz_copy(i, t).start()

    def place(self, j):
        x, y, z = j % 2, (j // 2) % 2, j // 4
        a = x * (1 - self.s) + y * self.s
        b = y * (1 - self.s) + x * self.s
        return a * 8 + b * 4 + z_place(z)

    def build(self, eye, source, g, origin):
        unit, rows = self.unit, self.rows
        left = (g * 3 + origin) * rows
        for f in range(self.hidden // TILE):
            turned = dot_t(eye, source[0:rows, f * TILE : (f + 1) * TILE]).astype(BF)
            for i in range(TILE // unit):
                row = self.place(f * (TILE // unit) + i) * unit
                at = pl.ds(pl.multiple_of(row, unit), unit)
                self.win[at, left : left + rows] = turned[i * unit : (i + 1) * unit, :]

    def build_own(self, eye):
        self.build(eye, self.u, 0, 0)
        self.build(eye, self.hs, 1, 0)

    def build_a(self, eye):
        for b in range(self.blocks):
            self.factor(0, b).wait_recv()
            self.factor(1, b).wait_recv()
        self.build(eye, self.u_a, 0, 1)
        self.build(eye, self.h_a, 1, 1)


    def p_out(self, c, row, size):
        return (
            pl.ds(pl.multiple_of((c // (self.hidden // WIDE)) * 512 + row, 64), size),
            pl.ds(pl.multiple_of((c % (self.hidden // WIDE)) * WIDE, WIDE), WIDE),
        )

    def p_in(self, c, row, size):
        return (
            pl.ds(pl.multiple_of((c // (2 * self.hidden // WIDE)) * 512 + row, 64), size),
            pl.ds(pl.multiple_of((c % (2 * self.hidden // WIDE)) * WIDE, WIDE), WIDE),
        )

    def p_kept(self, c, row, size):
        return (
            pl.ds(pl.multiple_of((c // (2 * self.hidden // WIDE)) * 256 + row, 64), size),
            pl.ds(pl.multiple_of((c % (2 * self.hidden // WIDE)) * WIDE, WIDE), WIDE),
        )

    def z_out(self, c, row, size):
        wide = self.hidden // CHUNK
        return (
            pl.ds(pl.multiple_of(2 * self.hidden + (c // wide) * self.hidden + row, 64), size),
            pl.ds(pl.multiple_of((c % wide) * CHUNK, CHUNK), CHUNK),
        )

    def z_in(self, c, row, size):
        return (
            pl.ds(pl.multiple_of(row, 64), size),
            pl.ds(pl.multiple_of(2 * self.hidden + c * CHUNK, CHUNK), CHUNK),
        )

    def p_moved(self, c, i, row, size, to):
        return self.remote(
            self.wrt.at[self.p_out(c, row, size)], self.wrec.at[self.p_in(c, row, size)],
            self.p_sems.at[2 * i, c], self.p_sems.at[2 * i + 1, c], to,
        )

    def z_moved(self, c, i, row, size, to):
        return self.remote(
            self.wrt.at[self.z_out(c, row, size)], self.wrec.at[self.z_in(c, row, size)],
            self.z_sems.at[2 * i, c], self.z_sems.at[2 * i + 1, c], to,
        )

    def p_along_b(self, c):
        return self.p_moved(c, 0, 0, 256, self.to_b)

    def p_mate(self, c):
        return self.p_moved(c, 1, 256, 128, self.to_mate)

    def p_across(self, c):
        return self.p_moved(c, 2, 384, 64, self.to_across)

    def z_along_a(self, c):
        return self.z_moved(c, 0, 0, 512, self.to_a)

    def z_along_b(self, c):
        return self.z_moved(c, 1, 512, 256, self.to_b)

    def z_all(self, c, i):
        return self.z_moved(c, 2 + i, 768 + 64 * i, 64, self.to_z[i])

    def product(self, c, row, size, origin, own, theirs):
        rows = self.rows
        at = pl.ds(pl.multiple_of(row, size), size)
        left = (c % 2) * 3 * rows
        one = dot(self.win[at, pl.ds(pl.multiple_of(left, rows), rows)], own)
        two = dot(self.win[at, pl.ds(pl.multiple_of(left + origin * rows, rows), rows)], theirs)
        return one + two

    def p_make(self, c):
        at = pl.ds(pl.multiple_of((c // 2) * WIDE, WIDE), WIDE)
        own, theirs = self.dz[:, at], self.dz_theirs[0][:, at]
        base = self.ca * 512
        self.wrt[self.p_out(c, 0, 256)] = self.product(c, base + (1 - self.cb) * 256, 256, 1, own, theirs).astype(BF)
        self.act[self.p_kept(c, 0, 256)] = self.product(c, base + self.cb * 256, 256, 1, own, theirs)
        self.p_along_b(c).start()

    def z_make(self, c):
        own = self.dz[:, pl.ds(pl.multiple_of((2 + self.zp) * self.quarter + (c // 2) * CHUNK, CHUNK), CHUNK)]
        theirs = self.dz_theirs[1][:, pl.ds(pl.multiple_of((c // 2) * CHUNK, CHUNK), CHUNK)]
        self.wrt[self.z_out(c, 0, 512)] = self.product(c, (1 - self.ca) * 512, 512, 2, own, theirs).astype(BF)
        self.act[self.z_in(c, 0, 512)] = self.product(c, self.ca * 512, 512, 2, own, theirs)
        self.z_along_a(c).start()

    def bias_plan(self, i):
        one = self.kz * 8
        two = one + self.zin * 4
        three = two + self.ca * 2
        return (
            ((1 - self.kz) * 8, one, 8, 0, self.to_mate),
            (one + (1 - self.zin) * 4, two, 4, 8, self.to_across),
            (two + (1 - self.ca) * 2, three, 2, 12, self.to_a),
            (three + 1 - self.cb, three + self.cb, 1, 14, self.to_b),
        )[i]

    def bias_copy(self, i):
        start, _, size, land, to = self.bias_plan(i)
        return self.remote(
            self.bsum.at[pl.ds(start, size)],
            self.brecv.at[pl.ds(land, size)],
            self.c_sems.at[0, i],
            self.c_sems.at[1, i],
            to,
        )

    def bias_start(self):
        ones = jnp.where(lax.broadcasted_iota(jnp.int32, (PAD, self.rows), 0) == 0, 1.0, 0.0).astype(BF)
        width = 4 * self.hidden // 16
        for j in range(16):
            x, y, z = j % 2, (j // 2) % 2, j // 4
            a = x * (1 - self.s) + y * self.s
            b = y * (1 - self.s) + x * self.s
            self.bsum[z_place(z) * 4 + a * 2 + b] = dot(ones, self.dz[:, j * width : (j + 1) * width])[0:8]
        self.bias_copy(0).start()

    def bias_step(self, i):
        self.bias_copy(i).wait_recv()
        _, start, size, land, _ = self.bias_plan(i)
        mine = pl.ds(start, size)
        self.bsum[mine] = self.bsum[mine] + self.brecv[land : land + size]
        if i < 3:
            self.bias_copy(i + 1).start()

    def put(self, c, column, value):
        quarter, width = self.quarter, value.shape[1]
        rows = pl.ds(pl.multiple_of(((c % 2) * 4 + column // quarter) * self.unit, self.unit), self.unit)
        self.cs[rows, pl.ds(pl.multiple_of(column % quarter, width), width)] = value

    def run(self, eye, write_pieces, out_in, out_rec, out_bias, store_sem):
        act, wrec, wrt = self.act, self.wrec, self.wrt
        chunks, blocks, steps = self.chunks, self.blocks, self.steps

        def loop(start, stop, body):
            def wrapped(c, carry):
                body(c)
                return carry

            lax.fori_loop(start, stop, wrapped, 0)

        def span(start, size):
            return pl.ds(pl.multiple_of(start, size), size)

        def dz_arrived(i):
            def one(t):
                self.dz_copy(i, t).wait_recv()

            loop(0, steps, one)

        dz_arrived(0)
        self.wait_ready()
        loop(0, P_AHEAD, self.p_make)

        @pl.when(self.first)
        def _():
            for b in range(blocks):
                self.factor(2, b).wait_recv()

        @pl.when(self.second)
        def _():
            for b in range(blocks):
                self.factor(3, b).wait_recv()
                self.hand_over(b).wait_recv()

        self.build_z(eye)
        dz_arrived(1)
        loop(0, Z_AHEAD, self.z_make)

        pieces = write_pieces(self.u_a.at[:, 0 : self.rows])

        def first_piece():
            for b in range(blocks):
                for i in (0, 1, 3):
                    self.factor(i, b).wait_send()

            @pl.when(self.first)
            def _():
                for b in range(blocks):
                    self.factor(2, b).wait_send()
                    self.hand_over(b).wait_send()

            pieces[0]()

        extra = (
            (1, self.bias_start), (2, first_piece), (4, pieces[1]), (5, lambda: self.bias_step(0)), (6, pieces[2]),
            (8, pieces[3]), (9, lambda: self.bias_step(1)), (10, pieces[4]), (12, pieces[5]), (13, lambda: self.bias_step(2)),
        )

        def total(kept, landed):
            return act[kept] + wrec[landed].astype(F32)

        def p_after_b(c):
            self.p_along_b(c).wait_recv()
            theirs, mine = (1 - self.kz) * 128, self.kz * 128
            wrt[self.p_out(c, 256, 128)] = total(self.p_kept(c, theirs, 128), self.p_in(c, theirs, 128)).astype(BF)
            self.p_mate(c).start()
            kept = self.p_kept(c, mine, 128)
            act[kept] = total(kept, self.p_in(c, mine, 128))

        def p_after_mate(c):
            self.p_mate(c).wait_recv()
            base = self.kz * 128
            theirs, mine = (1 - self.zin) * 64, self.zin * 64
            wrt[self.p_out(c, 384, 64)] = total(
                self.p_kept(c, base + theirs, 64), self.p_in(c, 256 + theirs, 64)
            ).astype(BF)
            self.p_across(c).start()
            kept = self.p_kept(c, base + mine, 64)
            act[kept] = total(kept, self.p_in(c, 256 + mine, 64))

        def p_after_across(c):
            self.p_across(c).wait_recv()
            kept = self.p_kept(c, self.kz * 128 + self.zin * 64, 64)
            self.put(c, (c // 2) * WIDE, total(kept, self.p_in(c, 384, 64)))

        def z_after_a(c):
            self.z_along_a(c).wait_recv()
            theirs, mine = (1 - self.cb) * 256, self.cb * 256
            wrt[self.z_out(c, 512, 256)] = total(self.z_in(c, theirs, 256), self.z_in(c, theirs, 256)).astype(BF)
            self.z_along_b(c).start()
            kept = self.z_in(c, mine, 256)
            act[kept] = total(kept, kept)

        def z_after_b(c):
            self.z_along_b(c).wait_recv()
            base = self.cb * 256
            for i in range(3):
                row = z_place((self.z + 3 - i) % 4) * 64
                wrt[self.z_out(c, 768 + 64 * i, 64)] = total(
                    self.z_in(c, base + row, 64), self.z_in(c, 512 + row, 64)
                ).astype(BF)
                self.z_all(c, i).start()
            row = z_place(self.z) * 64
            kept = self.z_in(c, base + row, 64)
            act[kept] = total(kept, self.z_in(c, 512 + row, 64))

        def z_after_all(c):
            for i in range(3):
                self.z_all(c, i).wait_recv()
            column = 2 * self.quarter + (c // 2) * CHUNK
            kept = self.z_in(c, self.cb * 256 + z_place(self.z) * 64, 64)
            self.put(c, column + self.zp * self.quarter, total(kept, self.z_in(c, 832, 64)))
            opposite = wrec[self.z_in(c, 768, 64)].astype(F32) + wrec[self.z_in(c, 896, 64)].astype(F32)
            self.put(c, column + (1 - self.zp) * self.quarter, opposite)

        stages = (
            (p_after_mate, P_LAGS[0]), (z_after_b, Z_LAGS[0]),
            (p_after_across, P_LAGS[1]), (z_after_all, Z_LAGS[1]),
            (p_after_b, 0), (z_after_a, 0), (self.p_make, -P_AHEAD), (self.z_make, -Z_AHEAD),
        )

        def turn(n, carry):
            for work, lag in stages:
                c = n - lag
                pl.when((c >= 0) & (c < chunks))(lambda: work(c))
            for at, work in extra:
                pl.when(n == at)(work)
            return carry

        lax.fori_loop(0, chunks + max(P_LAGS[1], Z_LAGS[1]), turn, 0)
        self.bias_step(3)

        mine = self.bias_plan(3)[1]
        self.brecv[0, 0:1, :] = jnp.sum(self.bsum[mine], axis=0, keepdims=True)
        bias_store = pltpu.make_async_copy(self.brecv.at[0, pl.ds(0, 1)], out_bias, store_sem.at[2])
        bias_store.start()

        def result(n):
            g, q = n // 4, n % 4
            out = (out_in, out_rec)[g]
            rows = pl.ds(n * self.unit, self.unit)
            return pltpu.make_async_copy(
                self.cs.at[rows], out.at[:, pl.ds(q * self.quarter, self.quarter)], store_sem.at[3 + n]
            )

        for n in range(8):
            result(n).start()

        def dz_sent(t):
            for i in range(2):
                self.dz_copy(i, t).wait_send()

        loop(0, steps, dz_sent)
        for i in range(4):
            self.bias_copy(i).wait_send()

        def sent(c):
            for part in (self.p_along_b, self.p_mate, self.p_across, self.z_along_a, self.z_along_b):
                part(c).wait_send()
            for i in range(3):
                self.z_all(c, i).wait_send()

        loop(0, chunks, sent)
        bias_store.wait()
        for n in range(8):
            result(n).wait()


def deliver_kernel(count, *refs):
    sources, targets, held, sems = refs[:count], refs[count : 2 * count], refs[2 * count : 3 * count], refs[3 * count]
    loads = [pltpu.make_async_copy(sources[i], held[i], sems.at[0, i]) for i in range(count)]
    stores = [pltpu.make_async_copy(held[i], targets[i], sems.at[1, i]) for i in range(count)]
    for copy in loads:
        copy.start()
    for load, store in zip(loads, stores):
        load.wait()
        store.start()
    for copy in stores:
        copy.wait()


def deliver(arrays):
    anywhere = [pl.BlockSpec(memory_space=pl.ANY)] * len(arrays)
    return pl.pallas_call(
        functools.partial(deliver_kernel, len(arrays)),
        out_shape=tuple(jax.ShapeDtypeStruct(a.shape, a.dtype) for a in arrays),
        in_specs=anywhere,
        out_specs=tuple(anywhere),
        scratch_shapes=[pltpu.VMEM(a.shape, a.dtype) for a in arrays] + [pltpu.SemaphoreType.DMA((2, len(arrays)))],
        compiler_params=pltpu.CompilerParams(vmem_limit_bytes=62 * 2**20),
        name="deliver",
    )(*arrays)


def on_device(inputs, lengths, w_in, w_rec, bias, cotangent):
    micro, per, steps, feats = inputs.shape
    hidden = w_rec.shape[1]
    seqs = micro * per
    total = steps * seqs
    vmem = pltpu.VMEM
    dma = pltpu.SemaphoreType.DMA
    blocks = block_count(steps)
    shards = lax.axis_size("dp")
    fused = shards == 16
    if fused:
        last_three = (
            jax.ShapeDtypeStruct((feats // shards, 4 * hidden), F32),
            jax.ShapeDtypeStruct((hidden // shards, 4 * hidden), F32),
            jax.ShapeDtypeStruct((1, 4 * hidden // shards), F32),
        )
        chunks = 2 * hidden // CHUNK
        more = [
            vmem((total, feats), BF),
            vmem((total + seqs, hidden), BF),
            vmem((total, feats), BF),
            vmem((total + seqs, hidden), BF),
            vmem((total, 2 * hidden), BF),
            vmem((total, hidden), BF),
            vmem((16, 8, 4 * hidden // 16), F32),
            vmem((15, 8, 4 * hidden // 16), F32),
            pltpu.SemaphoreType.REGULAR,
            dma((2, 4, blocks)),
            dma((2, blocks)),
            dma((4, steps)),
            dma((6, chunks)),
            dma((10, chunks)),
            dma((2, 4)),
        ]
    else:
        last_three = (
            jax.ShapeDtypeStruct((total, feats), BF),
            jax.ShapeDtypeStruct((total, hidden), BF),
            jax.ShapeDtypeStruct((total, 4 * hidden), BF),
        )
        more = []
    anywhere = pl.BlockSpec(memory_space=pl.ANY)
    results = pl.pallas_call(
        functools.partial(lstm_kernel, steps, seqs, fused),
        out_shape=(
            jax.ShapeDtypeStruct((total, hidden), BF),
            jax.ShapeDtypeStruct((total, feats), BF),
            *last_three,
        ),
        in_specs=[anywhere, pl.BlockSpec(memory_space=pltpu.VMEM)] + [anywhere] * 4,
        out_specs=(anywhere,) * 5,
        scratch_shapes=[
            vmem((total, feats), BF),
            vmem((total + seqs, hidden), BF),
            vmem((total, hidden), BF),
            vmem((total, feats), BF),
            vmem((total, 4 * hidden), F32),
            vmem((total + seqs, hidden), F32),
            vmem((total, 4 * hidden), BF),
            vmem((feats, 4 * hidden), BF),
            vmem((hidden, 4 * hidden), BF),
            vmem((4 * hidden, hidden), BF),
            vmem((4 * hidden, feats), BF),
            vmem((seqs, hidden), F32),
            vmem((seqs, hidden), F32),
            vmem((seqs, 128), F32),
            vmem((1, 4 * hidden), F32),
            dma((7,)),
            dma((11,)),
            dma((blocks,)),
            dma((blocks,)),
            dma((blocks,)),
            dma((blocks,)),
            *more,
        ],
        compiler_params=pltpu.CompilerParams(
            collective_id=0, has_side_effects=True, vmem_limit_bytes=62 * 2**20
        ),
        name="lstm_both_ways",
    )(
        inputs.reshape(total, feats),
        lengths,
        w_in[0],
        w_rec[0],
        bias,
        cotangent.reshape(total, hidden),
    )
    if fused:
        hid, dx, share_in, share_rec, share_bias = deliver(results)
    else:
        hid, dx, u, hp, dz = results
        sum_in = lax.dot_general(u, dz, (((0,), (0,)), ((), ())), preferred_element_type=F32)
        sum_rec = lax.dot_general(hp, dz, (((0,), (0,)), ((), ())), preferred_element_type=F32)
        sum_bias = jnp.sum(dz, axis=0, dtype=F32)
        share_in = lax.psum_scatter(sum_in, "dp", scatter_dimension=0, tiled=True)
        share_rec = lax.psum_scatter(sum_rec, "dp", scatter_dimension=0, tiled=True)
        share_bias = lax.psum_scatter(sum_bias, "dp", scatter_dimension=0, tiled=True)[None]
    shape = inputs.shape
    return (
        hid.reshape(shape)[None],
        dx.reshape(shape)[None],
        share_in[None],
        share_rec[None],
        share_bias,
    )


def solution(mesh):
    placed = (
        P(None, "dp", None, None),
        P(None, "dp"),
        P("section", None, None),
        P("section", None, None),
        P("section", None),
        P(None, "dp", None, None),
    )
    return jax.shard_map(
        on_device,
        mesh=mesh,
        in_specs=placed,
        out_specs=(
            P("section", None, "dp", None, None),
            P("section", None, "dp", None, None),
            P("section", "dp", None),
            P("section", "dp", None),
            P("section", "dp"),
        ),
        check_vma=False,
    )
```

```python
import functools

import jax
import jax.numpy as jnp
from jax import lax
from jax.experimental import pallas as pl
from jax.experimental.pallas import tpu as pltpu
from jax.sharding import PartitionSpec as P

BF = jnp.bfloat16
F32 = jnp.float32
MESH = pl.DeviceIdType.MESH
BLOCK = 4
EDGE = 2
PAD = 128
TILE = 256
CHUNK = 128
WIDE = 256
SOON = True
P_AHEAD = 3
Z_AHEAD = 4
HAND_AFTER = 2
P_LAGS = (2, 4)
Z_LAGS = (2, 4)


def sigmoid(v):
    return 0.5 * jnp.tanh(0.5 * v) + 0.5


def rows_at(start, size):
    return pl.ds(pl.multiple_of(start, size), size)


def dot(a, b):
    return jnp.dot(a, b, preferred_element_type=F32)


def dot_t(a, b):
    return lax.dot_general(a, b, (((1,), (1,)), ((), ())), preferred_element_type=F32)


def padded(rows):
    lack = PAD - rows.shape[0]
    return jnp.concatenate([rows, jnp.zeros((lack, rows.shape[1]), rows.dtype)], axis=0) if lack > 0 else rows


def block_count(steps):
    return 2 + (steps - 2 * EDGE) // BLOCK


def block_span(steps, b):
    if isinstance(b, int):
        if b == 0:
            return 0, EDGE
        if b == block_count(steps) - 1:
            return steps - EDGE, EDGE
    return EDGE + (b - 1) * BLOCK, BLOCK


def z_place(z):
    return 2 * (((z + 1) // 2) % 2) + z // 2


def lstm_kernel(
    steps, seqs, fused,
    x_ref, len_ref, win_ref, wrec_ref, bias_ref, ct_ref,
    hid_out, dx_out, out_a, out_b, out_c,
    u, hs, dy, dx, act, cs, dz, win, wrec, wrt, wint, dr, dc, lens, bias,
    load_sem, store_sem, up_send, up_recv, down_send, down_recv, *more,
):
    hidden = wrec.shape[0]
    gates = 4 * hidden
    total = steps * seqs
    blocks = block_count(steps)
    section = lax.axis_index("section")
    first = section == 0
    second = section == 1
    other = {"section": 1 - section}

    tail = Tail(section, seqs, steps, u, hs, act, cs, dz, win, wrec, wrt, *more) if fused else None

    barrier = pltpu.get_barrier_semaphore()
    pl.semaphore_signal(barrier, inc=1, device_id=other, device_id_type=MESH)
    if fused:
        for partner in tail.partners:
            pl.semaphore_signal(barrier, inc=1, device_id=partner, device_id_type=MESH)

    load_x = pltpu.make_async_copy(x_ref, dx, load_sem.at[0])
    load_ct = pltpu.make_async_copy(ct_ref, dx, load_sem.at[0])
    load_wrec = pltpu.make_async_copy(wrec_ref, wrec, load_sem.at[1])

    def load_win(g):
        part = pl.ds(g * hidden, hidden)
        return pltpu.make_async_copy(win_ref.at[:, part], win.at[:, part], load_sem.at[2 + g])

    load_bias = pltpu.make_async_copy(bias_ref, bias, load_sem.at[6])
    pl.when(first)(lambda: load_x.start())
    pl.when(second)(lambda: load_ct.start())
    load_bias.start()
    for g in range(4):
        load_win(g).start()
    load_wrec.start()

    micro, per = len_ref.shape
    row_id = lax.broadcasted_iota(jnp.int32, (per, per), 0)
    col_id = lax.broadcasted_iota(jnp.int32, (per, per), 1)
    for m in range(micro):
        row = jnp.broadcast_to(len_ref[m : m + 1, :].astype(F32), (per, per))
        column = jnp.sum(jnp.where(row_id == col_id, row, 0.0), axis=1, keepdims=True)
        lens[m * per : (m + 1) * per, :] = jnp.broadcast_to(column, (per, lens.shape[1]))

    hs[0:seqs, :] = jnp.zeros((seqs, hidden), BF)
    cs[0:seqs, :] = jnp.zeros((seqs, hidden), F32)
    dr[...] = jnp.zeros_like(dr)
    dc[...] = jnp.zeros_like(dc)
    if fused:
        tail.clear()

    def order(outer, inner, perm):
        to_id = lax.broadcasted_iota(jnp.int32, (inner, total), 0)
        from_id = lax.broadcasted_iota(jnp.int32, (inner, total), 1)
        for n in range(outer):
            perm[n * inner : (n + 1) * inner, :] = jnp.where(to_id * outer + n == from_id, 1.0, 0.0).astype(BF)

    def reorder(perm, source, skip, columns, write):
        for j in columns:
            cols = slice(j, j + TILE)
            write(cols, dot(perm[...], source[skip : skip + total, cols]).astype(BF))

    def write_first(cols, value):
        @pl.when(first)
        def _():
            u[:, cols] = value

        @pl.when(second)
        def _():
            dy[:, cols] = value

    load_x.wait()
    order(steps, seqs, wrt.at[0:total, 0:total])
    reorder(wrt.at[0:total, 0:total], dx, 0, range(0, hidden, TILE), write_first)

    load_bias.wait()

    eye = jnp.where(
        lax.broadcasted_iota(jnp.int32, (TILE, TILE), 0) == lax.broadcasted_iota(jnp.int32, (TILE, TILE), 1), 1.0, 0.0
    ).astype(BF)

    def turn_over(source, target):
        def piece(i, carry):
            at = rows_at(i * TILE, TILE)
            target[at, :] = dot_t(eye, source[:, at]).astype(BF)
            return carry

        lax.fori_loop(0, gates // TILE, piece, 0)

    @pl.when(second)
    def _():
        for g in range(4):
            load_win(g).wait()
        turn_over(win, wint)
        load_wrec.wait()
        turn_over(wrec, wrt)

    def arrived():
        pl.semaphore_wait(barrier, 1 + len(tail.partners) if fused else 1)

    def rows_of(b, shift=0):
        start, length = block_span(steps, b)
        return pl.ds(pl.multiple_of((start + shift) * seqs, seqs), length * seqs)

    def send_up(b):
        return pltpu.make_async_remote_copy(
            src_ref=hs.at[rows_of(b, 1)],
            dst_ref=u.at[rows_of(b)],
            send_sem=up_send.at[b],
            recv_sem=up_recv.at[b],
            device_id=other,
            device_id_type=MESH,
        )

    def send_down(b):
        return pltpu.make_async_remote_copy(
            src_ref=dx.at[rows_of(b)],
            dst_ref=dy.at[rows_of(b)],
            send_sem=down_send.at[b],
            recv_sem=down_recv.at[b],
            device_id=other,
            device_id_type=MESH,
        )

    def cell(t, recur):
        here = rows_at(t * seqs, seqs)
        after = rows_at((t + 1) * seqs, seqs)
        h_prev = padded(hs[here, :]) if recur else None
        mask = jnp.where(jnp.float32(t) < lens[:, 0:1], 1.0, 0.0)
        for j in range(0, hidden, TILE):
            z = []
            for g in range(4):
                cols = slice(g * hidden + j, g * hidden + j + TILE)
                z.append(act[here, cols] + dot(h_prev, wrec[:, cols])[:seqs] if recur else act[here, cols])
            gi, gf, gg, go = sigmoid(z[0]), sigmoid(z[1]), jnp.tanh(z[2]), sigmoid(z[3])
            c_new = gf * cs[here, j : j + TILE] + gi * gg if recur else gi * gg
            cs[after, j : j + TILE] = c_new
            act[here, j : j + TILE] = gi
            act[here, hidden + j : hidden + j + TILE] = gf
            act[here, 2 * hidden + j : 2 * hidden + j + TILE] = gg
            act[here, 3 * hidden + j : 3 * hidden + j + TILE] = go
            hs[after, j : j + TILE] = (go * jnp.tanh(c_new) * mask).astype(BF)

    def forward_block(b):
        pl.when(second)(lambda: send_up(b).wait_recv())
        start, length = block_span(steps, b)
        here = rows_of(b)
        given = u[here, :]
        given = padded(given)
        for j in range(0, gates, TILE):
            if isinstance(b, int) and b == 0 and j % hidden == 0:
                pl.when(first)(lambda: load_win(j // hidden).wait())
            act[here, j : j + TILE] = dot(given, win[:, j : j + TILE])[: length * seqs] + bias[:, j : j + TILE]
        for k in range(length):
            at_zero = isinstance(b, int) and b == 0 and k == 0
            cell(start + k, not at_zero)
            if at_zero:
                pl.when(first)(lambda: load_wrec.wait())
        if isinstance(b, int) and b == 0:
            arrived()
        pl.when(first)(lambda: send_up(b).start())
        if fused:
            tail.send_factors(b)

    def each_inner(body):
        def wrapped(b, carry):
            body(b)
            return carry

        lax.fori_loop(1, blocks - 1, wrapped, 0)

    forward_block(0)
    each_inner(forward_block)
    forward_block(blocks - 1)

    @pl.when(first)
    def _():
        turn_over(wrec, wrt)
        turn_over(win, wint)

    if fused:
        @pl.when(first)
        def _():
            tail.build_own(eye)
            tail.build_a(eye)

        tail.say_ready()

    def cell_back(t, more_to_come):
        here = rows_at(t * seqs, seqs)
        after = rows_at((t + 1) * seqs, seqs)
        mask = jnp.where(jnp.float32(t) < lens[:, 0:1], 1.0, 0.0)
        for j in range(0, hidden, TILE):
            cols = slice(j, j + TILE)
            dh = dy[here, cols].astype(F32) * mask + dr[:, cols]
            gi = act[here, j : j + TILE]
            gf = act[here, hidden + j : hidden + j + TILE]
            gg = act[here, 2 * hidden + j : 2 * hidden + j + TILE]
            go = act[here, 3 * hidden + j : 3 * hidden + j + TILE]
            tc = jnp.tanh(cs[after, cols])
            e = dc[:, cols] + dh * go * (1.0 - tc * tc)
            dz[here, j : j + TILE] = (e * gg * gi * (1.0 - gi)).astype(BF)
            dz[here, hidden + j : hidden + j + TILE] = (e * cs[here, cols] * gf * (1.0 - gf)).astype(BF)
            dz[here, 2 * hidden + j : 2 * hidden + j + TILE] = (e * gi * (1.0 - gg * gg)).astype(BF)
            dz[here, 3 * hidden + j : 3 * hidden + j + TILE] = (dh * tc * go * (1.0 - go)).astype(BF)
            dc[:, cols] = e * gf
        if fused and SOON:
            tail.send_dz(t)
        if more_to_come:
            dr[...] = dot(padded(dz[here, :]), wrt[...])[:seqs]

    def backward_block(b):
        pl.when(first)(lambda: send_down(b).wait_recv())
        start, length = block_span(steps, b)
        for k in reversed(range(length)):
            cell_back(start + k, not (isinstance(b, int) and b == 0 and k == 0))
        if fused and not SOON:
            for k in range(length):
                tail.send_dz(start + k)
        here = rows_of(b)

        @pl.when(second)
        def _():
            dx[here, :] = dot(padded(dz[here, :]), wint[...])[: length * seqs].astype(BF)
            send_down(b).start()

    def backward_inner(n):
        backward_block(blocks - 1 - n)
        if fused:
            pl.when(first & (n == HAND_AFTER))(lambda: tail.take_from_mate())

    backward_block(blocks - 1)
    each_inner(backward_inner)
    backward_block(0)

    def write_u(cols, value):
        u[:, cols] = value

    def write_dy(cols, value):
        dy[:, cols] = value

    def write_pieces(perm):
        middle = hidden // 2
        left, right = range(0, middle, TILE), range(middle, hidden, TILE)

        def hidden_left():
            order(seqs, steps, perm)
            reorder(perm, hs, seqs, left, write_u)

        def hidden_right():
            reorder(perm, hs, seqs, right, write_u)
            pltpu.make_async_copy(u, hid_out, store_sem.at[0]).start()

        def late_dx(columns):
            @pl.when(first)
            def _():
                for j in columns:
                    dx[:, j : j + TILE] = dot(dz[...], wint[:, j : j + TILE]).astype(BF)

        def grads_right():
            reorder(perm, dx, 0, right, write_dy)
            pltpu.make_async_copy(dy, dx_out, store_sem.at[1]).start()

        return (
            hidden_left, hidden_right, lambda: late_dx(left), lambda: late_dx(right),
            lambda: reorder(perm, dx, 0, left, write_dy), grads_right,
        )

    if fused:
        @pl.when(second)
        def _():
            tail.build_own(eye)
            tail.build_a(eye)

        tail.run(eye, write_pieces, out_a, out_b, out_c, store_sem)
    else:
        stores = [
            pltpu.make_async_copy(u, out_a, store_sem.at[2]),
            pltpu.make_async_copy(hs.at[pl.ds(0, total)], out_b, store_sem.at[3]),
            pltpu.make_async_copy(dz, out_c, store_sem.at[4]),
        ]
        for copy in stores:
            copy.start()
        for copy in stores:
            copy.wait()
        for piece in write_pieces(wrt.at[0:total, 0:total]):
            piece()
    pltpu.make_async_copy(u, hid_out, store_sem.at[0]).wait()
    pltpu.make_async_copy(dy, dx_out, store_sem.at[1]).wait()
    for b in range(blocks):
        pl.when(first)(lambda: send_up(b).wait_send())
        pl.when(second)(lambda: send_down(b).wait_send())


class Tail:
    def __init__(self, section, seqs, steps, u, hs, act, cs, dz, win, wrec, wrt,
                 u_a, h_a, u_z, h_z, dz_a, dz_z, bsum, brecv, ready,
                 f_sems, o_sems, dz_sems, p_sems, z_sems, c_sems):
        self.s, self.seqs, self.steps, self.blocks = section, seqs, steps, block_count(steps)
        self.first, self.second = section == 0, section == 1
        self.hidden = wrec.shape[0]
        self.quarter = self.hidden
        self.u, self.hs, self.act, self.cs, self.dz = u, hs, act, cs, dz
        self.win, self.wrec, self.wrt = win, wrec, wrt
        self.u_a, self.h_a, self.u_z, self.h_z = u_a, h_a, u_z, h_z
        self.dz_theirs = (dz_a, dz_z)
        self.bsum, self.brecv, self.ready = bsum, brecv, ready
        self.f_sems, self.o_sems, self.dz_sems, self.p_sems = f_sems, o_sems, dz_sems, p_sems
        self.z_sems, self.c_sems = z_sems, c_sems
        j = lax.axis_index("dp")
        x, y, z = j % 2, (j // 2) % 2, j // 4
        s = section
        self.x, self.y, self.z = x, y, z
        self.ca = x * (1 - s) + y * s
        self.cb = y * (1 - s) + x * s
        self.zp, self.zin, self.kz = z % 2, z // 2, ((z + 1) // 2) % 2
        jx, jy = j + 1 - 2 * x, j + 2 - 4 * y
        self.to_a = {"dp": jx * (1 - s) + jy * s}
        self.to_b = {"dp": jy * (1 - s) + jx * s}
        self.to_mate = {"dp": j + 4 - 8 * self.zp}
        self.to_across = {"dp": j + 4 * (3 - 2 * z)}
        self.to_z = [{"dp": j - 4 * z + 4 * ((z + 3 - i) % 4)} for i in range(3)]
        self.partners = [{"dp": jx}, {"dp": jy}] + self.to_z
        self.rows = dz.shape[0]
        self.chunks = 2 * (self.quarter // CHUNK)
        self.unit = self.hidden // 16

    def remote(self, src, dst, send, recv, to):
        return pltpu.make_async_remote_copy(
            src_ref=src, dst_ref=dst, send_sem=send, recv_sem=recv, device_id=to, device_id_type=MESH
        )

    def clear(self):
        zeros = jnp.zeros((self.seqs, self.hidden), BF)
        self.h_a[0 : self.seqs, :] = zeros
        self.h_z[0 : self.seqs, :] = zeros


    def rows_of(self, b, shift=0):
        start, length = block_span(self.steps, b)
        return pl.ds(pl.multiple_of((start + shift) * self.seqs, self.seqs), length * self.seqs)

    def factor(self, i, b):
        at_u, at_h = self.rows_of(b), self.rows_of(b, 1)
        src, dst, at, to = (
            (self.u, self.u_a, at_u, self.to_a),
            (self.hs, self.h_a, at_h, self.to_a),
            (self.u, self.u_z, at_u, self.to_mate),
            (self.hs, self.h_z, at_h, self.to_mate),
        )[i]
        return self.remote(src.at[at], dst.at[at], self.f_sems.at[0, i, b], self.f_sems.at[1, i, b], to)

    def send_factors(self, b):
        if isinstance(b, int) and b == 0:

            @pl.when(self.first)
            def _():
                for n in range(self.blocks):
                    self.factor(0, n).start()
                    self.factor(2, n).start()

        pl.when(self.second)(lambda: self.factor(0, b).start())
        self.factor(1, b).start()
        self.factor(3, b).start()

    def hand_over(self, b):
        return self.remote(
            self.h_z.at[self.rows_of(b, 1)],
            self.u_z.at[self.rows_of(b)],
            self.o_sems.at[0, b],
            self.o_sems.at[1, b],
            {"section": 1 - self.s},
        )

    def build_z(self, eye):
        self.build(eye, self.u_z, 0, 2)
        self.build(eye, self.h_z, 1, 2)

    def take_from_mate(self):
        for b in range(self.blocks):
            self.factor(3, b).wait_recv()
            self.hand_over(b).start()
    def say_ready(self):
        for partner in self.partners:
            pl.semaphore_signal(self.ready, inc=1, device_id=partner, device_id_type=MESH)

    def wait_ready(self):
        pl.semaphore_wait(self.ready, len(self.partners))

    def dz_copy(self, i, t):
        at = pl.ds(pl.multiple_of(t * self.seqs, self.seqs), self.seqs)
        cols = pl.ds(0, 2 * self.quarter)
        if i == 1:
            cols = pl.ds(pl.multiple_of((3 - self.zp) * self.quarter, self.quarter), self.quarter)
        return self.remote(
            self.dz.at[at, cols],
            self.dz_theirs[i].at[at],
            self.dz_sems.at[2 * i, t],
            self.dz_sems.at[2 * i + 1, t],
            (self.to_a, self.to_mate)[i],
        )

    def send_dz(self, t):
        for i in range(2):
            self.dz_copy(i, t).start()

    def place(self, j):
        x, y, z = j % 2, (j // 2) % 2, j // 4
        a = x * (1 - self.s) + y * self.s
        b = y * (1 - self.s) + x * self.s
        return a * 8 + b * 4 + z_place(z)

    def build(self, eye, source, g, origin):
        unit, rows = self.unit, self.rows
        left = (g * 3 + origin) * rows
        for f in range(self.hidden // TILE):
            turned = dot_t(eye, source[0:rows, f * TILE : (f + 1) * TILE]).astype(BF)
            for i in range(TILE // unit):
                row = self.place(f * (TILE // unit) + i) * unit
                at = pl.ds(pl.multiple_of(row, unit), unit)
                self.win[at, left : left + rows] = turned[i * unit : (i + 1) * unit, :]

    def build_own(self, eye):
        self.build(eye, self.u, 0, 0)
        self.build(eye, self.hs, 1, 0)

    def build_a(self, eye):
        for b in range(self.blocks):
            self.factor(0, b).wait_recv()
            self.factor(1, b).wait_recv()
        self.build(eye, self.u_a, 0, 1)
        self.build(eye, self.h_a, 1, 1)


    def p_out(self, c, row, size):
        return (
            pl.ds(pl.multiple_of((c // (self.hidden // WIDE)) * 512 + row, 64), size),
            pl.ds(pl.multiple_of((c % (self.hidden // WIDE)) * WIDE, WIDE), WIDE),
        )

    def p_in(self, c, row, size):
        return (
            pl.ds(pl.multiple_of((c // (2 * self.hidden // WIDE)) * 512 + row, 64), size),
            pl.ds(pl.multiple_of((c % (2 * self.hidden // WIDE)) * WIDE, WIDE), WIDE),
        )

    def p_kept(self, c, row, size):
        return (
            pl.ds(pl.multiple_of((c // (2 * self.hidden // WIDE)) * 256 + row, 64), size),
            pl.ds(pl.multiple_of((c % (2 * self.hidden // WIDE)) * WIDE, WIDE), WIDE),
        )

    def z_out(self, c, row, size):
        wide = self.hidden // CHUNK
        return (
            pl.ds(pl.multiple_of(2 * self.hidden + (c // wide) * self.hidden + row, 64), size),
            pl.ds(pl.multiple_of((c % wide) * CHUNK, CHUNK), CHUNK),
        )

    def z_in(self, c, row, size):
        return (
            pl.ds(pl.multiple_of(row, 64), size),
            pl.ds(pl.multiple_of(2 * self.hidden + c * CHUNK, CHUNK), CHUNK),
        )

    def p_moved(self, c, i, row, size, to):
        return self.remote(
            self.wrt.at[self.p_out(c, row, size)], self.wrec.at[self.p_in(c, row, size)],
            self.p_sems.at[2 * i, c], self.p_sems.at[2 * i + 1, c], to,
        )

    def z_moved(self, c, i, row, size, to):
        return self.remote(
            self.wrt.at[self.z_out(c, row, size)], self.wrec.at[self.z_in(c, row, size)],
            self.z_sems.at[2 * i, c], self.z_sems.at[2 * i + 1, c], to,
        )

    def p_along_b(self, c):
        return self.p_moved(c, 0, 0, 256, self.to_b)

    def p_mate(self, c):
        return self.p_moved(c, 1, 256, 128, self.to_mate)

    def p_across(self, c):
        return self.p_moved(c, 2, 384, 64, self.to_across)

    def z_along_a(self, c):
        return self.z_moved(c, 0, 0, 512, self.to_a)

    def z_along_b(self, c):
        return self.z_moved(c, 1, 512, 256, self.to_b)

    def z_all(self, c, i):
        return self.z_moved(c, 2 + i, 768 + 64 * i, 64, self.to_z[i])

    def product(self, c, row, size, origin, own, theirs):
        rows = self.rows
        at = pl.ds(pl.multiple_of(row, size), size)
        left = (c % 2) * 3 * rows
        one = dot(self.win[at, pl.ds(pl.multiple_of(left, rows), rows)], own)
        two = dot(self.win[at, pl.ds(pl.multiple_of(left + origin * rows, rows), rows)], theirs)
        return one + two

    def p_make(self, c):
        at = pl.ds(pl.multiple_of((c // 2) * WIDE, WIDE), WIDE)
        own, theirs = self.dz[:, at], self.dz_theirs[0][:, at]
        base = self.ca * 512
        self.wrt[self.p_out(c, 0, 256)] = self.product(c, base + (1 - self.cb) * 256, 256, 1, own, theirs).astype(BF)
        self.act[self.p_kept(c, 0, 256)] = self.product(c, base + self.cb * 256, 256, 1, own, theirs)
        self.p_along_b(c).start()

    def z_make(self, c):
        own = self.dz[:, pl.ds(pl.multiple_of((2 + self.zp) * self.quarter + (c // 2) * CHUNK, CHUNK), CHUNK)]
        theirs = self.dz_theirs[1][:, pl.ds(pl.multiple_of((c // 2) * CHUNK, CHUNK), CHUNK)]
        self.wrt[self.z_out(c, 0, 512)] = self.product(c, (1 - self.ca) * 512, 512, 2, own, theirs).astype(BF)
        self.act[self.z_in(c, 0, 512)] = self.product(c, self.ca * 512, 512, 2, own, theirs)
        self.z_along_a(c).start()

    def bias_plan(self, i):
        one = self.kz * 8
        two = one + self.zin * 4
        three = two + self.ca * 2
        return (
            ((1 - self.kz) * 8, one, 8, 0, self.to_mate),
            (one + (1 - self.zin) * 4, two, 4, 8, self.to_across),
            (two + (1 - self.ca) * 2, three, 2, 12, self.to_a),
            (three + 1 - self.cb, three + self.cb, 1, 14, self.to_b),
        )[i]

    def bias_copy(self, i):
        start, _, size, land, to = self.bias_plan(i)
        return self.remote(
            self.bsum.at[pl.ds(start, size)],
            self.brecv.at[pl.ds(land, size)],
            self.c_sems.at[0, i],
            self.c_sems.at[1, i],
            to,
        )

    def bias_start(self):
        ones = jnp.where(lax.broadcasted_iota(jnp.int32, (PAD, self.rows), 0) == 0, 1.0, 0.0).astype(BF)
        width = 4 * self.hidden // 16
        for j in range(16):
            x, y, z = j % 2, (j // 2) % 2, j // 4
            a = x * (1 - self.s) + y * self.s
            b = y * (1 - self.s) + x * self.s
            self.bsum[z_place(z) * 4 + a * 2 + b] = dot(ones, self.dz[:, j * width : (j + 1) * width])[0:8]
        self.bias_copy(0).start()

    def bias_step(self, i):
        self.bias_copy(i).wait_recv()
        _, start, size, land, _ = self.bias_plan(i)
        mine = pl.ds(start, size)
        self.bsum[mine] = self.bsum[mine] + self.brecv[land : land + size]
        if i < 3:
            self.bias_copy(i + 1).start()

    def put(self, c, column, value):
        quarter, width = self.quarter, value.shape[1]
        rows = pl.ds(pl.multiple_of(((c % 2) * 4 + column // quarter) * self.unit, self.unit), self.unit)
        self.cs[rows, pl.ds(pl.multiple_of(column % quarter, width), width)] = value

    def run(self, eye, write_pieces, out_in, out_rec, out_bias, store_sem):
        act, wrec, wrt = self.act, self.wrec, self.wrt
        chunks, blocks, steps = self.chunks, self.blocks, self.steps

        def loop(start, stop, body):
            def wrapped(c, carry):
                body(c)
                return carry

            lax.fori_loop(start, stop, wrapped, 0)

        def span(start, size):
            return pl.ds(pl.multiple_of(start, size), size)

        def dz_arrived(i):
            def one(t):
                self.dz_copy(i, t).wait_recv()

            loop(0, steps, one)

        dz_arrived(0)
        self.wait_ready()
        loop(0, P_AHEAD, self.p_make)

        @pl.when(self.first)
        def _():
            for b in range(blocks):
                self.factor(2, b).wait_recv()

        @pl.when(self.second)
        def _():
            for b in range(blocks):
                self.factor(3, b).wait_recv()
                self.hand_over(b).wait_recv()

        self.build_z(eye)
        dz_arrived(1)
        loop(0, Z_AHEAD, self.z_make)

        pieces = write_pieces(self.u_a.at[:, 0 : self.rows])

        def first_piece():
            for b in range(blocks):
                for i in (0, 1, 3):
                    self.factor(i, b).wait_send()

            @pl.when(self.first)
            def _():
                for b in range(blocks):
                    self.factor(2, b).wait_send()
                    self.hand_over(b).wait_send()

            pieces[0]()

        extra = (
            (1, self.bias_start), (2, first_piece), (4, pieces[1]), (5, lambda: self.bias_step(0)), (6, pieces[2]),
            (8, pieces[3]), (9, lambda: self.bias_step(1)), (10, pieces[4]), (12, pieces[5]), (13, lambda: self.bias_step(2)),
        )

        def total(kept, landed):
            return act[kept] + wrec[landed].astype(F32)

        def p_after_b(c):
            self.p_along_b(c).wait_recv()
            theirs, mine = (1 - self.kz) * 128, self.kz * 128
            wrt[self.p_out(c, 256, 128)] = total(self.p_kept(c, theirs, 128), self.p_in(c, theirs, 128)).astype(BF)
            self.p_mate(c).start()
            kept = self.p_kept(c, mine, 128)
            act[kept] = total(kept, self.p_in(c, mine, 128))

        def p_after_mate(c):
            self.p_mate(c).wait_recv()
            base = self.kz * 128
            theirs, mine = (1 - self.zin) * 64, self.zin * 64
            wrt[self.p_out(c, 384, 64)] = total(
                self.p_kept(c, base + theirs, 64), self.p_in(c, 256 + theirs, 64)
            ).astype(BF)
            self.p_across(c).start()
            kept = self.p_kept(c, base + mine, 64)
            act[kept] = total(kept, self.p_in(c, 256 + mine, 64))

        def p_after_across(c):
            self.p_across(c).wait_recv()
            kept = self.p_kept(c, self.kz * 128 + self.zin * 64, 64)
            self.put(c, (c // 2) * WIDE, total(kept, self.p_in(c, 384, 64)))

        def z_after_a(c):
            self.z_along_a(c).wait_recv()
            theirs, mine = (1 - self.cb) * 256, self.cb * 256
            wrt[self.z_out(c, 512, 256)] = total(self.z_in(c, theirs, 256), self.z_in(c, theirs, 256)).astype(BF)
            self.z_along_b(c).start()
            kept = self.z_in(c, mine, 256)
            act[kept] = total(kept, kept)

        def z_after_b(c):
            self.z_along_b(c).wait_recv()
            base = self.cb * 256
            for i in range(3):
                row = z_place((self.z + 3 - i) % 4) * 64
                wrt[self.z_out(c, 768 + 64 * i, 64)] = total(
                    self.z_in(c, base + row, 64), self.z_in(c, 512 + row, 64)
                ).astype(BF)
                self.z_all(c, i).start()
            row = z_place(self.z) * 64
            kept = self.z_in(c, base + row, 64)
            act[kept] = total(kept, self.z_in(c, 512 + row, 64))

        def z_after_all(c):
            for i in range(3):
                self.z_all(c, i).wait_recv()
            column = 2 * self.quarter + (c // 2) * CHUNK
            kept = self.z_in(c, self.cb * 256 + z_place(self.z) * 64, 64)
            self.put(c, column + self.zp * self.quarter, total(kept, self.z_in(c, 832, 64)))
            opposite = wrec[self.z_in(c, 768, 64)].astype(F32) + wrec[self.z_in(c, 896, 64)].astype(F32)
            self.put(c, column + (1 - self.zp) * self.quarter, opposite)

        stages = (
            (p_after_b, 0), (z_after_a, 0), (self.p_make, -P_AHEAD), (self.z_make, -Z_AHEAD),
            (p_after_mate, P_LAGS[0]), (z_after_b, Z_LAGS[0]),
            (p_after_across, P_LAGS[1]), (z_after_all, Z_LAGS[1]),
        )

        def turn(n, carry):
            for work, lag in stages:
                c = n - lag
                pl.when((c >= 0) & (c < chunks))(lambda: work(c))
            for at, work in extra:
                pl.when(n == at)(work)
            return carry

        lax.fori_loop(0, chunks + max(P_LAGS[1], Z_LAGS[1]), turn, 0)
        self.bias_step(3)

        mine = self.bias_plan(3)[1]
        self.brecv[0, 0:1, :] = jnp.sum(self.bsum[mine], axis=0, keepdims=True)
        bias_store = pltpu.make_async_copy(self.brecv.at[0, pl.ds(0, 1)], out_bias, store_sem.at[2])
        bias_store.start()

        def result(n):
            g, q = n // 4, n % 4
            out = (out_in, out_rec)[g]
            rows = pl.ds(n * self.unit, self.unit)
            return pltpu.make_async_copy(
                self.cs.at[rows], out.at[:, pl.ds(q * self.quarter, self.quarter)], store_sem.at[3 + n]
            )

        for n in range(8):
            result(n).start()

        def dz_sent(t):
            for i in range(2):
                self.dz_copy(i, t).wait_send()

        loop(0, steps, dz_sent)
        for i in range(4):
            self.bias_copy(i).wait_send()

        def sent(c):
            for part in (self.p_along_b, self.p_mate, self.p_across, self.z_along_a, self.z_along_b):
                part(c).wait_send()
            for i in range(3):
                self.z_all(c, i).wait_send()

        loop(0, chunks, sent)
        bias_store.wait()
        for n in range(8):
            result(n).wait()


def deliver_kernel(count, *refs):
    sources, targets, held, sems = refs[:count], refs[count : 2 * count], refs[2 * count : 3 * count], refs[3 * count]
    loads = [pltpu.make_async_copy(sources[i], held[i], sems.at[0, i]) for i in range(count)]
    stores = [pltpu.make_async_copy(held[i], targets[i], sems.at[1, i]) for i in range(count)]
    for copy in loads:
        copy.start()
    for load, store in zip(loads, stores):
        load.wait()
        store.start()
    for copy in stores:
        copy.wait()


def deliver(arrays):
    anywhere = [pl.BlockSpec(memory_space=pl.ANY)] * len(arrays)
    return pl.pallas_call(
        functools.partial(deliver_kernel, len(arrays)),
        out_shape=tuple(jax.ShapeDtypeStruct(a.shape, a.dtype) for a in arrays),
        in_specs=anywhere,
        out_specs=tuple(anywhere),
        scratch_shapes=[pltpu.VMEM(a.shape, a.dtype) for a in arrays] + [pltpu.SemaphoreType.DMA((2, len(arrays)))],
        compiler_params=pltpu.CompilerParams(vmem_limit_bytes=62 * 2**20),
        name="deliver",
    )(*arrays)


def on_device(inputs, lengths, w_in, w_rec, bias, cotangent):
    micro, per, steps, feats = inputs.shape
    hidden = w_rec.shape[1]
    seqs = micro * per
    total = steps * seqs
    vmem = pltpu.VMEM
    dma = pltpu.SemaphoreType.DMA
    blocks = block_count(steps)
    shards = lax.axis_size("dp")
    fused = shards == 16
    if fused:
        last_three = (
            jax.ShapeDtypeStruct((feats // shards, 4 * hidden), F32),
            jax.ShapeDtypeStruct((hidden // shards, 4 * hidden), F32),
            jax.ShapeDtypeStruct((1, 4 * hidden // shards), F32),
        )
        chunks = 2 * hidden // CHUNK
        more = [
            vmem((total, feats), BF),
            vmem((total + seqs, hidden), BF),
            vmem((total, feats), BF),
            vmem((total + seqs, hidden), BF),
            vmem((total, 2 * hidden), BF),
            vmem((total, hidden), BF),
            vmem((16, 8, 4 * hidden // 16), F32),
            vmem((15, 8, 4 * hidden // 16), F32),
            pltpu.SemaphoreType.REGULAR,
            dma((2, 4, blocks)),
            dma((2, blocks)),
            dma((4, steps)),
            dma((6, chunks)),
            dma((10, chunks)),
            dma((2, 4)),
        ]
    else:
        last_three = (
            jax.ShapeDtypeStruct((total, feats), BF),
            jax.ShapeDtypeStruct((total, hidden), BF),
            jax.ShapeDtypeStruct((total, 4 * hidden), BF),
        )
        more = []
    anywhere = pl.BlockSpec(memory_space=pl.ANY)
    results = pl.pallas_call(
        functools.partial(lstm_kernel, steps, seqs, fused),
        out_shape=(
            jax.ShapeDtypeStruct((total, hidden), BF),
            jax.ShapeDtypeStruct((total, feats), BF),
            *last_three,
        ),
        in_specs=[anywhere, pl.BlockSpec(memory_space=pltpu.VMEM)] + [anywhere] * 4,
        out_specs=(anywhere,) * 5,
        scratch_shapes=[
            vmem((total, feats), BF),
            vmem((total + seqs, hidden), BF),
            vmem((total, hidden), BF),
            vmem((total, feats), BF),
            vmem((total, 4 * hidden), F32),
            vmem((total + seqs, hidden), F32),
            vmem((total, 4 * hidden), BF),
            vmem((feats, 4 * hidden), BF),
            vmem((hidden, 4 * hidden), BF),
            vmem((4 * hidden, hidden), BF),
            vmem((4 * hidden, feats), BF),
            vmem((seqs, hidden), F32),
            vmem((seqs, hidden), F32),
            vmem((seqs, 128), F32),
            vmem((1, 4 * hidden), F32),
            dma((7,)),
            dma((11,)),
            dma((blocks,)),
            dma((blocks,)),
            dma((blocks,)),
            dma((blocks,)),
            *more,
        ],
        compiler_params=pltpu.CompilerParams(
            collective_id=0, has_side_effects=True, vmem_limit_bytes=62 * 2**20
        ),
        name="lstm_both_ways",
    )(
        inputs.reshape(total, feats),
        lengths,
        w_in[0],
        w_rec[0],
        bias,
        cotangent.reshape(total, hidden),
    )
    if fused:
        hid, dx, share_in, share_rec, share_bias = deliver(results)
    else:
        hid, dx, u, hp, dz = results
        sum_in = lax.dot_general(u, dz, (((0,), (0,)), ((), ())), preferred_element_type=F32)
        sum_rec = lax.dot_general(hp, dz, (((0,), (0,)), ((), ())), preferred_element_type=F32)
        sum_bias = jnp.sum(dz, axis=0, dtype=F32)
        share_in = lax.psum_scatter(sum_in, "dp", scatter_dimension=0, tiled=True)
        share_rec = lax.psum_scatter(sum_rec, "dp", scatter_dimension=0, tiled=True)
        share_bias = lax.psum_scatter(sum_bias, "dp", scatter_dimension=0, tiled=True)[None]
    shape = inputs.shape
    return (
        hid.reshape(shape)[None],
        dx.reshape(shape)[None],
        share_in[None],
        share_rec[None],
        share_bias,
    )


def solution(mesh):
    placed = (
        P(None, "dp", None, None),
        P(None, "dp"),
        P("section", None, None),
        P("section", None, None),
        P("section", None),
        P(None, "dp", None, None),
    )
    return jax.shard_map(
        on_device,
        mesh=mesh,
        in_specs=placed,
        out_specs=(
            P("section", None, "dp", None, None),
            P("section", None, "dp", None, None),
            P("section", "dp", None),
            P("section", "dp", None),
            P("section", "dp"),
        ),
        check_vma=False,
    )
```
